32 devices in a mesh: rep: 2 (over x), row: 4 (over y, core), col: 4 (over z).
Axes of the slice: x: 2, y: 2, z: 4, core: 2. Of those that a mesh axis runs over, the one named last changes fastest.
Arguments:
- tokens: bfloat16 [4096, 2048], P(('rep', 'row', 'col')), may hold values from -18 to 18
- norm_gain: float32 [2048], replicated, may hold values from 0.1 to 1.9
- gate_weights: float32 [4096, 6], P(('rep', 'row', 'col')), may hold values from 0.05 to 0.5
- routes: int32 [4096, 6], P(('rep', 'row', 'col')), may hold values from 0 to 63, all different within a row; in each aligned block of 128 rows (0 to 127, 128 to 255, ...) at most 18 rows name the same one
- moves: int32 [16, 2, 32], P(('row', 'col')), may hold values from 0 to 127, as said below
- w_gate: bfloat16 [64, 2048, 1408], P(('row', 'col')), may hold values from -0.125 to 0.125
- w_up: bfloat16 [64, 2048, 1408], P(('row', 'col')), may hold values from -0.125 to 0.125
- w_down: bfloat16 [64, 1408, 2048], P(('row', 'col')), may hold values from -0.15625 to 0.15625
Outputs:
- served: bfloat16 [4096, 2048], P(('rep', 'row', 'col'))
The draws below stay inside these ranges and needn't reach their ends.
Inputs may be any that keep to these rules, and one draw needn't show every extreme that they name: `routes`: in the 128 rows of one device no expert is named by more than 18 rows, a bound that some block reaches. For each p, moves[p, 0] holds 32 different rows and moves[p, 1] holds 32 different rows.
All inputs are finite; a program needn't handle non-finite values.
Results may differ from the reference program's by a relative error of at most 0.0037.
Values may be sent and summed in bfloat16 or wider, within the bound.
No kernel may reach another device: no remote copies, remote signals or barrier semaphores. Data moves between devices by JAX's collectives and lax.ppermute only.
A program may use at most 128 MiB of HBM per device.

```python
import math
import jax
import jax.numpy as jnp
import numpy as np
from jax import lax

D = 2048
FF = 1408
EXPERTS = 64
TOP = 6
TOK_DEV = 128
CAP = 18
MIG = 32
PAIRS = 16
TOKENS = 4096


def draw_tokens(key, part):
    keys = jax.random.split(key, 3)
    row_scale = jnp.exp(jax.random.uniform(keys[1], (TOKENS, 1), jnp.float32, math.log(0.3), math.log(3.0)))
    col_scale = jnp.exp(jax.random.uniform(keys[2], (1, D), jnp.float32, math.log(0.5), math.log(2.0)))
    base = jnp.clip(jax.random.normal(keys[0], (TOKENS, D), jnp.float32), -3.0, 3.0)
    return (base * row_scale * col_scale).astype(jnp.bfloat16)


def pick_rows(key):
    scores = jax.random.randint(key, (PAIRS, TOK_DEV), 0, 1 << 20, jnp.int32) * TOK_DEV
    scores = scores + jnp.arange(TOK_DEV, dtype=jnp.int32)[None, :]
    scores = scores.at[0, 0].set(-2)
    scores = scores.at[0, TOK_DEV - 1].set(-1)
    order = jnp.argsort(scores, axis=1, stable=True)
    return order[:, :MIG].astype(jnp.int32)


def draw_moves(key, part):
    leaving = pick_rows(jax.random.fold_in(key, 11))
    arriving = pick_rows(jax.random.fold_in(key, 23))
    return jnp.stack([leaving, arriving], axis=1)


def block_scale(stream_key, dims, cuts, low, top_value):
    def one(dim, blocks):
        steps = jax.random.uniform(jax.random.fold_in(jax.random.fold_in(stream_key, 6), dim), (blocks,), jnp.float32, low / len(cuts), top_value / len(cuts))
        return jnp.repeat(jnp.exp(steps), dims[dim] // blocks).reshape((-1,) + (1,) * (len(dims) - dim - 1))

    level = one(*cuts[0])
    for cut in cuts[1:]:
        level = level * one(*cut)
    return level


def shared_out(rng, own, number, rows, amount, top, bound, slope):
    sequence = jax.random.permutation(rng, amount)
    packed, common = load_shares(amount, rows * top, bound, slope, True), load_shares(amount, rows * top, bound, slope, False)
    places = jnp.arange(amount)

    def named(lengths, rotation):
        used = int((lengths > 0).sum())
        fixed = max(1, used // 4)
        moved = fixed + (places - fixed + rotation * (used - fixed)) % max(1, amount - fixed)
        return jnp.zeros((amount,), jnp.int32).at[sequence[jnp.where(places < fixed, places, moved)]].set(jnp.asarray(lengths, jnp.int32))

    lengths = jnp.where(number % 4 == 0, named(packed, number // 4), named(common, number - number // 4 - 1))
    mixed = jax.random.permutation(jax.random.fold_in(own, 3), amount)
    giver, sink = mixed[0:amount // 2 * 2:2], mixed[1:amount // 2 * 2:2]
    room = jnp.minimum(lengths[giver] - 1, bound - lengths[sink]) // 2
    room = jnp.where((giver == sequence[0]) | (sink == sequence[0]) | (lengths[sink] == 0), 0, jnp.maximum(room, 0))
    moved = jax.random.randint(jax.random.fold_in(own, 4), (amount // 2,), 0, 1 << 20) % (room + 1)
    lengths = lengths.at[giver].add(-moved).at[sink].add(moved)
    members = jnp.searchsorted(jnp.cumsum(lengths), jnp.arange(rows * top), side="right").astype(jnp.int32)
    grid = members.reshape(top, rows).T
    grid = grid[jax.random.permutation(jax.random.fold_in(own, 1), rows)]
    rotation = jax.random.randint(jax.random.fold_in(own, 2), (rows, 1), 0, top)
    return jnp.take_along_axis(grid, (jnp.arange(top)[None, :] + rotation) % top, axis=1)


def load_shares(count, total, bound, lean, full):
    weights = [(1 << 20) // math.isqrt(rank ** lean) + 1 for rank in range(1, count + 1)]
    largest = bound if full else min(bound, max(-(-total // count), total * weights[0] // sum(weights)))
    least = 1 if total - largest >= count - 1 else 0
    holding, rest = [largest] + [least] * (count - 1), total - largest - least * (count - 1)
    while rest > 0:
        free = [i for i in range(1, count) if holding[i] < largest] or [i for i in range(1, count) if holding[i] < bound]
        mass, remaining = sum([weights[i] for i in free]), rest
        for i in free:
            extra = min(bound - holding[i], max(1, remaining * weights[i] // mass), rest)
            holding[i] = holding[i] + extra
            rest = rest - extra
    return np.array(holding)


def gaussian(key, extent, width, limit, shards=(), kind=jnp.bfloat16):
    loudness = block_scale(key, extent, shards, -0.22, 0.18) if shards else 1.0
    values = jax.random.normal(key, extent, jnp.float32) * width * loudness
    return jnp.minimum(jnp.maximum(values, -limit), limit).astype(kind)


def setup_inputs(seed: int = 0) -> dict:
    splits = jax.random.split(jax.random.key(seed), 9)
    tokens = draw_tokens(jax.random.fold_in(splits[8], 71), 0)
    norm_gain = jnp.clip(1.0 + 0.18 * jax.random.normal(splits[1], (D,), jnp.float32), 0.1, 1.9)
    gate_weights = jnp.clip(jnp.exp(math.log(0.5) - 2.3025851 * jax.random.uniform(splits[2], (TOKENS, TOP), jnp.float32) ** block_scale(splits[2], (TOKENS, TOP), ((0, 32),), -0.2, 0.2)), 0.05, 0.5)
    routes_keys = jax.random.split(jax.random.fold_in(splits[3], 1), TOKENS // TOK_DEV)
    routes_turns = jax.random.permutation(jax.random.fold_in(splits[3], 3), TOKENS // TOK_DEV)
    routes = jax.vmap(lambda own, number: shared_out(jax.random.fold_in(splits[3], 2), own, number, TOK_DEV, EXPERTS, TOP, CAP, 2))(routes_keys, routes_turns).reshape((TOKENS, TOP))
    moves = draw_moves(jax.random.fold_in(splits[8], 71), 0)
    w_gate = gaussian(splits[5], (EXPERTS, D, FF), D ** -0.5, 0.125, ((0, 16),))
    w_up = gaussian(splits[6], (EXPERTS, D, FF), D ** -0.5, 0.125, ((0, 16),))
    w_down = gaussian(splits[7], (EXPERTS, FF, D), FF ** -0.5, 0.15625, ((0, 16),))
    return dict(tokens=tokens, norm_gain=norm_gain, gate_weights=gate_weights, routes=routes, moves=moves, w_gate=w_gate, w_up=w_up, w_down=w_down)


def expert_rows(rows, gate_one, up_one, down_one):
    gate_part = jnp.dot(rows, gate_one, preferred_element_type=jnp.float32)
    upward = jnp.dot(rows, up_one, preferred_element_type=jnp.float32)
    active = (jax.nn.silu(gate_part) * upward).astype(jnp.bfloat16)
    return jnp.dot(active, down_one, preferred_element_type=jnp.float32).astype(jnp.bfloat16)

def reference(tokens, norm_gain, gate_weights, routes, moves, w_gate, w_up, w_down):
    widened = tokens.astype(jnp.float32)
    normed = (widened * lax.rsqrt(lax.optimization_barrier(jnp.mean(widened * widened, axis=-1, keepdims=True)) + 1e-06) * norm_gain).astype(jnp.bfloat16)
    tok_total = tokens.shape[0]
    features = tokens.shape[1]
    blocks = tok_total // TOK_DEV
    chosen = routes.reshape(blocks, TOK_DEV * TOP).astype(jnp.int32)
    labels = jnp.arange(EXPERTS, dtype=jnp.int32)
    onehot = (chosen[:, :, None] == labels[None, None, :]).astype(jnp.int32)
    position = lax.optimization_barrier(jnp.sum(jnp.cumsum(onehot, axis=1) * onehot, axis=2)) - 1
    block_ids = jnp.arange(blocks, dtype=jnp.int32)[:, None]
    entries = jnp.arange(TOK_DEV * TOP, dtype=jnp.int32)[None, :]
    sources = block_ids * TOK_DEV + entries // TOP
    column = (block_ids * CAP + position).astype(jnp.int32)
    slot_table = jnp.full((EXPERTS, blocks * CAP), tok_total, jnp.int32)
    slot_table = slot_table.at[chosen.ravel(), column.ravel()].set(sources.ravel().astype(jnp.int32))
    weight_table = jnp.zeros((EXPERTS, blocks * CAP), jnp.float32)
    weight_table = weight_table.at[chosen.ravel(), column.ravel()].set(gate_weights.reshape(-1).astype(jnp.float32))
    padded = jnp.concatenate([normed, jnp.zeros((1, features), jnp.bfloat16)], axis=0)

    def one_expert(total, entry):
        sources_here, weights_here, gate_one, up_one, down_one = entry
        rows = padded[sources_here]
        result = expert_rows(rows, gate_one, up_one, down_one)
        total = total.at[sources_here].add(result.astype(jnp.float32) * weights_here[:, None], mode='drop')
        return (total, None)
    total, unused = lax.scan(one_expert, jnp.zeros((tok_total, features), jnp.float32), (slot_table, weight_table, w_gate, w_up, w_down))
    combined = (widened + total).astype(jnp.bfloat16)
    pair_ids = jnp.arange(PAIRS, dtype=jnp.int32)[:, None]
    leaving = (pair_ids * TOK_DEV + moves[:, 0, :].astype(jnp.int32)).ravel()
    arriving = ((PAIRS + pair_ids) * TOK_DEV + moves[:, 1, :].astype(jnp.int32)).ravel()
    served = combined.at[arriving].set(combined[leaving])
    served = served.at[leaving].set(jnp.zeros((leaving.shape[0], features), jnp.bfloat16))
    return served
```

```python
import jax
import jax.numpy as jnp
from jax import lax
from jax.sharding import PartitionSpec as P


def shifted(value, axis, steps):
    count = lax.axis_size(axis)
    first, last = (max(0, -steps), min(count, count - steps))
    return lax.ppermute(value, axis, [(source, source + steps) for source in range(first, last)])


def body(tokens, norm_gain, gate_weights, routes, moves, w_gate, w_up, w_down):
    tok_rows, features = tokens.shape
    per_token = routes.shape[1]
    exp_dev = w_gate.shape[0]
    group = lax.axis_size("row") * lax.axis_size("col")
    experts = group * exp_dev
    capacity = tok_rows * per_token * 3 // (2 * experts)
    axes = ("row", "col")
    widened = tokens.astype(jnp.float32)
    normed = (
        widened * lax.rsqrt(jnp.mean(widened * widened, axis=-1, keepdims=True) + 1e-06) * norm_gain
    ).astype(jnp.bfloat16)
    everyone = lax.all_gather(normed, axes, axis=0, tiled=True).reshape(group, tok_rows, features)
    all_routes = lax.all_gather(routes, axes, axis=0, tiled=True).reshape(group, tok_rows, per_token)
    all_weights = lax.all_gather(gate_weights, axes, axis=0, tiled=True).reshape(
        group, tok_rows, per_token
    )
    mine = lax.axis_index(axes) * exp_dev + jnp.arange(exp_dev, dtype=jnp.int32)
    hit = all_routes[:, :, :, None] == mine[None, None, None, :]
    named = jnp.any(hit, axis=2)
    weight = jnp.sum(jnp.where(hit, all_weights[:, :, :, None], 0.0), axis=2)
    position = jnp.cumsum(named.astype(jnp.int32), axis=1) - 1
    slots = jnp.arange(capacity, dtype=jnp.int32)
    pick = (position[:, :, :, None] == slots) & named[:, :, :, None]
    pick16 = pick.astype(jnp.bfloat16)
    rows = jnp.einsum("btes,btd->ebsd", pick16, everyone, preferred_element_type=jnp.float32)
    rows = rows.astype(jnp.bfloat16).reshape(exp_dev, group * capacity, features)
    slot_weight = jnp.sum(jnp.where(pick, weight[:, :, :, None], 0.0), axis=1)
    slot_weight = jnp.transpose(slot_weight, (1, 0, 2)).reshape(exp_dev, group * capacity, 1)
    gate_part = jnp.einsum("erd,edf->erf", rows, w_gate, preferred_element_type=jnp.float32)
    upward = jnp.einsum("erd,edf->erf", rows, w_up, preferred_element_type=jnp.float32)
    active = (jax.nn.silu(gate_part) * upward * slot_weight).astype(jnp.bfloat16)
    outs = jnp.einsum("erf,efd->erd", active, w_down, preferred_element_type=jnp.float32)
    outs = outs.astype(jnp.bfloat16).reshape(exp_dev, group, capacity, features)
    partial = jnp.einsum("btes,ebsd->btd", pick16, outs, preferred_element_type=jnp.float32)
    partial = partial.astype(jnp.bfloat16).reshape(group * tok_rows, features)
    summed = lax.psum_scatter(partial, axes, scatter_dimension=0, tiled=True)
    combined = (widened + summed.astype(jnp.float32)).astype(jnp.bfloat16)
    leaving = moves[0, 0]
    arriving = moves[0, 1]
    incoming = shifted(combined[leaving], "rep", 1)
    placed = combined.at[arriving].set(incoming)
    cleared = combined.at[leaving].set(jnp.zeros((leaving.shape[0], features), jnp.bfloat16))
    return jnp.where(lax.axis_index("rep") == 1, placed, cleared)


def solution(mesh):
    return jax.shard_map(
        body,
        mesh=mesh,
        in_specs=(
            P(("rep", "row", "col"), None),
            P(),
            P(("rep", "row", "col"), None),
            P(("rep", "row", "col"), None),
            P(("row", "col"), None, None),
            P(("row", "col"), None, None),
            P(("row", "col"), None, None),
            P(("row", "col"), None, None),
        ),
        out_specs=P(("rep", "row", "col"), None),
        check_vma=False,
    )
```

```python
import jax
import jax.numpy as jnp
from jax import lax
from jax.sharding import PartitionSpec as P

META = 128


def shifted(value, axis, steps):
    count = lax.axis_size(axis)
    first, last = (max(0, -steps), min(count, count - steps))
    return lax.ppermute(value, axis, [(source, source + steps) for source in range(first, last)])


def turned(value, steps):
    count = lax.axis_size("col")
    return lax.ppermute(value, "col", [(source, (source + steps) % count) for source in range(count)])


def swapped(value, bit):
    count = lax.axis_size("row")
    return lax.ppermute(value, "row", [(source, source ^ bit) for source in range(count)])


def spread(block):
    cols, rows = lax.axis_size("col"), lax.axis_size("row")
    blocks = [[block] + [turned(block, step) for step in range(1, cols)]]
    bit = rows // 2
    while bit:
        blocks = blocks + [[swapped(one, bit) for one in line] for line in blocks]
        bit //= 2
    return [one for line in blocks for one in line]


def collected(parts):
    cols, rows = lax.axis_size("col"), lax.axis_size("row")
    bit = 1
    parts = parts.reshape(rows, cols, *parts.shape[1:])
    lines = [parts[i] for i in range(rows)]
    while bit < rows:
        half = len(lines) // 2
        there = [swapped(lines[half + i], bit) for i in range(half)]
        lines = [
            (lines[i].astype(jnp.float32) + there[i].astype(jnp.float32)).astype(jnp.bfloat16)
            for i in range(half)
        ]
        bit *= 2
    line = lines[0]
    total = line[0].astype(jnp.float32)
    for step in range(1, cols):
        total = total + turned(line[step], -step).astype(jnp.float32)
    return total


def split3(value):
    high = lax.reduce_precision(value, 8, 7)
    rest = value - high
    middle = lax.reduce_precision(rest, 8, 7)
    return [part.astype(jnp.bfloat16) for part in (high, middle, rest - middle)]


def body(tokens, norm_gain, gate_weights, routes, moves, w_gate, w_up, w_down):
    tok_rows, features = tokens.shape
    per_token = routes.shape[1]
    exp_dev = w_gate.shape[0]
    group = lax.axis_size("row") * lax.axis_size("col")
    experts = group * exp_dev
    capacity = tok_rows * per_token * 3 // (2 * experts)
    axes = ("row", "col")
    widened = tokens.astype(jnp.float32)
    normed = (
        widened * lax.rsqrt(jnp.mean(widened * widened, axis=-1, keepdims=True) + 1e-06) * norm_gain
    ).astype(jnp.bfloat16)
    meta = jnp.concatenate([routes.astype(jnp.bfloat16)] + split3(gate_weights), axis=1)
    meta = jnp.pad(meta, ((0, 0), (0, META - meta.shape[1])))
    everyone = jnp.stack(spread(jnp.concatenate([normed, meta], axis=1)))
    all_meta = everyone[:, :, features:].astype(jnp.float32)
    everyone = everyone[:, :, :features]
    all_routes = all_meta[:, :, :per_token].astype(jnp.int32)
    all_weights = (
        all_meta[:, :, per_token : 2 * per_token]
        + all_meta[:, :, 2 * per_token : 3 * per_token]
        + all_meta[:, :, 3 * per_token : 4 * per_token]
    )
    mine = lax.axis_index(axes) * exp_dev + jnp.arange(exp_dev, dtype=jnp.int32)
    hit = all_routes[:, :, :, None] == mine[None, None, None, :]
    named = jnp.any(hit, axis=2)
    weight = jnp.sum(jnp.where(hit, all_weights[:, :, :, None], 0.0), axis=2)
    lower = jnp.tril(jnp.ones((tok_rows, tok_rows), jnp.bfloat16))
    position = jnp.einsum(
        "st,bte->bse", lower, named.astype(jnp.bfloat16), preferred_element_type=jnp.float32
    )
    position = position.astype(jnp.int32) - 1
    slots = jnp.arange(capacity, dtype=jnp.int32)
    pick = (position[:, :, :, None] == slots) & named[:, :, :, None]
    pick16 = pick.astype(jnp.bfloat16)
    rows = jnp.einsum("btes,btd->ebsd", pick16, everyone, preferred_element_type=jnp.float32)
    rows = rows.astype(jnp.bfloat16).reshape(exp_dev, group * capacity, features)
    slot_weight = jnp.sum(jnp.where(pick, weight[:, :, :, None], 0.0), axis=1)
    slot_weight = jnp.transpose(slot_weight, (1, 0, 2)).reshape(exp_dev, group * capacity, 1)
    gate_part = jnp.einsum("erd,edf->erf", rows, w_gate, preferred_element_type=jnp.float32)
    upward = jnp.einsum("erd,edf->erf", rows, w_up, preferred_element_type=jnp.float32)
    active = (jax.nn.silu(gate_part) * upward * slot_weight).astype(jnp.bfloat16)
    outs = jnp.einsum("erf,efd->erd", active, w_down, preferred_element_type=jnp.float32)
    outs = outs.astype(jnp.bfloat16).reshape(exp_dev, group, capacity, features)
    partial = jnp.einsum("btes,ebsd->btd", pick16, outs, preferred_element_type=jnp.float32)
    partial = partial.astype(jnp.bfloat16)
    combined = (widened + collected(partial)).astype(jnp.bfloat16)
    leaving = moves[0, 0]
    arriving = moves[0, 1]
    incoming = shifted(combined[leaving], "rep", 1)
    placed = combined.at[arriving].set(incoming)
    cleared = combined.at[leaving].set(jnp.zeros((leaving.shape[0], features), jnp.bfloat16))
    return jnp.where(lax.axis_index("rep") == 1, placed, cleared)


def solution(mesh):
    return jax.shard_map(
        body,
        mesh=mesh,
        in_specs=(
            P(("rep", "row", "col"), None),
            P(),
            P(("rep", "row", "col"), None),
            P(("rep", "row", "col"), None),
            P(("row", "col"), None, None),
            P(("row", "col"), None, None),
            P(("row", "col"), None, None),
            P(("row", "col"), None, None),
        ),
        out_specs=P(("rep", "row", "col"), None),
        check_vma=False,
    )
```

```python
import functools

import jax
import jax.numpy as jnp
from jax import lax
from jax.experimental import pallas as pl
from jax.experimental.pallas import tpu as pltpu
from jax.sharding import PartitionSpec as P

META = 128
GROUP = 8
LANE = 8


def shifted(value, axis, steps):
    count = lax.axis_size(axis)
    first, last = (max(0, -steps), min(count, count - steps))
    return lax.ppermute(value, axis, [(source, source + steps) for source in range(first, last)])


def turned(value, steps):
    count = lax.axis_size("col")
    return lax.ppermute(value, "col", [(source, (source + steps) % count) for source in range(count)])


def swapped(value, bit):
    count = lax.axis_size("row")
    return lax.ppermute(value, "row", [(source, source ^ bit) for source in range(count)])


def spread(block):
    cols, rows = lax.axis_size("col"), lax.axis_size("row")
    line = [block]
    for _ in range(1, cols):
        line.append(turned(line[-1], 1))
    lines = [line]
    bit = rows // 2
    while bit:
        lines = lines + [[swapped(one, bit) for one in line] for line in lines]
        bit //= 2
    return [one for line in lines for one in line]


def added(first, second):
    return (first.astype(jnp.float32) + second.astype(jnp.float32)).astype(jnp.bfloat16)


def collected(near, far):
    cols, rows = lax.axis_size("col"), lax.axis_size("row")
    lines, bit = near, 1
    there = [swapped(line, bit) for line in reversed(far)][::-1]
    lines = [[added(line[i], other[i]) for i in range(cols)] for line, other in zip(lines, there)]
    bit *= 2
    while bit < rows:
        half = len(lines) // 2
        there = [[swapped(one, bit) for one in line[::-1]][::-1] for line in lines[half:]]
        lines = [
            [added(one, other) for one, other in zip(line, others)]
            for line, others in zip(lines[:half], there)
        ]
        bit *= 2
    line = lines[0]
    total = line[0].astype(jnp.float32)
    for step in range(1, cols):
        total = total + turned(line[step], -step).astype(jnp.float32)
    return total


def split3(value):
    high = lax.reduce_precision(value, 8, 7)
    rest = value - high
    middle = lax.reduce_precision(rest, 8, 7)
    return [part.astype(jnp.bfloat16) for part in (high, middle, rest - middle)]


def moe_kernel(
    plan, first_ref, *refs
):
    nb, exp_dev, slots, per_token, places, tiles, wide = plan
    xs, refs = refs[:nb], refs[nb:]
    gate_ref, up_ref, down_ref = refs[:3]
    refs = refs[3:]
    out_count = 1 + max(index for index, _ in places)
    outs, refs = refs[:out_count], refs[out_count:]
    gate_b, up_b, down_b, xbuf, gbuf, pbuf, act, slotw, named_s, weight_s, wsem, xsem, osem = refs
    groups = nb // GROUP
    tok = xs[0].shape[0]
    features = down_ref.shape[2]
    rows = groups * slots

    def weight_copy(kind, e, slot):
        source = (gate_ref, up_ref, down_ref)[kind]
        target = (gate_b, up_b, down_b)[kind]
        return pltpu.make_async_copy(source.at[e], target.at[slot], wsem.at[kind, slot])

    def block_copy(g, b):
        return pltpu.make_async_copy(
            xs[g * GROUP + b], xbuf.at[g % 2, pl.ds(b * tok, tok), :], xsem.at[g % 2, b]
        )

    def load(g):
        for b in range(GROUP):
            block_copy(g, b).start()

    load(0)
    for kind in range(3):
        weight_copy(kind, 0, 0).start()
    if groups > 1:
        load(1)
    if exp_dev > 1:
        for kind in range(3):
            weight_copy(kind, 1, 1).start()

    lane = lax.broadcasted_iota(jnp.int32, (tok, tok), 1)
    sub = lax.broadcasted_iota(jnp.int32, (tok, tok), 0)
    upto = (sub <= lane).astype(jnp.bfloat16)
    pairs = exp_dev * GROUP
    pair_r = lax.broadcasted_iota(jnp.int32, (pairs, pairs), 0)
    pair_c = lax.broadcasted_iota(jnp.int32, (pairs, pairs), 1)
    before = ((pair_r // GROUP == pair_c // GROUP) & (pair_c < pair_r)).astype(jnp.bfloat16)
    slot_id = lax.broadcasted_iota(jnp.int32, (slots, tok), 0).astype(jnp.float32)
    first = first_ref[0]

    for g in range(groups):
        for b in range(GROUP):
            block_copy(g, b).wait()
        for b in range(GROUP):
            meta = xbuf[g % 2, b * tok : (b + 1) * tok, features:].astype(jnp.float32).T
            chosen = meta[:LANE]
            given = meta[LANE : 2 * LANE] + meta[2 * LANE : 3 * LANE] + meta[3 * LANE : 4 * LANE]
            for e in range(exp_dev):
                hit = chosen == (first + e).astype(jnp.float32)
                named_s[e * GROUP + b : e * GROUP + b + 1, :] = jnp.sum(
                    hit.astype(jnp.float32), axis=0, keepdims=True
                )
                weight_s[e * GROUP + b : e * GROUP + b + 1, :] = jnp.sum(
                    jnp.where(hit, given, 0.0), axis=0, keepdims=True
                )
        named = named_s[...]
        count = jnp.dot(named.astype(jnp.bfloat16), upto, preferred_element_type=jnp.float32)
        totals = jnp.broadcast_to(count[:, tok - 1 :], (pairs, tok)).astype(jnp.bfloat16)
        base = jnp.dot(before, totals, preferred_element_type=jnp.float32)
        named_s[...] = jnp.where(named > 0.5, base + count - 1.0, -1.0)
        for e in range(exp_dev):
            total = jnp.zeros((slots, tok), jnp.float32)
            for b in range(GROUP):
                place = named_s[e * GROUP + b : e * GROUP + b + 1, :]
                pick = slot_id == place
                pbuf[g, e * slots : (e + 1) * slots, b * tok : (b + 1) * tok] = pick.astype(
                    jnp.float32
                ).astype(jnp.bfloat16)
                total += jnp.where(pick, weight_s[e * GROUP + b : e * GROUP + b + 1, :], 0.0)
            slotw[e, g * slots : (g + 1) * slots, :] = jnp.sum(total, axis=1, keepdims=True)

        @pl.loop(0, features // wide)
        def _(n):
            cols = pl.ds(pl.multiple_of(n * wide, wide), wide)
            got = jnp.dot(pbuf[g], xbuf[g % 2, :, cols], preferred_element_type=jnp.float32)
            got = got.astype(jnp.bfloat16)
            for e in range(exp_dev):
                gbuf[e, g * slots : (g + 1) * slots, cols] = got[e * slots : (e + 1) * slots]

        if g + 2 < groups:
            load(g + 2)

    @pl.loop(0, exp_dev)
    def _(e):
        slot = lax.rem(e, 2)
        weight_copy(0, e, slot).wait()
        weight_copy(1, e, slot).wait()
        for start, size in tiles:
            gate = jnp.dot(
                gbuf[e], gate_b[slot, :, start : start + size], preferred_element_type=jnp.float32
            )
            upward = jnp.dot(
                gbuf[e], up_b[slot, :, start : start + size], preferred_element_type=jnp.float32
            )
            act[:, start : start + size] = (
                gate / (1.0 + jnp.exp(-gate)) * upward * slotw[e]
            ).astype(jnp.bfloat16)

        @pl.when(e + 2 < exp_dev)
        def _():
            weight_copy(0, e + 2, slot).start()
            weight_copy(1, e + 2, slot).start()

        weight_copy(2, e, slot).wait()

        @pl.loop(0, features // wide)
        def _(n):
            cols = pl.ds(pl.multiple_of(n * wide, wide), wide)
            gbuf[e, :, cols] = jnp.dot(
                act[...], down_b[slot, :, cols], preferred_element_type=jnp.float32
            ).astype(jnp.bfloat16)

        @pl.when(e + 2 < exp_dev)
        def _():
            weight_copy(2, e + 2, slot).start()

    def out_copy(g, b):
        index, inner = places[g * GROUP + b]
        target = outs[index] if inner is None else outs[index].at[inner]
        return pltpu.make_async_copy(
            xbuf.at[g % 2, pl.ds(b * tok, tok), pl.ds(0, features)], target, osem.at[g % 2, b]
        )

    for g in reversed(range(groups)):
        if g + 2 < groups:
            for b in range(GROUP):
                out_copy(g + 2, b).wait()

        @pl.loop(0, features // wide)
        def _(n):
            cols = pl.ds(pl.multiple_of(n * wide, wide), wide)
            made = jnp.concatenate(
                [gbuf[e, g * slots : (g + 1) * slots, cols] for e in range(exp_dev)], axis=0
            )
            xbuf[g % 2, :, cols] = lax.dot_general(
                pbuf[g], made, (((0,), (0,)), ((), ())), preferred_element_type=jnp.float32
            ).astype(jnp.bfloat16)

        for b in range(GROUP):
            out_copy(g, b).start()
    for g in range(min(groups, 2)):
        for b in range(GROUP):
            out_copy(g, b).wait()


def experts_of(blocks, first, capacity, per_token, w_gate, w_up, w_down):
    nb = len(blocks)
    tok = blocks[0].shape[0]
    exp_dev, features, hidden = w_gate.shape
    cols, rows = lax.axis_size("col"), lax.axis_size("row")
    slots = -(-GROUP * capacity // 16) * 16
    groups = nb // GROUP
    wide = 512
    tiles = [(start, min(wide, hidden - start)) for start in range(0, hidden, wide)]
    near = (rows // 2) * cols
    places = [(i, None) for i in range(near)]
    places += [(near + i // cols, i % cols) for i in range(nb - near)]
    shapes = [jax.ShapeDtypeStruct((tok, features), jnp.bfloat16)] * near
    shapes += [jax.ShapeDtypeStruct((cols, tok, features), jnp.bfloat16)] * (rows // 2)
    plan = (nb, exp_dev, slots, per_token, places, tiles, wide)
    pairs = exp_dev * GROUP
    got = pl.pallas_call(
        functools.partial(moe_kernel, plan),
        out_shape=shapes,
        in_specs=[pl.BlockSpec(memory_space=pltpu.SMEM)]
        + [pl.BlockSpec(memory_space=pl.ANY)] * (nb + 3),
        out_specs=[pl.BlockSpec(memory_space=pl.ANY)] * len(shapes),
        scratch_shapes=[
            pltpu.VMEM((2, features, hidden), jnp.bfloat16),
            pltpu.VMEM((2, features, hidden), jnp.bfloat16),
            pltpu.VMEM((2, hidden, features), jnp.bfloat16),
            pltpu.VMEM((2, GROUP * tok, features + META), jnp.bfloat16),
            pltpu.VMEM((exp_dev, groups * slots, features), jnp.bfloat16),
            pltpu.VMEM((groups, exp_dev * slots, GROUP * tok), jnp.bfloat16),
            pltpu.VMEM((groups * slots, hidden), jnp.bfloat16),
            pltpu.VMEM((exp_dev, groups * slots, 1), jnp.float32),
            pltpu.VMEM((pairs, tok), jnp.float32),
            pltpu.VMEM((pairs, tok), jnp.float32),
            pltpu.SemaphoreType.DMA((3, 2)),
            pltpu.SemaphoreType.DMA((2, GROUP)),
            pltpu.SemaphoreType.DMA((2, GROUP)),
        ],
        compiler_params=pltpu.CompilerParams(vmem_limit_bytes=60 * 1024 * 1024),
        cost_estimate=pl.CostEstimate(
            flops=6 * exp_dev * groups * slots * features * hidden,
            bytes_accessed=6 * exp_dev * features * hidden + 4 * nb * tok * features,
            transcendentals=0,
        ),
        name="experts",
    )(first, *blocks, w_gate, w_up, w_down)
    lines = [list(got[i * cols : (i + 1) * cols]) for i in range(rows // 2)]
    return lines, list(got[near:])


def body(tokens, norm_gain, gate_weights, routes, moves, w_gate, w_up, w_down):
    tok_rows, features = tokens.shape
    per_token = routes.shape[1]
    exp_dev = w_gate.shape[0]
    group = lax.axis_size("row") * lax.axis_size("col")
    experts = group * exp_dev
    capacity = tok_rows * per_token * 3 // (2 * experts)
    axes = ("row", "col")
    widened = tokens.astype(jnp.float32)
    normed = (
        widened * lax.rsqrt(jnp.mean(widened * widened, axis=-1, keepdims=True) + 1e-06) * norm_gain
    ).astype(jnp.bfloat16)
    gap = ((0, 0), (0, LANE - per_token))
    meta = [jnp.pad(routes.astype(jnp.bfloat16), gap, constant_values=-1)]
    meta += [jnp.pad(part, gap) for part in split3(gate_weights)]
    meta += [jnp.zeros((tok_rows, META - 4 * LANE), jnp.bfloat16)]
    blocks = spread(jnp.concatenate([normed] + meta, axis=1))
    first = (lax.axis_index(axes) * exp_dev).astype(jnp.int32).reshape(1)
    near, far = experts_of(blocks, first, capacity, per_token, w_gate, w_up, w_down)
    combined = (widened + collected(near, far)).astype(jnp.bfloat16)
    leaving = moves[0, 0]
    arriving = moves[0, 1]
    incoming = shifted(combined[leaving], "rep", 1)
    placed = combined.at[arriving].set(incoming)
    cleared = combined.at[leaving].set(jnp.zeros((leaving.shape[0], features), jnp.bfloat16))
    return jnp.where(lax.axis_index("rep") == 1, placed, cleared)


def solution(mesh):
    return jax.shard_map(
        body,
        mesh=mesh,
        in_specs=(
            P(("rep", "row", "col"), None),
            P(),
            P(("rep", "row", "col"), None),
            P(("rep", "row", "col"), None),
            P(("row", "col"), None, None),
            P(("row", "col"), None, None),
            P(("row", "col"), None, None),
            P(("row", "col"), None, None),
        ),
        out_specs=P(("rep", "row", "col"), None),
        check_vma=False,
    )
```

```python
import functools

import jax
import jax.numpy as jnp
from jax import lax
from jax.experimental import pallas as pl
from jax.experimental.pallas import tpu as pltpu
from jax.sharding import PartitionSpec as P

GROUP = 8
LANE = 8


def shifted(value, axis, steps):
    count = lax.axis_size(axis)
    first, last = (max(0, -steps), min(count, count - steps))
    return lax.ppermute(value, axis, [(source, source + steps) for source in range(first, last)])


def turned(value, steps):
    count = lax.axis_size("col")
    return lax.ppermute(value, "col", [(source, (source + steps) % count) for source in range(count)])


def swapped(value, bit):
    count = lax.axis_size("row")
    return lax.ppermute(value, "row", [(source, source ^ bit) for source in range(count)])


def join_kernel(*refs):
    pass


def joined(*values):
    return pl.pallas_call(
        join_kernel,
        out_shape=[jax.ShapeDtypeStruct(value.shape, value.dtype) for value in values],
        in_specs=[pl.BlockSpec(memory_space=pl.ANY)] * len(values),
        out_specs=[pl.BlockSpec(memory_space=pl.ANY)] * len(values),
        input_output_aliases={i: i for i in range(len(values))},
        name="join",
    )(*values)


def spread(block):
    cols, rows = lax.axis_size("col"), lax.axis_size("row")
    bit = rows // 2
    line, other, last = [block], [], block
    for _ in range(1, cols):
        ahead, across = joined(turned(last, 1), swapped(last, bit))
        line.append(ahead)
        other.append(across)
        last = ahead
    lines = [line, other + [swapped(last, bit)]]
    while bit > 1:
        bit //= 2
        lines = lines + [[swapped(one, bit) for one in line] for line in lines]
    return [one for line in lines for one in line]


def add_kernel(*refs):
    total = refs[0][...].astype(jnp.float32)
    for ref in refs[1:-1]:
        total = total + ref[...].astype(jnp.float32).reshape(total.shape)
    refs[-1][...] = total.astype(jnp.bfloat16)


def part_spec(value, index):
    if index is None:
        return pl.BlockSpec(value.shape, lambda i: (0, 0))
    return pl.BlockSpec((1,) + value.shape[1:], lambda i: (index, 0, 0))


def added(*parts):
    parts = [part if isinstance(part, tuple) else (part, None) for part in parts]
    shape = parts[0][0].shape
    return pl.pallas_call(
        add_kernel,
        grid=(1,),
        out_shape=jax.ShapeDtypeStruct(shape, jnp.bfloat16),
        in_specs=[part_spec(value, index) for value, index in parts],
        out_specs=pl.BlockSpec(shape, lambda i: (0, 0)),
        name="add",
    )(*[value for value, _ in parts])


def collected(near, far):
    cols, rows = lax.axis_size("col"), lax.axis_size("row")
    lines, bit = near, 1
    there = []
    for line in reversed(far):
        if isinstance(line, list):
            there.append([swapped(one, bit) for one in line[::-1]][::-1])
        else:
            whole = swapped(line, bit)
            there.append([(whole, i) for i in range(cols)])
    there = there[::-1]
    terms = [[[line[i], other[i]] for i in range(cols)] for line, other in zip(lines, there)]
    bit *= 2
    while bit < rows:
        half = len(terms) // 2
        sent = [[swapped(added(*one), bit) for one in line[::-1]][::-1] for line in terms[half:]]
        terms = [
            [one + [other] for one, other in zip(line, others)]
            for line, others in zip(terms[:half], sent)
        ]
        bit *= 2
    line = terms[0]
    run = []
    for step in range(cols - 1, 0, -1):
        run = [turned(added(*(line[step] + run)), -1)]
    return line[0] + run


def head_kernel(tokens_ref, gain_ref, weights_ref, routes_ref, out_ref):
    features, per_token = tokens_ref.shape[1], routes_ref.shape[0]
    widened = tokens_ref[...].astype(jnp.float32)
    scale = lax.rsqrt(jnp.mean(widened * widened, axis=-1, keepdims=True) + 1e-06)
    out_ref[:, :features] = (widened * scale * gain_ref[...]).astype(jnp.bfloat16)
    weights = weights_ref[...]
    high = weights.astype(jnp.bfloat16).astype(jnp.float32)
    middle = (weights - high).astype(jnp.bfloat16).astype(jnp.float32)
    low = weights - high - middle
    gap = jnp.zeros((LANE - per_token, weights.shape[1]), jnp.float32)
    meta = [routes_ref[...].astype(jnp.float32), gap - 1.0, high, gap, middle, gap, low, gap]
    out_ref[: 4 * LANE, features:] = jnp.concatenate(meta, axis=0).astype(jnp.bfloat16)
    out_ref[4 * LANE :, features:] = jnp.zeros(
        (out_ref.shape[0] - 4 * LANE, weights.shape[1]), jnp.bfloat16
    )


def sum_kernel(moves_ref, *refs):
    *parts, total_ref, leave_ref = refs
    total = parts[0][...].astype(jnp.float32)
    for ref in parts[1:]:
        total = total + ref[...].astype(jnp.float32).reshape(total.shape)
    total = total.astype(jnp.bfloat16)
    total_ref[...] = total
    moved = moves_ref.shape[2]
    rows = lax.broadcasted_iota(jnp.int32, (total.shape[0], moved), 0)
    pick = (rows == moves_ref[0, 0:1, :]).astype(jnp.float32).astype(jnp.bfloat16)
    leave_ref[...] = lax.dot_general(
        pick, total, (((0,), (0,)), ((), ())), preferred_element_type=jnp.float32
    ).astype(jnp.bfloat16)


def serve_kernel(rep_ref, moves_ref, total_ref, incoming_ref, out_ref):
    moved = moves_ref.shape[2]
    rows = lax.broadcasted_iota(jnp.int32, (total_ref.shape[0], moved), 0)
    second = rep_ref[0] == 1
    target = jnp.where(second, moves_ref[0, 1:2, :], moves_ref[0, 0:1, :])
    pick = (rows == target).astype(jnp.float32)
    taken = jnp.sum(pick, axis=1, keepdims=True) > 0.5
    placed = jnp.dot(pick.astype(jnp.bfloat16), incoming_ref[...], preferred_element_type=jnp.float32)
    placed = jnp.where(second, placed, 0.0)
    out_ref[...] = jnp.where(taken, placed, total_ref[...].astype(jnp.float32)).astype(jnp.bfloat16)


def moe_kernel(
    plan, first_ref, *refs
):
    nb, exp_dev, slots, per_token, places, tiles, wide = plan
    xs, refs = refs[:nb], refs[nb:]
    gate_ref, up_ref, down_ref = refs[:3]
    refs = refs[3:]
    out_count = 1 + max(index for index, _ in places)
    outs, refs = refs[:out_count], refs[out_count:]
    gate_b, up_b, down_b, xbuf, gbuf, pbuf, tbuf, act, slotw, named_s, weight_s, wsem, xsem, osem = refs
    groups = nb // GROUP
    tok = xs[0].shape[0]
    features = down_ref.shape[2]
    rows = groups * slots

    def weight_copy(kind, e, slot):
        source = (gate_ref, up_ref, down_ref)[kind]
        target = (gate_b, up_b, down_b)[kind]
        return pltpu.make_async_copy(source.at[e], target.at[slot], wsem.at[kind, slot])

    def block_copy(g, b):
        return pltpu.make_async_copy(
            xs[g * GROUP + b], xbuf.at[g % 2, pl.ds(b * tok, tok), :], xsem.at[g % 2, b]
        )

    def load(g):
        for b in range(GROUP):
            block_copy(g, b).start()

    load(0)
    for kind in range(3):
        weight_copy(kind, 0, 0).start()
    if groups > 1:
        load(1)
    if exp_dev > 1:
        for kind in range(3):
            weight_copy(kind, 1, 1).start()

    lane = lax.broadcasted_iota(jnp.int32, (tok, tok), 1)
    sub = lax.broadcasted_iota(jnp.int32, (tok, tok), 0)
    upto = (sub <= lane).astype(jnp.bfloat16)
    pairs = exp_dev * GROUP
    pair_r = lax.broadcasted_iota(jnp.int32, (pairs, pairs), 0)
    pair_c = lax.broadcasted_iota(jnp.int32, (pairs, pairs), 1)
    before = ((pair_r // GROUP == pair_c // GROUP) & (pair_c < pair_r)).astype(jnp.bfloat16)
    slot_id = lax.broadcasted_iota(jnp.int32, (slots, tok), 0).astype(jnp.float32)
    wide_id = lax.broadcasted_iota(jnp.int32, (tok, exp_dev * slots), 1).astype(jnp.float32)
    first = first_ref[0]

    for g in range(groups):
        for b in range(GROUP):
            block_copy(g, b).wait()
        for b in range(GROUP):
            meta = xbuf[g % 2, b * tok : b * tok + 4 * LANE, features:].astype(jnp.float32)
            chosen = meta[:LANE]
            given = meta[LANE : 2 * LANE] + meta[2 * LANE : 3 * LANE] + meta[3 * LANE : 4 * LANE]
            for e in range(exp_dev):
                hit = chosen == (first + e).astype(jnp.float32)
                named_s[e * GROUP + b : e * GROUP + b + 1, :] = jnp.sum(
                    hit.astype(jnp.float32), axis=0, keepdims=True
                )
                weight_s[e * GROUP + b : e * GROUP + b + 1, :] = jnp.sum(
                    jnp.where(hit, given, 0.0), axis=0, keepdims=True
                )
        named = named_s[...]
        count = jnp.dot(named.astype(jnp.bfloat16), upto, preferred_element_type=jnp.float32)
        totals = jnp.broadcast_to(count[:, tok - 1 :], (pairs, tok)).astype(jnp.bfloat16)
        base = jnp.dot(before, totals, preferred_element_type=jnp.float32)
        named_s[...] = jnp.where(named > 0.5, base + count - 1.0, -1.0)
        for e in range(exp_dev):
            total = jnp.zeros((slots, tok), jnp.float32)
            for b in range(GROUP):
                place = named_s[e * GROUP + b : e * GROUP + b + 1, :]
                pick = slot_id == place
                pbuf[g, e * slots : (e + 1) * slots, b * tok : (b + 1) * tok] = pick.astype(
                    jnp.float32
                ).astype(jnp.bfloat16)
                total += jnp.where(pick, weight_s[e * GROUP + b : e * GROUP + b + 1, :], 0.0)
            slotw[e, g * slots : (g + 1) * slots, :] = jnp.sum(total, axis=1, keepdims=True)
        start = (lax.broadcasted_iota(jnp.int32, (pairs, tok), 0) // GROUP * slots).astype(jnp.float32)
        place = named_s[...]
        place = jnp.where(place < -0.5, place, place + start)
        place = jnp.concatenate([place, jnp.zeros((tok - pairs, tok), jnp.float32)], axis=0).T
        for b in range(GROUP):
            pick = wide_id == place[:, b : b + 1]
            for e in range(1, exp_dev):
                pick = pick | (wide_id == place[:, e * GROUP + b : e * GROUP + b + 1])
            tbuf[g, b * tok : (b + 1) * tok, :] = pick.astype(jnp.float32).astype(jnp.bfloat16)

        @pl.loop(0, features // wide)
        def _(n):
            cols = pl.ds(pl.multiple_of(n * wide, wide), wide)
            got = jnp.dot(pbuf[g], xbuf[g % 2, :, cols], preferred_element_type=jnp.float32)
            got = got.astype(jnp.bfloat16)
            for e in range(exp_dev):
                gbuf[e, g * slots : (g + 1) * slots, cols] = got[e * slots : (e + 1) * slots]

        if g + 2 < groups:
            load(g + 2)

    @pl.loop(0, exp_dev)
    def _(e):
        slot = lax.rem(e, 2)
        weight_copy(0, e, slot).wait()
        weight_copy(1, e, slot).wait()
        for start, size in tiles:
            gate = jnp.dot(
                gbuf[e], gate_b[slot, :, start : start + size], preferred_element_type=jnp.float32
            )
            upward = jnp.dot(
                gbuf[e], up_b[slot, :, start : start + size], preferred_element_type=jnp.float32
            )
            act[:, start : start + size] = (
                0.5 * gate * (1.0 + jnp.tanh(0.5 * gate)) * upward * slotw[e]
            ).astype(jnp.bfloat16)

        @pl.when(e + 2 < exp_dev)
        def _():
            weight_copy(0, e + 2, slot).start()
            weight_copy(1, e + 2, slot).start()

        weight_copy(2, e, slot).wait()

        @pl.loop(0, features // wide)
        def _(n):
            cols = pl.ds(pl.multiple_of(n * wide, wide), wide)
            gbuf[e, :, cols] = jnp.dot(
                act[...], down_b[slot, :, cols], preferred_element_type=jnp.float32
            ).astype(jnp.bfloat16)

        @pl.when(e + 2 < exp_dev)
        def _():
            weight_copy(2, e + 2, slot).start()

    def out_copy(g, b):
        index, inner = places[g * GROUP + b]
        target = outs[index] if inner is None else outs[index].at[inner]
        return pltpu.make_async_copy(
            xbuf.at[g % 2, pl.ds(b * tok, tok), pl.ds(0, features)], target, osem.at[g % 2, b]
        )

    for g in reversed(range(groups)):
        if g + 2 < groups:
            for b in range(GROUP):
                out_copy(g + 2, b).wait()

        @pl.loop(0, features // wide)
        def _(n):
            cols = pl.ds(pl.multiple_of(n * wide, wide), wide)
            made = jnp.concatenate(
                [gbuf[e, g * slots : (g + 1) * slots, cols] for e in range(exp_dev)], axis=0
            )
            xbuf[g % 2, :, cols] = jnp.dot(
                tbuf[g], made, preferred_element_type=jnp.float32
            ).astype(jnp.bfloat16)

        for b in range(GROUP):
            out_copy(g, b).start()
    for g in range(min(groups, 2)):
        for b in range(GROUP):
            out_copy(g, b).wait()


def experts_of(blocks, first, capacity, per_token, w_gate, w_up, w_down):
    nb = len(blocks)
    tok = blocks[0].shape[0]
    exp_dev, features, hidden = w_gate.shape
    cols, rows = lax.axis_size("col"), lax.axis_size("row")
    slots = -(-GROUP * capacity // 16) * 16
    groups = nb // GROUP
    wide, narrow = 512, 256
    tiles = [(start, min(narrow, hidden - start)) for start in range(0, hidden, narrow)]
    near = (rows // 2) * cols
    places = [(i, None) for i in range(near)]
    places += [(near + i // cols, i % cols) for i in range(near // 2)]
    places += [(near + near // 2 // cols + i, None) for i in range(near // 2)]
    stacked = near // 2 // cols
    block = jax.ShapeDtypeStruct((tok, features), jnp.bfloat16)
    stack = jax.ShapeDtypeStruct((cols, tok, features), jnp.bfloat16)
    shapes = [block] * near + [stack] * stacked + [block] * (near // 2)
    plan = (nb, exp_dev, slots, per_token, places, tiles, wide)
    pairs = exp_dev * GROUP
    got = pl.pallas_call(
        functools.partial(moe_kernel, plan),
        out_shape=shapes,
        in_specs=[pl.BlockSpec(memory_space=pltpu.SMEM)]
        + [pl.BlockSpec(memory_space=pl.ANY)] * (nb + 3),
        out_specs=[pl.BlockSpec(memory_space=pl.ANY)] * len(shapes),
        scratch_shapes=[
            pltpu.VMEM((2, features, hidden), jnp.bfloat16),
            pltpu.VMEM((2, features, hidden), jnp.bfloat16),
            pltpu.VMEM((2, hidden, features), jnp.bfloat16),
            pltpu.VMEM((2, GROUP * tok, features + tok), jnp.bfloat16),
            pltpu.VMEM((exp_dev, groups * slots, features), jnp.bfloat16),
            pltpu.VMEM((groups, exp_dev * slots, GROUP * tok), jnp.bfloat16),
            pltpu.VMEM((groups, GROUP * tok, exp_dev * slots), jnp.bfloat16),
            pltpu.VMEM((groups * slots, hidden), jnp.bfloat16),
            pltpu.VMEM((exp_dev, groups * slots, 1), jnp.float32),
            pltpu.VMEM((pairs, tok), jnp.float32),
            pltpu.VMEM((pairs, tok), jnp.float32),
            pltpu.SemaphoreType.DMA((3, 2)),
            pltpu.SemaphoreType.DMA((2, GROUP)),
            pltpu.SemaphoreType.DMA((2, GROUP)),
        ],
        compiler_params=pltpu.CompilerParams(vmem_limit_bytes=60 * 1024 * 1024),
        cost_estimate=pl.CostEstimate(
            flops=6 * exp_dev * groups * slots * features * hidden,
            bytes_accessed=6 * exp_dev * features * hidden + 4 * nb * tok * features,
            transcendentals=0,
        ),
        name="experts",
    )(first, *blocks, w_gate, w_up, w_down)
    lines = [list(got[i * cols : (i + 1) * cols]) for i in range(rows // 2)]
    far = list(got[near : near + stacked])
    rest = got[near + stacked :]
    far += [list(rest[i * cols : (i + 1) * cols]) for i in range(rows // 2 - stacked)]
    return lines, far


def body(tokens, norm_gain, gate_weights, routes, moves, w_gate, w_up, w_down):
    tok_rows, features = tokens.shape
    per_token = routes.shape[1]
    exp_dev = w_gate.shape[0]
    group = lax.axis_size("row") * lax.axis_size("col")
    experts = group * exp_dev
    capacity = tok_rows * per_token * 3 // (2 * experts)
    axes = ("row", "col")
    block = pl.pallas_call(
        head_kernel,
        out_shape=jax.ShapeDtypeStruct((tok_rows, features + tok_rows), jnp.bfloat16),
        name="head",
    )(tokens, norm_gain.reshape(1, features), gate_weights.T, routes.T)
    blocks = spread(block)
    first = (lax.axis_index(axes) * exp_dev).astype(jnp.int32).reshape(1)
    near, far = experts_of(blocks, first, capacity, per_token, w_gate, w_up, w_down)
    parts = [
        part if isinstance(part, tuple) else (part, None) for part in [tokens] + collected(near, far)
    ]
    moved = moves.shape[2]
    whole = pl.BlockSpec(moves.shape, lambda i: (0, 0, 0))
    rows_spec = pl.BlockSpec((tok_rows, features), lambda i: (0, 0))
    few_spec = pl.BlockSpec((moved, features), lambda i: (0, 0))
    total, leaving = pl.pallas_call(
        sum_kernel,
        grid=(1,),
        out_shape=[
            jax.ShapeDtypeStruct((tok_rows, features), jnp.bfloat16),
            jax.ShapeDtypeStruct((moved, features), jnp.bfloat16),
        ],
        in_specs=[whole] + [part_spec(value, index) for value, index in parts],
        out_specs=[rows_spec, few_spec],
        name="total",
    )(moves, *[value for value, _ in parts])
    incoming = shifted(leaving, "rep", 1)
    rep = lax.axis_index("rep").astype(jnp.int32).reshape(1)
    return pl.pallas_call(
        serve_kernel,
        grid=(1,),
        out_shape=jax.ShapeDtypeStruct((tok_rows, features), jnp.bfloat16),
        in_specs=[pl.BlockSpec(memory_space=pltpu.SMEM), whole, rows_spec, few_spec],
        out_specs=rows_spec,
        name="serve",
    )(rep, moves, total, incoming)


def solution(mesh):
    return jax.shard_map(
        body,
        mesh=mesh,
        in_specs=(
            P(("rep", "row", "col"), None),
            P(),
            P(("rep", "row", "col"), None),
            P(("rep", "row", "col"), None),
            P(("row", "col"), None, None),
            P(("row", "col"), None, None),
            P(("row", "col"), None, None),
            P(("row", "col"), None, None),
        ),
        out_specs=P(("rep", "row", "col"), None),
        check_vma=False,
    )
```

```python
import functools

import jax
import jax.numpy as jnp
from jax import lax
from jax.experimental import pallas as pl
from jax.experimental.pallas import tpu as pltpu
from jax.sharding import PartitionSpec as P

GROUP = 8
PIECES = 8
LANE = 8


def shifted(value, axis, steps):
    count = lax.axis_size(axis)
    first, last = (max(0, -steps), min(count, count - steps))
    return lax.ppermute(value, axis, [(source, source + steps) for source in range(first, last)])


def turned(value, steps):
    count = lax.axis_size("col")
    return lax.ppermute(value, "col", [(source, (source + steps) % count) for source in range(count)])


def swapped(value, bit):
    count = lax.axis_size("row")
    return lax.ppermute(value, "row", [(source, source ^ bit) for source in range(count)])


def spread(block):
    cols, rows = lax.axis_size("col"), lax.axis_size("row")
    bit = rows // 2
    line, other, last = [block], [], block
    for _ in range(1, cols):
        ahead, across = lax.optimization_barrier((turned(last, 1), swapped(last, bit)))
        line.append(ahead)
        other.append(across)
        last = ahead
    lines = [line, other + [swapped(last, bit)]]
    while bit > 1:
        bit //= 2
        lines = lines + [[swapped(one, bit) for one in line] for line in lines]
    return [one for line in lines for one in line]


def added(*parts):
    return sum(part.astype(jnp.float32) for part in parts).astype(jnp.bfloat16)


def collected(near, far):
    cols, rows = lax.axis_size("col"), lax.axis_size("row")
    order = [step for step in range(cols // 2, 0, -1)] + list(range(cols // 2 + 1, cols)) + [0]
    bit, half = 1, rows // 4
    first = [[swapped(one, bit) for one in line] for line in far[half:]]
    later = [
        [swapped(lax.optimization_barrier((one, held))[0], bit) for one, held in zip(line, holds)]
        for line, holds in zip(far[:half], first)
    ]
    there = later + first
    terms = [[list(pair) for pair in zip(line, other)] for line, other in zip(near, there)]
    bit *= 2
    while bit < rows:
        half = len(terms) // 2
        sent = []
        for line in terms[half:]:
            got = {step: swapped(added(*line[step]), bit) for step in order}
            sent.append([got[step] for step in range(cols)])
        terms = [
            [one + [other] for one, other in zip(line, others)]
            for line, others in zip(terms[:half], sent)
        ]
        bit *= 2
    line = terms[0]
    down, up = [], []
    for step in range(cols // 2, 0, -1):
        down = [turned(added(*(line[step] + down)), -1)]
    for step in range(cols // 2 + 1, cols):
        up = [turned(added(*(line[step] + up)), 1)]
    return line[0] + up + down


def head_kernel(tokens_ref, gain_ref, weights_ref, routes_ref, out_ref):
    features, per_token = tokens_ref.shape[1], routes_ref.shape[0]
    widened = tokens_ref[...].astype(jnp.float32)
    scale = lax.rsqrt(jnp.mean(widened * widened, axis=-1, keepdims=True) + 1e-06)
    out_ref[:, :features] = (widened * scale * gain_ref[...]).astype(jnp.bfloat16)
    weights = weights_ref[...]
    high = weights.astype(jnp.bfloat16).astype(jnp.float32)
    middle = (weights - high).astype(jnp.bfloat16).astype(jnp.float32)
    low = weights - high - middle
    gap = jnp.zeros((LANE - per_token, weights.shape[1]), jnp.float32)
    meta = [routes_ref[...].astype(jnp.float32), gap - 1.0, high, gap, middle, gap, low, gap]
    out_ref[: 4 * LANE, features:] = jnp.concatenate(meta, axis=0).astype(jnp.bfloat16)
    out_ref[4 * LANE :, features:] = jnp.zeros(
        (out_ref.shape[0] - 4 * LANE, weights.shape[1]), jnp.bfloat16
    )


def moe_kernel(
    plan, first_ref, *refs
):
    nb, exp_dev, slots, tiles, wide = plan
    xs, refs = refs[:nb], refs[nb:]
    gate_ref, up_ref, down_ref = refs[:3]
    refs = refs[3:]
    outs, refs = refs[:nb], refs[nb:]
    gate_b, up_b, down_b, xbuf, gbuf, pbuf, tbuf, act, slotw, named_s, weight_s, wsem, xsem, osem = refs
    groups = nb // GROUP
    tok = xs[0].shape[0]
    features = down_ref.shape[2]
    rows = groups * slots

    def weight_refs(kind, e, slot):
        source = (gate_ref, up_ref, down_ref)[kind]
        target = (gate_b, up_b, down_b)[kind]
        return source.at[e], target.at[slot], wsem.at[kind, slot]

    def fetch(kind, e, slot):
        source, target, sem = weight_refs(kind, e, slot)
        size = target.shape[0] // PIECES
        for piece in range(PIECES):
            part = pl.ds(piece * size, size)
            pltpu.make_async_copy(source.at[part, :], target.at[part, :], sem).start()

    def arrive(kind, e, slot):
        pltpu.make_async_copy(*weight_refs(kind, e, slot)).wait()

    def block_copy(g, b):
        return pltpu.make_async_copy(
            xs[g * GROUP + b], xbuf.at[g % 2, pl.ds(b * tok, tok), :], xsem.at[g % 2, b]
        )

    def load(g):
        for b in range(GROUP):
            block_copy(g, b).start()

    load(0)
    for kind in range(3):
        fetch(kind, 0, 0)
    if groups > 1:
        load(1)
    if exp_dev > 1:
        for kind in range(3):
            fetch(kind, 1, 1)

    lane = lax.broadcasted_iota(jnp.int32, (tok, tok), 1)
    sub = lax.broadcasted_iota(jnp.int32, (tok, tok), 0)
    upto = (sub <= lane).astype(jnp.bfloat16)
    pairs = exp_dev * GROUP
    pair_r = lax.broadcasted_iota(jnp.int32, (pairs, pairs), 0)
    pair_c = lax.broadcasted_iota(jnp.int32, (pairs, pairs), 1)
    before = ((pair_r // GROUP == pair_c // GROUP) & (pair_c < pair_r)).astype(jnp.bfloat16)
    slot_id = lax.broadcasted_iota(jnp.int32, (slots, tok), 0).astype(jnp.float32)
    wide_id = lax.broadcasted_iota(jnp.int32, (tok, exp_dev * slots), 1).astype(jnp.float32)
    first = first_ref[0]

    for g in range(groups):
        for b in range(GROUP):
            block_copy(g, b).wait()
        for b in range(GROUP):
            meta = xbuf[g % 2, b * tok : b * tok + 4 * LANE, features:].astype(jnp.float32)
            chosen = meta[:LANE]
            given = meta[LANE : 2 * LANE] + meta[2 * LANE : 3 * LANE] + meta[3 * LANE : 4 * LANE]
            for e in range(exp_dev):
                hit = chosen == (first + e).astype(jnp.float32)
                named_s[e * GROUP + b : e * GROUP + b + 1, :] = jnp.sum(
                    hit.astype(jnp.float32), axis=0, keepdims=True
                )
                weight_s[e * GROUP + b : e * GROUP + b + 1, :] = jnp.sum(
                    jnp.where(hit, given, 0.0), axis=0, keepdims=True
                )
        named = named_s[...]
        count = jnp.dot(named.astype(jnp.bfloat16), upto, preferred_element_type=jnp.float32)
        totals = jnp.broadcast_to(count[:, tok - 1 :], (pairs, tok)).astype(jnp.bfloat16)
        base = jnp.dot(before, totals, preferred_element_type=jnp.float32)
        named_s[...] = jnp.where(named > 0.5, base + count - 1.0, -1.0)
        for e in range(exp_dev):
            total = jnp.zeros((slots, tok), jnp.float32)
            for b in range(GROUP):
                place = named_s[e * GROUP + b : e * GROUP + b + 1, :]
                pick = slot_id == place
                pbuf[g, e * slots : (e + 1) * slots, b * tok : (b + 1) * tok] = pick.astype(
                    jnp.float32
                ).astype(jnp.bfloat16)
                total += jnp.where(pick, weight_s[e * GROUP + b : e * GROUP + b + 1, :], 0.0)
            slotw[e, g * slots : (g + 1) * slots, :] = jnp.sum(total, axis=1, keepdims=True)
        start = (lax.broadcasted_iota(jnp.int32, (pairs, tok), 0) // GROUP * slots).astype(jnp.float32)
        place = named_s[...]
        place = jnp.where(place < -0.5, place, place + start)
        place = jnp.concatenate([place, jnp.zeros((tok - pairs, tok), jnp.float32)], axis=0).T
        for b in range(GROUP):
            pick = wide_id == place[:, b : b + 1]
            for e in range(1, exp_dev):
                pick = pick | (wide_id == place[:, e * GROUP + b : e * GROUP + b + 1])
            tbuf[g, b * tok : (b + 1) * tok, :] = pick.astype(jnp.float32).astype(jnp.bfloat16)

        @pl.loop(0, features // wide)
        def _(n):
            cols = pl.ds(pl.multiple_of(n * wide, wide), wide)
            got = jnp.dot(pbuf[g], xbuf[g % 2, :, cols], preferred_element_type=jnp.float32)
            got = got.astype(jnp.bfloat16)
            for e in range(exp_dev):
                gbuf[e, g * slots : (g + 1) * slots, cols] = got[e * slots : (e + 1) * slots]

        if g + 2 < groups:
            load(g + 2)

    @pl.loop(0, exp_dev)
    def _(e):
        slot = lax.rem(e, 2)
        arrive(0, e, slot)
        arrive(1, e, slot)
        for start, size in tiles:
            gate = jnp.dot(
                gbuf[e], gate_b[slot, :, start : start + size], preferred_element_type=jnp.float32
            )
            upward = jnp.dot(
                gbuf[e], up_b[slot, :, start : start + size], preferred_element_type=jnp.float32
            )
            act[:, start : start + size] = (
                0.5 * gate * (1.0 + jnp.tanh(0.5 * gate)) * upward * slotw[e]
            ).astype(jnp.bfloat16)

        @pl.when(e + 2 < exp_dev)
        def _():
            fetch(0, e + 2, slot)
            fetch(1, e + 2, slot)

        arrive(2, e, slot)

        @pl.loop(0, features // wide)
        def _(n):
            cols = pl.ds(pl.multiple_of(n * wide, wide), wide)
            gbuf[e, :, cols] = jnp.dot(
                act[...], down_b[slot, :, cols], preferred_element_type=jnp.float32
            ).astype(jnp.bfloat16)

        @pl.when(e + 2 < exp_dev)
        def _():
            fetch(2, e + 2, slot)

    def out_copy(g, b):
        return pltpu.make_async_copy(
            xbuf.at[g % 2, pl.ds(b * tok, tok), pl.ds(0, features)],
            outs[g * GROUP + b],
            osem.at[g % 2, b],
        )

    for g in reversed(range(groups)):
        if g + 2 < groups:
            for b in range(GROUP):
                out_copy(g + 2, b).wait()

        @pl.loop(0, features // wide)
        def _(n):
            cols = pl.ds(pl.multiple_of(n * wide, wide), wide)
            made = jnp.concatenate(
                [gbuf[e, g * slots : (g + 1) * slots, cols] for e in range(exp_dev)], axis=0
            )
            xbuf[g % 2, :, cols] = jnp.dot(
                tbuf[g], made, preferred_element_type=jnp.float32
            ).astype(jnp.bfloat16)

        for b in range(GROUP):
            out_copy(g, b).start()
    for g in range(min(groups, 2)):
        for b in range(GROUP):
            out_copy(g, b).wait()


def experts_of(blocks, first, capacity, w_gate, w_up, w_down):
    nb = len(blocks)
    tok = blocks[0].shape[0]
    exp_dev, features, hidden = w_gate.shape
    cols, rows = lax.axis_size("col"), lax.axis_size("row")
    slots = -(-GROUP * capacity // 16) * 16
    groups = nb // GROUP
    wide, narrow = 512, 256
    tiles = [(start, min(narrow, hidden - start)) for start in range(0, hidden, narrow)]
    block = jax.ShapeDtypeStruct((tok, features), jnp.bfloat16)
    shapes = [block] * nb
    plan = (nb, exp_dev, slots, tiles, wide)
    pairs = exp_dev * GROUP
    got = pl.pallas_call(
        functools.partial(moe_kernel, plan),
        out_shape=shapes,
        in_specs=[pl.BlockSpec(memory_space=pltpu.SMEM)]
        + [pl.BlockSpec(memory_space=pl.ANY)] * (nb + 3),
        out_specs=[pl.BlockSpec(memory_space=pl.ANY)] * len(shapes),
        scratch_shapes=[
            pltpu.VMEM((2, features, hidden), jnp.bfloat16),
            pltpu.VMEM((2, features, hidden), jnp.bfloat16),
            pltpu.VMEM((2, hidden, features), jnp.bfloat16),
            pltpu.VMEM((2, GROUP * tok, features + tok), jnp.bfloat16),
            pltpu.VMEM((exp_dev, groups * slots, features), jnp.bfloat16),
            pltpu.VMEM((groups, exp_dev * slots, GROUP * tok), jnp.bfloat16),
            pltpu.VMEM((groups, GROUP * tok, exp_dev * slots), jnp.bfloat16),
            pltpu.VMEM((groups * slots, hidden), jnp.bfloat16),
            pltpu.VMEM((exp_dev, groups * slots, 1), jnp.float32),
            pltpu.VMEM((pairs, tok), jnp.float32),
            pltpu.VMEM((pairs, tok), jnp.float32),
            pltpu.SemaphoreType.DMA((3, 2)),
            pltpu.SemaphoreType.DMA((2, GROUP)),
            pltpu.SemaphoreType.DMA((2, GROUP)),
        ],
        compiler_params=pltpu.CompilerParams(vmem_limit_bytes=60 * 1024 * 1024),
        cost_estimate=pl.CostEstimate(
            flops=6 * exp_dev * groups * slots * features * hidden,
            bytes_accessed=6 * exp_dev * features * hidden + 4 * nb * tok * features,
            transcendentals=0,
        ),
        name="experts",
    )(first, *blocks, w_gate, w_up, w_down)
    lines = [list(got[i * cols : (i + 1) * cols]) for i in range(rows)]
    return lines[: rows // 2], lines[rows // 2 :]


def body(tokens, norm_gain, gate_weights, routes, moves, w_gate, w_up, w_down):
    tok_rows, features = tokens.shape
    per_token = routes.shape[1]
    exp_dev = w_gate.shape[0]
    group = lax.axis_size("row") * lax.axis_size("col")
    experts = group * exp_dev
    capacity = tok_rows * per_token * 3 // (2 * experts)
    axes = ("row", "col")
    block = pl.pallas_call(
        head_kernel,
        out_shape=jax.ShapeDtypeStruct((tok_rows, features + tok_rows), jnp.bfloat16),
        name="head",
    )(tokens, norm_gain.reshape(1, features), gate_weights.T, routes.T)
    blocks = spread(block)
    first = (lax.axis_index(axes) * exp_dev).astype(jnp.int32).reshape(1)
    near, far = experts_of(blocks, first, capacity, w_gate, w_up, w_down)
    total = added(tokens, *collected(near, far))
    rows = jnp.arange(tok_rows, dtype=jnp.int32)
    pick = (moves[0, 0][:, None] == rows[None, :]).astype(jnp.bfloat16)
    leaving = jnp.dot(pick, total, preferred_element_type=jnp.float32).astype(jnp.bfloat16)
    incoming = shifted(leaving, "rep", 1)
    second = lax.axis_index("rep") == 1
    target = jnp.where(second, moves[0, 1], moves[0, 0])
    match = rows[:, None] == target[None, :]
    placed = jnp.dot(match.astype(jnp.bfloat16), incoming, preferred_element_type=jnp.float32)
    placed = jnp.where(second, placed, 0.0).astype(jnp.bfloat16)
    return jnp.where(jnp.any(match, axis=1, keepdims=True), placed, total)


def solution(mesh):
    return jax.shard_map(
        body,
        mesh=mesh,
        in_specs=(
            P(("rep", "row", "col"), None),
            P(),
            P(("rep", "row", "col"), None),
            P(("rep", "row", "col"), None),
            P(("row", "col"), None, None),
            P(("row", "col"), None, None),
            P(("row", "col"), None, None),
            P(("row", "col"), None, None),
        ),
        out_specs=P(("rep", "row", "col"), None),
        check_vma=False,
    )
```

```python
import functools

import jax
import jax.numpy as jnp
from jax import lax
from jax.experimental import pallas as pl
from jax.experimental.pallas import tpu as pltpu
from jax.sharding import PartitionSpec as P

GROUP = 8
PIECES = 4
LANE = 8
WIDE = 512
NARROW = 256
LIMIT = 60 * 1024 * 1024
LIGHT = pl.CostEstimate(flops=1, bytes_accessed=1, transcendentals=0)


def shifted(value, axis, steps):
    count = lax.axis_size(axis)
    first, last = (max(0, -steps), min(count, count - steps))
    return lax.ppermute(value, axis, [(source, source + steps) for source in range(first, last)])


def turned(value, steps):
    count = lax.axis_size("col")
    return lax.ppermute(value, "col", [(source, (source + steps) % count) for source in range(count)])


def swapped(value, bit):
    count = lax.axis_size("row")
    return lax.ppermute(value, "row", [(source, source ^ bit) for source in range(count)])


def spread(halves, gather):
    line, other, last = [halves], [], halves
    for _ in range(1, lax.axis_size("col")):
        pairs = [lax.optimization_barrier((turned(one, 1), swapped(one, 2))) for one in last]
        last = [ahead for ahead, _ in pairs]
        line.append(last)
        other.append([across for _, across in pairs])
    ready = gather(line + [[swapped(one, 1) for one in block] for block in line])
    final = [swapped(one, 2) for one in last]
    held = lax.optimization_barrier((*final, ready[2]))[: len(final)]
    far = [[swapped(one, 1) for one in block] for block in other + [list(held)]]
    return ready, other + [final] + far


def added(*parts):
    return sum(part.astype(jnp.float32) for part in parts).astype(jnp.bfloat16)


def collected(late, early):
    cols = lax.axis_size("col")
    order = list(range(cols // 2, 0, -1)) + list(range(cols // 2 + 1, cols)) + [0]
    held = {step: swapped(late[cols + step], 1) for step in order}
    sent = {step: swapped(added(late[step], held[step]), 2) for step in order}
    far = {
        step: swapped(lax.optimization_barrier((early[cols + step], held[step]))[0], 1)
        for step in order
    }
    line = [[early[step], far[step], sent[step]] for step in range(cols)]
    down, up = [], []
    for step in range(cols // 2, 0, -1):
        down = [turned(added(*(line[step] + down)), -1)]
        if step == cols // 2:
            ahead = down[0]
    for step in range(cols // 2 + 1, cols):
        value = added(*(line[step] + up))
        if not up:
            value = lax.optimization_barrier((value, ahead))[0]
        up = [turned(value, 1)]
    return line[0] + up + down


def head_kernel(tokens_ref, gain_ref, weights_ref, routes_ref, *outs):
    features, per_token = tokens_ref.shape[1], routes_ref.shape[0]
    widened = tokens_ref[...].astype(jnp.float32)
    scale = lax.rsqrt(jnp.mean(widened * widened, axis=-1, keepdims=True) + 1e-06)
    normed = (widened * scale * gain_ref[...]).astype(jnp.bfloat16)
    half = outs[0].shape[0]
    for i, out_ref in enumerate(outs):
        out_ref[:, :features] = normed[i * half : (i + 1) * half]
    weights = weights_ref[...]
    high = weights.astype(jnp.bfloat16).astype(jnp.float32)
    middle = (weights - high).astype(jnp.bfloat16).astype(jnp.float32)
    low = weights - high - middle
    gap = jnp.zeros((LANE - per_token, weights.shape[1]), jnp.float32)
    meta = [routes_ref[...].astype(jnp.float32), gap - 1.0, high, gap, middle, gap, low, gap]
    outs[0][: 4 * LANE, features:] = jnp.concatenate(meta, axis=0).astype(jnp.bfloat16)
    outs[0][4 * LANE :, features:] = jnp.zeros(
        (half - 4 * LANE, weights.shape[1]), jnp.bfloat16
    )


def gather_groups(xs, first, slots, xbuf, xsem, named_s, weight_s, pbuf, tbuf, put_weight, put_rows):
    groups = len(xs) // (2 * GROUP)
    half = xs[0].shape[0]
    tok = 2 * half
    features = xs[1].shape[1]
    pairs = named_s.shape[0]
    exp_dev = pairs // GROUP

    def copies(g):
        for b in range(GROUP):
            for h in range(2):
                source = xs[2 * (g * GROUP + b) + h]
                target = xbuf.at[
                    g % 2, pl.ds(b * tok + h * half, half), pl.ds(0, source.shape[1])
                ]
                yield pltpu.make_async_copy(source, target, xsem.at[g % 2, 2 * b + h])

    def load(g):
        for copy in copies(g):
            copy.start()

    for g in range(min(2, groups)):
        load(g)
    lane = lax.broadcasted_iota(jnp.int32, (tok, tok), 1)
    sub = lax.broadcasted_iota(jnp.int32, (tok, tok), 0)
    upto = (sub <= lane).astype(jnp.bfloat16)
    pair_r = lax.broadcasted_iota(jnp.int32, (pairs, pairs), 0)
    pair_c = lax.broadcasted_iota(jnp.int32, (pairs, pairs), 1)
    before = ((pair_r // GROUP == pair_c // GROUP) & (pair_c < pair_r)).astype(jnp.bfloat16)
    slot_id = lax.broadcasted_iota(jnp.int32, (slots, tok), 0).astype(jnp.float32)
    wide_id = lax.broadcasted_iota(jnp.int32, (tok, exp_dev * slots), 1).astype(jnp.float32)
    offset = lax.broadcasted_iota(jnp.int32, (pairs, tok), 0) // GROUP * slots
    offset = offset.astype(jnp.float32)

    for g in range(groups):
        for copy in copies(g):
            copy.wait()
        for b in range(GROUP):
            meta = xbuf[g % 2, b * tok : b * tok + 4 * LANE, features:].astype(jnp.float32)
            chosen = meta[:LANE]
            given = meta[LANE : 2 * LANE] + meta[2 * LANE : 3 * LANE] + meta[3 * LANE : 4 * LANE]
            for e in range(exp_dev):
                hit = chosen == (first + e).astype(jnp.float32)
                named_s[e * GROUP + b : e * GROUP + b + 1, :] = jnp.sum(
                    hit.astype(jnp.float32), axis=0, keepdims=True
                )
                weight_s[e * GROUP + b : e * GROUP + b + 1, :] = jnp.sum(
                    jnp.where(hit, given, 0.0), axis=0, keepdims=True
                )
        named = named_s[...]
        count = jnp.dot(named.astype(jnp.bfloat16), upto, preferred_element_type=jnp.float32)
        totals = jnp.broadcast_to(count[:, tok - 1 :], (pairs, tok)).astype(jnp.bfloat16)
        base = jnp.dot(before, totals, preferred_element_type=jnp.float32)
        named_s[...] = jnp.where(named > 0.5, base + count - 1.0, -1.0)
        for e in range(exp_dev):
            total = jnp.zeros((slots, tok), jnp.float32)
            for b in range(GROUP):
                pick = slot_id == named_s[e * GROUP + b : e * GROUP + b + 1, :]
                pbuf[e * slots : (e + 1) * slots, b * tok : (b + 1) * tok] = pick.astype(
                    jnp.float32
                ).astype(jnp.bfloat16)
                total += jnp.where(pick, weight_s[e * GROUP + b : e * GROUP + b + 1, :], 0.0)
            put_weight(g, e, jnp.sum(total, axis=1, keepdims=True))
        place = named_s[...]
        place = jnp.where(place < -0.5, place, place + offset)
        place = jnp.concatenate([place, jnp.zeros((tok - pairs, tok), jnp.float32)], axis=0).T
        for b in range(GROUP):
            pick = wide_id == place[:, b : b + 1]
            for e in range(1, exp_dev):
                pick = pick | (wide_id == place[:, e * GROUP + b : e * GROUP + b + 1])
            tbuf[g, b * tok : (b + 1) * tok, :] = pick.astype(jnp.float32).astype(jnp.bfloat16)

        @pl.loop(0, features // WIDE)
        def _(n):
            cols = pl.ds(pl.multiple_of(n * WIDE, WIDE), WIDE)
            got = jnp.dot(pbuf[...], xbuf[g % 2, :, cols], preferred_element_type=jnp.float32)
            got = got.astype(jnp.bfloat16)
            for e in range(exp_dev):
                put_rows(g, e, cols, got[e * slots : (e + 1) * slots])

        if g + 2 < groups:
            load(g + 2)


def early_kernel(plan, first_ref, *refs):
    nb, slots = plan
    xs, refs = refs[: 2 * nb], refs[2 * nb :]
    rows_ref, tbuf, slotw, xbuf, pbuf, named_s, weight_s, xsem = refs

    def put_weight(g, e, value):
        slotw[e, g * slots : (g + 1) * slots, :] = value

    def put_rows(g, e, cols, value):
        rows_ref[e, g * slots : (g + 1) * slots, cols] = value

    gather_groups(
        xs, first_ref[0], slots, xbuf, xsem, named_s, weight_s, pbuf, tbuf, put_weight, put_rows
    )


def expert_kernel(plan, first_ref, *refs):
    nb, exp_dev, slots, tiles = plan
    xs, refs = refs[: 2 * nb], refs[2 * nb :]
    rows_ref, table_ref, slotw_ref, gate_ref, up_ref, down_ref = refs[:6]
    outs, refs = refs[6 : 6 + 2 * nb], refs[6 + 2 * nb :]
    gate_b, up_b, down_b, xbuf, gbuf, pbuf, tbuf, act, slotw = refs[:9]
    named_s, weight_s, wsem, xsem, osem, rsem = refs[9:]
    groups = nb // GROUP
    tok = outs[0].shape[0]
    features = down_ref.shape[2]
    early = groups * slots

    def weight_refs(kind, e, slot):
        source = (gate_ref, up_ref, down_ref)[kind]
        target = (gate_b, up_b, down_b)[kind]
        return source.at[e], target.at[slot], wsem.at[kind, slot]

    def fetch(kind, e, slot):
        source, target, sem = weight_refs(kind, e, slot)
        size = target.shape[0] // PIECES
        for piece in range(PIECES):
            part = pl.ds(piece * size, size)
            pltpu.make_async_copy(source.at[part, :], target.at[part, :], sem).start()

    def arrive(kind, e, slot):
        pltpu.make_async_copy(*weight_refs(kind, e, slot)).wait()

    def rows_copy(e):
        return pltpu.make_async_copy(rows_ref.at[e], gbuf.at[e, pl.ds(0, early), :], rsem.at[e])

    def put_weight(g, e, value):
        slotw[e, early + g * slots : early + (g + 1) * slots, :] = value

    def put_rows(g, e, cols, value):
        gbuf[e, early + g * slots : early + (g + 1) * slots, cols] = value

    for e in range(exp_dev):
        rows_copy(e).start()
    for e in range(min(2, exp_dev)):
        for kind in range(3):
            fetch(kind, e, e)
    slotw[:, :early, :] = slotw_ref[...]
    gather_groups(
        xs, first_ref[0], slots, xbuf, xsem, named_s, weight_s, pbuf, tbuf, put_weight, put_rows
    )

    @pl.loop(0, exp_dev)
    def _(e):
        slot = lax.rem(e, 2)
        rows_copy(e).wait()
        arrive(0, e, slot)
        arrive(1, e, slot)
        for start, size in tiles:
            gate = jnp.dot(
                gbuf[e], gate_b[slot, :, start : start + size], preferred_element_type=jnp.float32
            )
            upward = jnp.dot(
                gbuf[e], up_b[slot, :, start : start + size], preferred_element_type=jnp.float32
            )
            act[:, start : start + size] = (
                0.5 * gate * (1.0 + jnp.tanh(0.5 * gate)) * upward * slotw[e]
            ).astype(jnp.bfloat16)

        @pl.when(e + 2 < exp_dev)
        def _():
            fetch(0, e + 2, slot)
            fetch(1, e + 2, slot)

        arrive(2, e, slot)

        @pl.loop(0, features // WIDE)
        def _(n):
            cols = pl.ds(pl.multiple_of(n * WIDE, WIDE), WIDE)
            gbuf[e, :, cols] = jnp.dot(
                act[...], down_b[slot, :, cols], preferred_element_type=jnp.float32
            ).astype(jnp.bfloat16)

        @pl.when(e + 2 < exp_dev)
        def _():
            fetch(2, e + 2, slot)

    def out_copy(g, b):
        return pltpu.make_async_copy(
            xbuf.at[g % 2, pl.ds(b * tok, tok), pl.ds(0, features)],
            outs[g * GROUP + b],
            osem.at[g % 2, b],
        )

    tables = [tbuf.at[g] for g in range(groups)] + [table_ref.at[g] for g in range(groups)]
    starts = [early + g * slots for g in range(groups)] + [g * slots for g in range(groups)]
    for g in range(2 * groups):
        if g >= 2:
            for b in range(GROUP):
                out_copy(g - 2, b).wait()

        @pl.loop(0, features // WIDE)
        def _(n):
            cols = pl.ds(pl.multiple_of(n * WIDE, WIDE), WIDE)
            here = starts[g]
            made = jnp.concatenate(
                [gbuf[e, here : here + slots, cols] for e in range(exp_dev)], axis=0
            )
            xbuf[g % 2, :, cols] = jnp.dot(
                tables[g][...], made, preferred_element_type=jnp.float32
            ).astype(jnp.bfloat16)

        for b in range(GROUP):
            out_copy(g, b).start()
    for g in range(2 * groups - 2, 2 * groups):
        for b in range(GROUP):
            out_copy(g, b).wait()


def sizes(blocks, capacity, exp_dev):
    slots = -(-GROUP * capacity // 16) * 16
    return len(blocks), 2 * blocks[0][0].shape[0], slots, len(blocks) // GROUP, exp_dev * GROUP


def scratch(tok, features, exp_dev, slots):
    return [
        pltpu.VMEM((2, GROUP * tok, features + tok), jnp.bfloat16),
        pltpu.VMEM((exp_dev * slots, GROUP * tok), jnp.bfloat16),
        pltpu.VMEM((exp_dev * GROUP, tok), jnp.float32),
    ]


def gathered(blocks, first, capacity, exp_dev):
    nb, tok, slots, groups, _ = sizes(blocks, capacity, exp_dev)
    features = blocks[0][1].shape[1]
    xbuf, pbuf, small = scratch(tok, features, exp_dev, slots)
    return pl.pallas_call(
        functools.partial(early_kernel, (nb, slots)),
        out_shape=[
            jax.ShapeDtypeStruct((exp_dev, groups * slots, features), jnp.bfloat16),
            jax.ShapeDtypeStruct((groups, GROUP * tok, exp_dev * slots), jnp.bfloat16),
            jax.ShapeDtypeStruct((exp_dev, groups * slots, 1), jnp.float32),
        ],
        in_specs=[pl.BlockSpec(memory_space=pltpu.SMEM)]
        + [pl.BlockSpec(memory_space=pl.ANY)] * (2 * nb),
        out_specs=[pl.BlockSpec(memory_space=pltpu.VMEM)] * 3,
        scratch_shapes=[xbuf, pbuf, small, small, pltpu.SemaphoreType.DMA((2, 2 * GROUP))],
        compiler_params=pltpu.CompilerParams(vmem_limit_bytes=LIMIT // 2),
        cost_estimate=LIGHT,
        name="early",
    )(first, *[half for block in blocks for half in block])


def experts_of(ready, late, first, capacity, w_gate, w_up, w_down):
    rows, table, slotw = ready
    exp_dev, features, hidden = w_gate.shape
    nb, tok, slots, groups, pairs = sizes(late, capacity, exp_dev)
    tiles = [(start, min(NARROW, hidden - start)) for start in range(0, hidden, NARROW)]
    smem = pl.BlockSpec(memory_space=pltpu.SMEM)
    anywhere = pl.BlockSpec(memory_space=pl.ANY)
    vmem = pl.BlockSpec(memory_space=pltpu.VMEM)
    xbuf, pbuf, small = scratch(tok, features, exp_dev, slots)
    moving = 2 * groups * GROUP * tok * features * exp_dev * slots
    got = pl.pallas_call(
        functools.partial(expert_kernel, (nb, exp_dev, slots, tiles)),
        out_shape=[jax.ShapeDtypeStruct((tok, features), jnp.bfloat16)] * (2 * nb),
        in_specs=[smem] + [anywhere] * (2 * nb + 1) + [vmem] * 2 + [anywhere] * 3,
        out_specs=[anywhere] * (2 * nb),
        scratch_shapes=[
            pltpu.VMEM((2, features, hidden), jnp.bfloat16),
            pltpu.VMEM((2, features, hidden), jnp.bfloat16),
            pltpu.VMEM((2, hidden, features), jnp.bfloat16),
            xbuf,
            pltpu.VMEM((exp_dev, 2 * groups * slots, features), jnp.bfloat16),
            pbuf,
            pltpu.VMEM(table.shape, jnp.bfloat16),
            pltpu.VMEM((2 * groups * slots, hidden), jnp.bfloat16),
            pltpu.VMEM((exp_dev, 2 * groups * slots, 1), jnp.float32),
            small,
            small,
            pltpu.SemaphoreType.DMA((3, 2)),
            pltpu.SemaphoreType.DMA((2, 2 * GROUP)),
            pltpu.SemaphoreType.DMA((2, GROUP)),
            pltpu.SemaphoreType.DMA((exp_dev,)),
        ],
        compiler_params=pltpu.CompilerParams(vmem_limit_bytes=LIMIT),
        cost_estimate=pl.CostEstimate(
            flops=12 * exp_dev * groups * slots * features * hidden + 2 * moving,
            bytes_accessed=6 * exp_dev * features * hidden + 4 * nb * tok * features,
            transcendentals=0,
        ),
        name="experts",
    )(first, *[half for block in late for half in block], rows, table, slotw, w_gate, w_up, w_down)
    return list(got[:nb]), list(got[nb:])


def body(tokens, norm_gain, gate_weights, routes, moves, w_gate, w_up, w_down):
    tok_rows, features = tokens.shape
    per_token = routes.shape[1]
    exp_dev = w_gate.shape[0]
    group = lax.axis_size("row") * lax.axis_size("col")
    experts = group * exp_dev
    capacity = tok_rows * per_token * 3 // (2 * experts)
    half = tok_rows // 2
    halves = pl.pallas_call(
        head_kernel,
        out_shape=[
            jax.ShapeDtypeStruct((half, features + tok_rows), jnp.bfloat16),
            jax.ShapeDtypeStruct((half, features), jnp.bfloat16),
        ],
        name="head",
    )(tokens, norm_gain.reshape(1, features), gate_weights.T, routes.T)
    first = (lax.axis_index(("row", "col")) * exp_dev).astype(jnp.int32).reshape(1)
    ready, late = spread(
        list(halves), lambda blocks: gathered(blocks, first, capacity, exp_dev)
    )
    late, early = experts_of(ready, late, first, capacity, w_gate, w_up, w_down)
    total = added(tokens, *collected(late, early))
    rows = jnp.arange(tok_rows, dtype=jnp.int32)
    pick = (moves[0, 0][:, None] == rows[None, :]).astype(jnp.bfloat16)
    leaving = jnp.dot(pick, total, preferred_element_type=jnp.float32).astype(jnp.bfloat16)
    incoming = shifted(leaving, "rep", 1)
    second = lax.axis_index("rep") == 1
    target = jnp.where(second, moves[0, 1], moves[0, 0])
    match = rows[:, None] == target[None, :]
    placed = jnp.dot(match.astype(jnp.bfloat16), incoming, preferred_element_type=jnp.float32)
    placed = jnp.where(second, placed, 0.0).astype(jnp.bfloat16)
    return jnp.where(jnp.any(match, axis=1, keepdims=True), placed, total)


def solution(mesh):
    return jax.shard_map(
        body,
        mesh=mesh,
        in_specs=(
            P(("rep", "row", "col"), None),
            P(),
            P(("rep", "row", "col"), None),
            P(("rep", "row", "col"), None),
            P(("row", "col"), None, None),
            P(("row", "col"), None, None),
            P(("row", "col"), None, None),
            P(("row", "col"), None, None),
        ),
        out_specs=P(("rep", "row", "col"), None),
        check_vma=False,
    )
```

```python
import functools

import jax
import jax.numpy as jnp
from jax import lax
from jax.experimental import pallas as pl
from jax.experimental.pallas import tpu as pltpu
from jax.sharding import PartitionSpec as P

GROUP = 8
PIECES = 4
LANE = 8
WIDE = 512
NARROW = 256
LIMIT = 60 * 1024 * 1024
LIGHT = pl.CostEstimate(flops=1, bytes_accessed=1, transcendentals=0)


def shifted(value, axis, steps):
    count = lax.axis_size(axis)
    first, last = (max(0, -steps), min(count, count - steps))
    return lax.ppermute(value, axis, [(source, source + steps) for source in range(first, last)])


def turned(value, steps):
    count = lax.axis_size("col")
    return lax.ppermute(value, "col", [(source, (source + steps) % count) for source in range(count)])


def swapped(value, bit):
    count = lax.axis_size("row")
    return lax.ppermute(value, "row", [(source, source ^ bit) for source in range(count)])


def spread(halves, gather):
    line, other, last = [halves], [], halves
    for _ in range(1, lax.axis_size("col")):
        pairs = [lax.optimization_barrier((turned(one, 1), swapped(one, 2))) for one in last]
        last = [ahead for ahead, _ in pairs]
        line.append(last)
        other.append([across for _, across in pairs])
    ready = gather(line + [[swapped(one, 1) for one in block] for block in line])
    final = [swapped(one, 2) for one in last]
    held = lax.optimization_barrier((*final, ready[2]))[: len(final)]
    far = [[swapped(one, 1) for one in block] for block in other + [list(held)]]
    return ready, other + [final] + far


def added(*parts):
    return sum(part.astype(jnp.float32) for part in parts).astype(jnp.bfloat16)


def collected(near_late, far_late, near_early, far_early, held=()):
    cols = lax.axis_size("col")
    order = list(range(cols // 2, 0, -1)) + list(range(cols // 2 + 1, cols)) + [0]
    held = swapped(lax.optimization_barrier((far_late, *held))[0], 1)
    sums = {step: added(near_late[step], held[step]) for step in order}
    sent = {step: swapped(sums[step], 2) for step in order}
    far = swapped(lax.optimization_barrier((far_early, held))[0], 1)
    line = [[near_early[step], far[step], sent[step]] for step in range(cols)]
    down, up = [], []
    for step in range(cols // 2, 0, -1):
        down = [turned(added(*(line[step] + down)), -1)]
        if step == cols // 2:
            ahead = down[0]
    for step in range(cols // 2 + 1, cols):
        value = added(*(line[step] + up))
        if not up:
            value = lax.optimization_barrier((value, ahead))[0]
        up = [turned(value, 1)]
    return line[0] + up + down, sums[order[-1]], tuple(sent[step] for step in order[:-1])


def head_kernel(tokens_ref, gain_ref, weights_ref, routes_ref, *outs):
    features, per_token = tokens_ref.shape[1], routes_ref.shape[0]
    widened = tokens_ref[...].astype(jnp.float32)
    scale = lax.rsqrt(jnp.mean(widened * widened, axis=-1, keepdims=True) + 1e-06)
    normed = (widened * scale * gain_ref[...]).astype(jnp.bfloat16)
    half = outs[0].shape[0]
    for i, out_ref in enumerate(outs):
        out_ref[:, :features] = normed[i * half : (i + 1) * half]
    weights = weights_ref[...]
    high = weights.astype(jnp.bfloat16).astype(jnp.float32)
    middle = (weights - high).astype(jnp.bfloat16).astype(jnp.float32)
    low = weights - high - middle
    gap = jnp.zeros((LANE - per_token, weights.shape[1]), jnp.float32)
    meta = [routes_ref[...].astype(jnp.float32), gap - 1.0, high, gap, middle, gap, low, gap]
    outs[0][: 4 * LANE, features:] = jnp.concatenate(meta, axis=0).astype(jnp.bfloat16)
    outs[0][4 * LANE :, features:] = jnp.zeros(
        (half - 4 * LANE, weights.shape[1]), jnp.bfloat16
    )


def gather_groups(xs, first, slots, xbuf, xsem, named_s, weight_s, pbuf, tbuf, put_weight, put_rows, begin=None):
    groups = len(xs) // (2 * GROUP)
    half = xs[0].shape[0]
    tok = 2 * half
    features = xs[1].shape[1]
    pairs = named_s.shape[0]
    exp_dev = pairs // GROUP

    def copies(g):
        for b in range(GROUP):
            for h in range(2):
                source = xs[2 * (g * GROUP + b) + h]
                target = xbuf.at[
                    g % 2, pl.ds(b * tok + h * half, half), pl.ds(0, source.shape[1])
                ]
                yield pltpu.make_async_copy(source, target, xsem.at[g % 2, 2 * b + h])

    def load(g):
        for copy in copies(g):
            copy.start()

    for g in range(min(2, groups)):
        load(g)
    if begin is not None:
        begin()
    lane = lax.broadcasted_iota(jnp.int32, (tok, tok), 1)
    sub = lax.broadcasted_iota(jnp.int32, (tok, tok), 0)
    upto = (sub <= lane).astype(jnp.bfloat16)
    pair_r = lax.broadcasted_iota(jnp.int32, (pairs, pairs), 0)
    pair_c = lax.broadcasted_iota(jnp.int32, (pairs, pairs), 1)
    before = ((pair_r // GROUP == pair_c // GROUP) & (pair_c < pair_r)).astype(jnp.bfloat16)
    slot_id = lax.broadcasted_iota(jnp.int32, (slots, tok), 0).astype(jnp.float32)
    wide_id = lax.broadcasted_iota(jnp.int32, (tok, exp_dev * slots), 1).astype(jnp.float32)
    offset = lax.broadcasted_iota(jnp.int32, (pairs, tok), 0) // GROUP * slots
    offset = offset.astype(jnp.float32)

    for g in range(groups):
        for copy in copies(g):
            copy.wait()
        for b in range(GROUP):
            meta = xbuf[g % 2, b * tok : b * tok + 4 * LANE, features:].astype(jnp.float32)
            chosen = meta[:LANE]
            given = meta[LANE : 2 * LANE] + meta[2 * LANE : 3 * LANE] + meta[3 * LANE : 4 * LANE]
            for e in range(exp_dev):
                hit = chosen == (first + e).astype(jnp.float32)
                named_s[e * GROUP + b : e * GROUP + b + 1, :] = jnp.sum(
                    hit.astype(jnp.float32), axis=0, keepdims=True
                )
                weight_s[e * GROUP + b : e * GROUP + b + 1, :] = jnp.sum(
                    jnp.where(hit, given, 0.0), axis=0, keepdims=True
                )
        named = named_s[...]
        count = jnp.dot(named.astype(jnp.bfloat16), upto, preferred_element_type=jnp.float32)
        totals = jnp.broadcast_to(count[:, tok - 1 :], (pairs, tok)).astype(jnp.bfloat16)
        base = jnp.dot(before, totals, preferred_element_type=jnp.float32)
        named_s[...] = jnp.where(named > 0.5, base + count - 1.0, -1.0)
        for e in range(exp_dev):
            total = jnp.zeros((slots, tok), jnp.float32)
            for b in range(GROUP):
                pick = slot_id == named_s[e * GROUP + b : e * GROUP + b + 1, :]
                pbuf[e * slots : (e + 1) * slots, b * tok : (b + 1) * tok] = pick.astype(
                    jnp.float32
                ).astype(jnp.bfloat16)
                total += jnp.where(pick, weight_s[e * GROUP + b : e * GROUP + b + 1, :], 0.0)
            put_weight(g, e, jnp.sum(total, axis=1, keepdims=True))
        place = named_s[...]
        place = jnp.where(place < -0.5, place, place + offset)
        place = jnp.concatenate([place, jnp.zeros((tok - pairs, tok), jnp.float32)], axis=0).T
        for b in range(GROUP):
            pick = wide_id == place[:, b : b + 1]
            for e in range(1, exp_dev):
                pick = pick | (wide_id == place[:, e * GROUP + b : e * GROUP + b + 1])
            tbuf[g, b * tok : (b + 1) * tok, :] = pick.astype(jnp.float32).astype(jnp.bfloat16)

        @pl.loop(0, features // WIDE)
        def _(n):
            cols = pl.ds(pl.multiple_of(n * WIDE, WIDE), WIDE)
            got = jnp.dot(pbuf[...], xbuf[g % 2, :, cols], preferred_element_type=jnp.float32)
            got = got.astype(jnp.bfloat16)
            for e in range(exp_dev):
                put_rows(g, e, cols, got[e * slots : (e + 1) * slots])

        if g + 2 < groups:
            load(g + 2)


def early_kernel(plan, first_ref, *refs):
    nb, slots = plan
    xs, refs = refs[: 2 * nb], refs[2 * nb :]
    rows_ref, tbuf, slotw, xbuf, pbuf, named_s, weight_s, xsem = refs

    def put_weight(g, e, value):
        slotw[e, g * slots : (g + 1) * slots, :] = value

    def put_rows(g, e, cols, value):
        rows_ref[e, g * slots : (g + 1) * slots, cols] = value

    gather_groups(
        xs, first_ref[0], slots, xbuf, xsem, named_s, weight_s, pbuf, tbuf, put_weight, put_rows
    )


def place_of(index, cols, stacks):
    return stacks[index // cols].at[index % cols]


def expert_kernel(plan, first_ref, *refs):
    nb, exp_dev, slots, tiles, cols_here = plan
    xs, refs = refs[: 2 * nb], refs[2 * nb :]
    rows_ref, table_ref, slotw_ref, gate_ref, up_ref, down_ref = refs[:6]
    outs, refs = refs[6:10], refs[10:]
    act_ref, table_out, gate_b, up_b, down_b, xbuf, gbuf, pbuf, tbuf, act, slotw = refs[:11]
    named_s, weight_s, wsem, xsem, osem, rsem, asem, tsem = refs[11:]
    groups = nb // GROUP
    tok = outs[0].shape[1]
    part = outs[0].shape[2]
    early = groups * slots

    def weight_refs(kind, e, slot):
        source = (gate_ref, up_ref, down_ref)[kind].at[e]
        if kind == 2:
            source = source.at[:, pl.ds(0, part)]
        target = (gate_b, up_b, down_b)[kind]
        return source, target.at[slot], wsem.at[kind, slot]

    def fetch(kind, e, slot):
        source, target, sem = weight_refs(kind, e, slot)
        size = target.shape[0] // PIECES
        for piece in range(PIECES):
            rows = pl.ds(piece * size, size)
            pltpu.make_async_copy(source.at[rows, :], target.at[rows, :], sem).start()

    def arrive(kind, e, slot):
        pltpu.make_async_copy(*weight_refs(kind, e, slot)).wait()

    def rows_copy(e):
        return pltpu.make_async_copy(rows_ref.at[e], gbuf.at[e, pl.ds(0, early), :], rsem.at[e])

    def act_copy(e):
        return pltpu.make_async_copy(act.at[e], act_ref.at[e], asem.at[e])

    table_in = pltpu.make_async_copy(table_ref, tbuf.at[pl.ds(groups, groups)], tsem.at[0])
    table_back = pltpu.make_async_copy(tbuf.at[pl.ds(0, groups)], table_out, tsem.at[1])

    def put_weight(g, e, value):
        slotw[e, early + g * slots : early + (g + 1) * slots, :] = value

    def put_rows(g, e, cols, value):
        gbuf[e, early + g * slots : early + (g + 1) * slots, cols] = value

    def begin():
        fetch(0, 0, 0)
        for e in range(exp_dev):
            rows_copy(e).start()
        fetch(1, 0, 0)
        fetch(2, 0, 0)
        table_in.start()
        if exp_dev > 1:
            for kind in range(3):
                fetch(kind, 1, 1)
        slotw[:, :early, :] = slotw_ref[...]

    gather_groups(
        xs,
        first_ref[0],
        slots,
        xbuf,
        xsem,
        named_s,
        weight_s,
        pbuf,
        tbuf,
        put_weight,
        put_rows,
        begin,
    )
    table_back.start()

    @pl.loop(0, exp_dev)
    def _(e):
        slot = lax.rem(e, 2)
        rows_copy(e).wait()
        arrive(0, e, slot)
        arrive(1, e, slot)
        for start, size in tiles:
            gate = jnp.dot(
                gbuf[e], gate_b[slot, :, start : start + size], preferred_element_type=jnp.float32
            )
            upward = jnp.dot(
                gbuf[e], up_b[slot, :, start : start + size], preferred_element_type=jnp.float32
            )
            act[e, :, start : start + size] = (
                0.5 * gate * (1.0 + jnp.tanh(0.5 * gate)) * upward * slotw[e]
            ).astype(jnp.bfloat16)
        act_copy(e).start()

        @pl.when(e + 2 < exp_dev)
        def _():
            fetch(0, e + 2, slot)
            fetch(1, e + 2, slot)

        arrive(2, e, slot)

        @pl.loop(0, part // WIDE)
        def _(n):
            cols = pl.ds(pl.multiple_of(n * WIDE, WIDE), WIDE)
            gbuf[e, :, cols] = jnp.dot(
                act[e], down_b[slot, :, cols], preferred_element_type=jnp.float32
            ).astype(jnp.bfloat16)

        @pl.when(e + 2 < exp_dev)
        def _():
            fetch(2, e + 2, slot)

    table_back.wait()
    table_in.wait()
    scatter_groups(groups, slots, exp_dev, gbuf, tbuf, xbuf, outs, osem, cols_here)
    for e in range(exp_dev):
        act_copy(e).wait()


def scatter_groups(groups, slots, exp_dev, gbuf, tbuf, xbuf, outs, osem, cols_here):
    tok, part = outs[0].shape[1:]

    def out_copy(g, b):
        late = g < groups
        stacks = outs[:2] if late else outs[2:]
        index = (g if late else g - groups) * GROUP + b
        return pltpu.make_async_copy(
            xbuf.at[g % 2, pl.ds(b * tok, tok), pl.ds(0, part)],
            place_of(index, cols_here, stacks),
            osem.at[g % 2, b],
        )

    for g in range(2 * groups):
        if g >= 2:
            for b in range(GROUP):
                out_copy(g - 2, b).wait()
        here = (groups + g if g < groups else g - groups) * slots

        @pl.loop(0, part // WIDE)
        def _(n):
            cols = pl.ds(pl.multiple_of(n * WIDE, WIDE), WIDE)
            made = jnp.concatenate(
                [gbuf[e, here : here + slots, cols] for e in range(exp_dev)], axis=0
            )
            xbuf[g % 2, :, cols] = jnp.dot(
                tbuf[g], made, preferred_element_type=jnp.float32
            ).astype(jnp.bfloat16)

        for b in range(GROUP):
            out_copy(g, b).start()
    for g in range(2 * groups - 2, 2 * groups):
        for b in range(GROUP):
            out_copy(g, b).wait()


def rest_kernel(plan, act_ref, late_ref, early_ref, down_ref, *refs):
    groups, exp_dev, slots, cols_here = plan
    outs, refs = refs[:4], refs[4:]
    act, down_b, gbuf, tbuf, xbuf, asem, wsem, tsem, osem = refs
    part = outs[0].shape[2]

    def act_copy(e):
        return pltpu.make_async_copy(act_ref.at[e], act.at[e], asem.at[e])

    def down_copy(e):
        source = down_ref.at[e, :, pl.ds(part, part)]
        return pltpu.make_async_copy(source, down_b.at[e], wsem.at[e])

    tables = [
        pltpu.make_async_copy(late_ref, tbuf.at[pl.ds(0, groups)], tsem.at[0]),
        pltpu.make_async_copy(early_ref, tbuf.at[pl.ds(groups, groups)], tsem.at[1]),
    ]
    for e in range(exp_dev):
        act_copy(e).start()
        down_copy(e).start()
    for table in tables:
        table.start()

    @pl.loop(0, exp_dev)
    def _(e):
        act_copy(e).wait()
        down_copy(e).wait()

        @pl.loop(0, part // WIDE)
        def _(n):
            cols = pl.ds(pl.multiple_of(n * WIDE, WIDE), WIDE)
            gbuf[e, :, cols] = jnp.dot(
                act[e], down_b[e, :, cols], preferred_element_type=jnp.float32
            ).astype(jnp.bfloat16)

    for table in tables:
        table.wait()
    scatter_groups(groups, slots, exp_dev, gbuf, tbuf, xbuf, outs, osem, cols_here)


def sizes(blocks, capacity, exp_dev):
    slots = -(-GROUP * capacity // 16) * 16
    return len(blocks), 2 * blocks[0][0].shape[0], slots, len(blocks) // GROUP, exp_dev * GROUP


def scratch(tok, features, exp_dev, slots):
    return [
        pltpu.VMEM((2, GROUP * tok, features + tok), jnp.bfloat16),
        pltpu.VMEM((exp_dev * slots, GROUP * tok), jnp.bfloat16),
        pltpu.VMEM((exp_dev * GROUP, tok), jnp.float32),
    ]


def gathered(blocks, first, capacity, exp_dev):
    nb, tok, slots, groups, _ = sizes(blocks, capacity, exp_dev)
    features = blocks[0][1].shape[1]
    xbuf, pbuf, small = scratch(tok, features, exp_dev, slots)
    return pl.pallas_call(
        functools.partial(early_kernel, (nb, slots)),
        out_shape=[
            jax.ShapeDtypeStruct((exp_dev, groups * slots, features), jnp.bfloat16),
            jax.ShapeDtypeStruct((groups, GROUP * tok, exp_dev * slots), jnp.bfloat16),
            jax.ShapeDtypeStruct((exp_dev, groups * slots, 1), jnp.float32),
        ],
        in_specs=[pl.BlockSpec(memory_space=pltpu.SMEM)]
        + [pl.BlockSpec(memory_space=pl.ANY)] * (2 * nb),
        grid=(1,),
        out_specs=[
            pl.BlockSpec((exp_dev, groups * slots, features), lambda i: (0, 0, 0)),
            pl.BlockSpec((groups, GROUP * tok, exp_dev * slots), lambda i: (0, 0, 0)),
            pl.BlockSpec((exp_dev, groups * slots, 1), lambda i: (0, 0, 0)),
        ],
        scratch_shapes=[xbuf, pbuf, small, small, pltpu.SemaphoreType.DMA((2, 2 * GROUP))],
        compiler_params=pltpu.CompilerParams(vmem_limit_bytes=LIMIT // 2),
        cost_estimate=LIGHT,
        name="early",
    )(first, *[half for block in blocks for half in block])


def experts_of(ready, late, first, capacity, w_gate, w_up, w_down):
    rows, table, slotw = ready
    exp_dev, features, hidden = w_gate.shape
    nb, tok, slots, groups, pairs = sizes(late, capacity, exp_dev)
    cols = lax.axis_size("col")
    part = features // 2
    every = 2 * groups * slots
    tiles = [(start, min(NARROW, hidden - start)) for start in range(0, hidden, NARROW)]
    smem = pl.BlockSpec(memory_space=pltpu.SMEM)
    anywhere = pl.BlockSpec(memory_space=pl.ANY)
    xbuf, pbuf, small = scratch(tok, features, exp_dev, slots)
    tbuf = pltpu.VMEM((2 * groups,) + table.shape[1:], jnp.bfloat16)
    act = pltpu.VMEM((exp_dev, every, hidden), jnp.bfloat16)
    stacks = [jax.ShapeDtypeStruct((cols, tok, part), jnp.bfloat16)] * 4
    kept = jax.ShapeDtypeStruct((exp_dev, every, hidden), jnp.bfloat16)
    got = pl.pallas_call(
        functools.partial(expert_kernel, (nb, exp_dev, slots, tiles, cols)),
        grid=(1,),
        out_shape=stacks + [kept, jax.ShapeDtypeStruct(table.shape, jnp.bfloat16)],
        in_specs=[smem]
        + [anywhere] * (2 * nb + 2)
        + [pl.BlockSpec(slotw.shape, lambda i: (0, 0, 0))]
        + [anywhere] * 3,
        out_specs=[anywhere] * 6,
        scratch_shapes=[
            pltpu.VMEM((2, features, hidden), jnp.bfloat16),
            pltpu.VMEM((2, features, hidden), jnp.bfloat16),
            pltpu.VMEM((2, hidden, part), jnp.bfloat16),
            xbuf,
            pltpu.VMEM((exp_dev, every, features), jnp.bfloat16),
            pbuf,
            tbuf,
            act,
            pltpu.VMEM((exp_dev, every, 1), jnp.float32),
            small,
            small,
            pltpu.SemaphoreType.DMA((3, 2)),
            pltpu.SemaphoreType.DMA((2, 2 * GROUP)),
            pltpu.SemaphoreType.DMA((2, GROUP)),
            pltpu.SemaphoreType.DMA((exp_dev,)),
            pltpu.SemaphoreType.DMA((exp_dev,)),
            pltpu.SemaphoreType.DMA((2,)),
        ],
        compiler_params=pltpu.CompilerParams(vmem_limit_bytes=LIMIT),
        cost_estimate=pl.CostEstimate(
            flops=10 * exp_dev * every * features * hidden // 2,
            bytes_accessed=5 * exp_dev * features * hidden + 4 * nb * tok * features,
            transcendentals=0,
        ),
        name="experts",
    )(first, *[half for block in late for half in block], rows, table, slotw, w_gate, w_up, w_down)
    near, kept, late_table = list(got[:4]), got[4], got[5]

    def rest_of(gate):
        value = lax.optimization_barrier((kept, gate))[0]
        return pl.pallas_call(
            functools.partial(rest_kernel, (groups, exp_dev, slots, cols)),
            out_shape=stacks,
            in_specs=[anywhere] * 4,
            out_specs=[anywhere] * 4,
            scratch_shapes=[
                act,
                pltpu.VMEM((exp_dev, hidden, part), jnp.bfloat16),
                pltpu.VMEM((exp_dev, every, part), jnp.bfloat16),
                tbuf,
                pltpu.VMEM((2, GROUP * tok, part), jnp.bfloat16),
                pltpu.SemaphoreType.DMA((exp_dev,)),
                pltpu.SemaphoreType.DMA((exp_dev,)),
                pltpu.SemaphoreType.DMA((2,)),
                pltpu.SemaphoreType.DMA((2, GROUP)),
            ],
            compiler_params=pltpu.CompilerParams(vmem_limit_bytes=LIMIT),
            cost_estimate=pl.CostEstimate(
                flops=4 * exp_dev * every * (hidden + groups * GROUP * tok) * part,
                bytes_accessed=4 * exp_dev * hidden * (every + part),
                transcendentals=0,
            ),
            name="rest",
        )(value, late_table, table, w_down)

    return near, rest_of


def body(tokens, norm_gain, gate_weights, routes, moves, w_gate, w_up, w_down):
    tok_rows, features = tokens.shape
    per_token = routes.shape[1]
    exp_dev = w_gate.shape[0]
    group = lax.axis_size("row") * lax.axis_size("col")
    experts = group * exp_dev
    capacity = tok_rows * per_token * 3 // (2 * experts)
    half = tok_rows // 2
    halves = pl.pallas_call(
        head_kernel,
        out_shape=[
            jax.ShapeDtypeStruct((half, features + tok_rows), jnp.bfloat16),
            jax.ShapeDtypeStruct((half, features), jnp.bfloat16),
        ],
        name="head",
    )(tokens, norm_gain.reshape(1, features), gate_weights.T, routes.T)
    first = (lax.axis_index(("row", "col")) * exp_dev).astype(jnp.int32).reshape(1)
    ready, late = spread(
        list(halves), lambda blocks: gathered(blocks, first, capacity, exp_dev)
    )
    stacks, rest_of = experts_of(ready, late, first, capacity, w_gate, w_up, w_down)
    part = features // 2
    rows = jnp.arange(tok_rows, dtype=jnp.int32)
    second = lax.axis_index("rep") == 1
    pick = (moves[0, 0][:, None] == rows[None, :]).astype(jnp.bfloat16)
    target = jnp.where(second, moves[0, 1], moves[0, 0])
    match = rows[:, None] == target[None, :]
    taken = jnp.any(match, axis=1, keepdims=True)
    match = match.astype(jnp.bfloat16)

    def served(pieces, start):
        total = added(tokens[:, start : start + part], *pieces)
        leaving = jnp.dot(pick, total, preferred_element_type=jnp.float32).astype(jnp.bfloat16)
        incoming = shifted(leaving, "rep", 1)
        placed = jnp.dot(match, incoming, preferred_element_type=jnp.float32)
        placed = jnp.where(second, placed, 0.0).astype(jnp.bfloat16)
        return jnp.where(taken, placed, total)

    pieces, gate, arrived = collected(*stacks)
    left = served(pieces, 0)
    pieces, _, _ = collected(*rest_of(gate), held=arrived)
    return jnp.concatenate([left, served(pieces, part)], axis=1)


def solution(mesh):
    return jax.shard_map(
        body,
        mesh=mesh,
        in_specs=(
            P(("rep", "row", "col"), None),
            P(),
            P(("rep", "row", "col"), None),
            P(("rep", "row", "col"), None),
            P(("row", "col"), None, None),
            P(("row", "col"), None, None),
            P(("row", "col"), None, None),
            P(("row", "col"), None, None),
        ),
        out_specs=P(("rep", "row", "col"), None),
        check_vma=False,
    )
```

```python
import functools

import jax
import jax.numpy as jnp
from jax import lax
from jax.experimental import pallas as pl
from jax.experimental.pallas import tpu as pltpu
from jax.sharding import PartitionSpec as P

GROUP = 8
PIECES = 4
LANE = 8
WIDE = 512
NARROW = 256
LIMIT = 60 * 1024 * 1024
LIGHT = pl.CostEstimate(flops=1, bytes_accessed=1, transcendentals=0)


def shifted(value, axis, steps):
    count = lax.axis_size(axis)
    first, last = (max(0, -steps), min(count, count - steps))
    return lax.ppermute(value, axis, [(source, source + steps) for source in range(first, last)])


def turned(value, steps):
    count = lax.axis_size("col")
    return lax.ppermute(value, "col", [(source, (source + steps) % count) for source in range(count)])


def swapped(value, bit):
    count = lax.axis_size("row")
    return lax.ppermute(value, "row", [(source, source ^ bit) for source in range(count)])


def spread(halves, gather):
    line, other, last = [halves], [], halves
    for _ in range(1, lax.axis_size("col")):
        pairs = [lax.optimization_barrier((turned(one, 1), swapped(one, 2))) for one in last]
        last = [ahead for ahead, _ in pairs]
        line.append(last)
        other.append([across for _, across in pairs])
    ready = gather(line + [[swapped(one, 1) for one in block] for block in line])
    final = [swapped(one, 2) for one in last]
    held = lax.optimization_barrier((*final, ready[2]))[: len(final)]
    far = [[swapped(one, 1) for one in block] for block in other + [list(held)]]
    return ready, other + [final] + far


def added(*parts):
    return sum(part.astype(jnp.float32) for part in parts).astype(jnp.bfloat16)


def collected(near_late, far_late, near_early, far_early):
    cols = lax.axis_size("col")
    order = list(range(cols // 2, 0, -1)) + list(range(cols // 2 + 1, cols)) + [0]
    held = swapped(far_late, 1)
    sent = {step: swapped(added(near_late[step], held[step]), 2) for step in order}
    far = swapped(lax.optimization_barrier((far_early, held))[0], 1)
    line = [[near_early[step], far[step], sent[step]] for step in range(cols)]
    down, up = [], []
    for step in range(cols // 2, 0, -1):
        down = [turned(added(*(line[step] + down)), -1)]
        if step == cols // 2:
            ahead = down[0]
    for step in range(cols // 2 + 1, cols):
        value = added(*(line[step] + up))
        if not up:
            value = lax.optimization_barrier((value, ahead))[0]
        up = [turned(value, 1)]
    return line[0] + up + down


def head_kernel(tokens_ref, gain_ref, weights_ref, routes_ref, *outs):
    features, per_token = tokens_ref.shape[1], routes_ref.shape[0]
    widened = tokens_ref[...].astype(jnp.float32)
    scale = lax.rsqrt(jnp.mean(widened * widened, axis=-1, keepdims=True) + 1e-06)
    normed = (widened * scale * gain_ref[...]).astype(jnp.bfloat16)
    half = outs[0].shape[0]
    for i, out_ref in enumerate(outs):
        out_ref[:, :features] = normed[i * half : (i + 1) * half]
    weights = weights_ref[...]
    high = weights.astype(jnp.bfloat16).astype(jnp.float32)
    middle = (weights - high).astype(jnp.bfloat16).astype(jnp.float32)
    low = weights - high - middle
    gap = jnp.zeros((LANE - per_token, weights.shape[1]), jnp.float32)
    meta = [routes_ref[...].astype(jnp.float32), gap - 1.0, high, gap, middle, gap, low, gap]
    outs[0][: 4 * LANE, features:] = jnp.concatenate(meta, axis=0).astype(jnp.bfloat16)
    outs[0][4 * LANE :, features:] = jnp.zeros(
        (half - 4 * LANE, weights.shape[1]), jnp.bfloat16
    )


def gather_groups(xs, first, slots, xbuf, xsem, named_s, weight_s, pbuf, tbuf, put_weight, put_rows, begin=None):
    groups = len(xs) // (2 * GROUP)
    half = xs[0].shape[0]
    tok = 2 * half
    features = xs[1].shape[1]
    pairs = named_s.shape[0]
    exp_dev = pairs // GROUP

    def copies(g):
        for b in range(GROUP):
            for h in range(2):
                source = xs[2 * (g * GROUP + b) + h]
                target = xbuf.at[
                    g % 2, pl.ds(b * tok + h * half, half), pl.ds(0, source.shape[1])
                ]
                yield pltpu.make_async_copy(source, target, xsem.at[g % 2, 2 * b + h])

    def load(g):
        for copy in copies(g):
            copy.start()

    for g in range(min(2, groups)):
        load(g)
    if begin is not None:
        begin()
    lane = lax.broadcasted_iota(jnp.int32, (tok, tok), 1)
    sub = lax.broadcasted_iota(jnp.int32, (tok, tok), 0)
    upto = (sub <= lane).astype(jnp.bfloat16)
    pair_r = lax.broadcasted_iota(jnp.int32, (pairs, pairs), 0)
    pair_c = lax.broadcasted_iota(jnp.int32, (pairs, pairs), 1)
    before = ((pair_r // GROUP == pair_c // GROUP) & (pair_c < pair_r)).astype(jnp.bfloat16)
    slot_id = lax.broadcasted_iota(jnp.int32, (slots, tok), 0).astype(jnp.float32)
    wide_id = lax.broadcasted_iota(jnp.int32, (tok, exp_dev * slots), 1).astype(jnp.float32)
    offset = lax.broadcasted_iota(jnp.int32, (pairs, tok), 0) // GROUP * slots
    offset = offset.astype(jnp.float32)

    for g in range(groups):
        for copy in copies(g):
            copy.wait()
        for b in range(GROUP):
            meta = xbuf[g % 2, b * tok : b * tok + 4 * LANE, features:].astype(jnp.float32)
            chosen = meta[:LANE]
            given = meta[LANE : 2 * LANE] + meta[2 * LANE : 3 * LANE] + meta[3 * LANE : 4 * LANE]
            for e in range(exp_dev):
                hit = chosen == (first + e).astype(jnp.float32)
                named_s[e * GROUP + b : e * GROUP + b + 1, :] = jnp.sum(
                    hit.astype(jnp.float32), axis=0, keepdims=True
                )
                weight_s[e * GROUP + b : e * GROUP + b + 1, :] = jnp.sum(
                    jnp.where(hit, given, 0.0), axis=0, keepdims=True
                )
        named = named_s[...]
        count = jnp.dot(named.astype(jnp.bfloat16), upto, preferred_element_type=jnp.float32)
        totals = jnp.broadcast_to(count[:, tok - 1 :], (pairs, tok)).astype(jnp.bfloat16)
        base = jnp.dot(before, totals, preferred_element_type=jnp.float32)
        named_s[...] = jnp.where(named > 0.5, base + count - 1.0, -1.0)
        for e in range(exp_dev):
            total = jnp.zeros((slots, tok), jnp.float32)
            for b in range(GROUP):
                pick = slot_id == named_s[e * GROUP + b : e * GROUP + b + 1, :]
                pbuf[e * slots : (e + 1) * slots, b * tok : (b + 1) * tok] = pick.astype(
                    jnp.float32
                ).astype(jnp.bfloat16)
                total += jnp.where(pick, weight_s[e * GROUP + b : e * GROUP + b + 1, :], 0.0)
            put_weight(g, e, jnp.sum(total, axis=1, keepdims=True))
        place = named_s[...]
        place = jnp.where(place < -0.5, place, place + offset)
        place = jnp.concatenate([place, jnp.zeros((tok - pairs, tok), jnp.float32)], axis=0).T
        for b in range(GROUP):
            pick = wide_id == place[:, b : b + 1]
            for e in range(1, exp_dev):
                pick = pick | (wide_id == place[:, e * GROUP + b : e * GROUP + b + 1])
            tbuf[g, b * tok : (b + 1) * tok, :] = pick.astype(jnp.float32).astype(jnp.bfloat16)

        @pl.loop(0, features // WIDE)
        def _(n):
            cols = pl.ds(pl.multiple_of(n * WIDE, WIDE), WIDE)
            got = jnp.dot(pbuf[...], xbuf[g % 2, :, cols], preferred_element_type=jnp.float32)
            got = got.astype(jnp.bfloat16)
            for e in range(exp_dev):
                put_rows(g, e, cols, got[e * slots : (e + 1) * slots])

        if g + 2 < groups:
            load(g + 2)


def early_kernel(plan, first_ref, *refs):
    nb, slots = plan
    xs, refs = refs[: 2 * nb], refs[2 * nb :]
    rows_ref, tbuf, slotw, xbuf, pbuf, named_s, weight_s, xsem = refs

    def put_weight(g, e, value):
        slotw[e, g * slots : (g + 1) * slots, :] = value

    def put_rows(g, e, cols, value):
        rows_ref[e, g * slots : (g + 1) * slots, cols] = value

    gather_groups(
        xs, first_ref[0], slots, xbuf, xsem, named_s, weight_s, pbuf, tbuf, put_weight, put_rows
    )


def expert_kernel(plan, first_ref, *refs):
    nb, exp_dev, slots, tiles, cols_here = plan
    xs, refs = refs[: 2 * nb], refs[2 * nb :]
    rows_ref, table_ref, slotw_ref, gate_ref, up_ref, down_ref = refs[:6]
    outs, refs = refs[6:14], refs[14:]
    gate_b, up_b, down_b, xbuf, gbuf, pbuf, tbuf, act, slotw = refs[:9]
    named_s, weight_s, wsem, xsem, osem, rsem, tsem = refs[9:]
    groups = nb // GROUP
    features = down_ref.shape[2]
    early = groups * slots

    def weight_refs(kind, e, slot):
        source = (gate_ref, up_ref, down_ref)[kind]
        target = (gate_b, up_b, down_b)[kind]
        return source.at[e], target.at[slot], wsem.at[kind, slot]

    def fetch(kind, e, slot):
        source, target, sem = weight_refs(kind, e, slot)
        size = target.shape[0] // PIECES
        for piece in range(PIECES):
            rows = pl.ds(piece * size, size)
            pltpu.make_async_copy(source.at[rows, :], target.at[rows, :], sem).start()

    def arrive(kind, e, slot):
        pltpu.make_async_copy(*weight_refs(kind, e, slot)).wait()

    def rows_copy(e):
        return pltpu.make_async_copy(rows_ref.at[e], gbuf.at[e, pl.ds(0, early), :], rsem.at[e])

    table_in = pltpu.make_async_copy(table_ref, tbuf.at[pl.ds(groups, groups)], tsem)

    def put_weight(g, e, value):
        slotw[e, early + g * slots : early + (g + 1) * slots, :] = value

    def put_rows(g, e, cols, value):
        gbuf[e, early + g * slots : early + (g + 1) * slots, cols] = value

    def begin():
        fetch(0, 0, 0)
        for e in range(exp_dev):
            rows_copy(e).start()
        fetch(1, 0, 0)
        fetch(2, 0, 0)
        table_in.start()
        if exp_dev > 1:
            for kind in range(3):
                fetch(kind, 1, 1)
        slotw[:, :early, :] = slotw_ref[...]

    gather_groups(
        xs,
        first_ref[0],
        slots,
        xbuf,
        xsem,
        named_s,
        weight_s,
        pbuf,
        tbuf,
        put_weight,
        put_rows,
        begin,
    )

    @pl.loop(0, exp_dev)
    def _(e):
        slot = lax.rem(e, 2)
        rows_copy(e).wait()
        arrive(0, e, slot)
        arrive(1, e, slot)
        for start, size in tiles:
            gate = jnp.dot(
                gbuf[e], gate_b[slot, :, start : start + size], preferred_element_type=jnp.float32
            )
            upward = jnp.dot(
                gbuf[e], up_b[slot, :, start : start + size], preferred_element_type=jnp.float32
            )
            act[:, start : start + size] = (
                0.5 * gate * (1.0 + jnp.tanh(0.5 * gate)) * upward * slotw[e]
            ).astype(jnp.bfloat16)

        @pl.when(e + 2 < exp_dev)
        def _():
            fetch(0, e + 2, slot)
            fetch(1, e + 2, slot)

        arrive(2, e, slot)

        @pl.loop(0, features // WIDE)
        def _(n):
            cols = pl.ds(pl.multiple_of(n * WIDE, WIDE), WIDE)
            gbuf[e, :, cols] = jnp.dot(
                act[...], down_b[slot, :, cols], preferred_element_type=jnp.float32
            ).astype(jnp.bfloat16)

        @pl.when(e + 2 < exp_dev)
        def _():
            fetch(2, e + 2, slot)

    table_in.wait()
    scatter_groups(groups, slots, exp_dev, gbuf, tbuf, xbuf, outs, osem, cols_here)


def scatter_groups(groups, slots, exp_dev, gbuf, tbuf, xbuf, outs, osem, cols_here):
    tok, part = outs[0].shape[1:]

    def out_copies(g):
        first = 0 if g < groups else 2
        for half in range(2):
            stacks = outs[4 * half + first : 4 * half + first + 2]
            for b in range(GROUP):
                index = g % groups * GROUP + b
                yield pltpu.make_async_copy(
                    xbuf.at[g % 2, pl.ds(b * tok, tok), pl.ds(half * part, part)],
                    stacks[index // cols_here].at[index % cols_here],
                    osem.at[g % 2, GROUP * half + b],
                )

    for g in range(2 * groups):
        if g >= 2:
            for copy in out_copies(g - 2):
                copy.wait()
        here = (groups + g if g < groups else g - groups) * slots

        @pl.loop(0, 2 * part // WIDE)
        def _(n):
            cols = pl.ds(pl.multiple_of(n * WIDE, WIDE), WIDE)
            made = jnp.concatenate(
                [gbuf[e, here : here + slots, cols] for e in range(exp_dev)], axis=0
            )
            xbuf[g % 2, :, cols] = jnp.dot(
                tbuf[g], made, preferred_element_type=jnp.float32
            ).astype(jnp.bfloat16)

        for copy in out_copies(g):
            copy.start()
    for g in range(2 * groups - 2, 2 * groups):
        for copy in out_copies(g):
            copy.wait()


def sizes(blocks, capacity, exp_dev):
    slots = -(-GROUP * capacity // 16) * 16
    return len(blocks), 2 * blocks[0][0].shape[0], slots, len(blocks) // GROUP, exp_dev * GROUP


def scratch(tok, features, exp_dev, slots):
    return [
        pltpu.VMEM((2, GROUP * tok, features + tok), jnp.bfloat16),
        pltpu.VMEM((exp_dev * slots, GROUP * tok), jnp.bfloat16),
        pltpu.VMEM((exp_dev * GROUP, tok), jnp.float32),
    ]


def gathered(blocks, first, capacity, exp_dev):
    nb, tok, slots, groups, _ = sizes(blocks, capacity, exp_dev)
    features = blocks[0][1].shape[1]
    xbuf, pbuf, small = scratch(tok, features, exp_dev, slots)
    return pl.pallas_call(
        functools.partial(early_kernel, (nb, slots)),
        out_shape=[
            jax.ShapeDtypeStruct((exp_dev, groups * slots, features), jnp.bfloat16),
            jax.ShapeDtypeStruct((groups, GROUP * tok, exp_dev * slots), jnp.bfloat16),
            jax.ShapeDtypeStruct((exp_dev, groups * slots, 1), jnp.float32),
        ],
        in_specs=[pl.BlockSpec(memory_space=pltpu.SMEM)]
        + [pl.BlockSpec(memory_space=pl.ANY)] * (2 * nb),
        grid=(1,),
        out_specs=[
            pl.BlockSpec((exp_dev, groups * slots, features), lambda i: (0, 0, 0)),
            pl.BlockSpec((groups, GROUP * tok, exp_dev * slots), lambda i: (0, 0, 0)),
            pl.BlockSpec((exp_dev, groups * slots, 1), lambda i: (0, 0, 0)),
        ],
        scratch_shapes=[xbuf, pbuf, small, small, pltpu.SemaphoreType.DMA((2, 2 * GROUP))],
        compiler_params=pltpu.CompilerParams(vmem_limit_bytes=LIMIT),
        cost_estimate=LIGHT,
        name="early",
    )(first, *[half for block in blocks for half in block])


def experts_of(ready, late, first, capacity, w_gate, w_up, w_down):
    rows, table, slotw = ready
    exp_dev, features, hidden = w_gate.shape
    nb, tok, slots, groups, pairs = sizes(late, capacity, exp_dev)
    cols = lax.axis_size("col")
    part = features // 2
    every = 2 * groups * slots
    tiles = [(start, min(NARROW, hidden - start)) for start in range(0, hidden, NARROW)]
    smem = pl.BlockSpec(memory_space=pltpu.SMEM)
    anywhere = pl.BlockSpec(memory_space=pl.ANY)
    xbuf, pbuf, small = scratch(tok, features, exp_dev, slots)
    tbuf = pltpu.VMEM((2 * groups,) + table.shape[1:], jnp.bfloat16)
    act = pltpu.VMEM((every, hidden), jnp.bfloat16)
    stacks = [jax.ShapeDtypeStruct((cols, tok, part), jnp.bfloat16)] * 8
    got = pl.pallas_call(
        functools.partial(expert_kernel, (nb, exp_dev, slots, tiles, cols)),
        grid=(1,),
        out_shape=stacks,
        in_specs=[smem]
        + [anywhere] * (2 * nb + 2)
        + [pl.BlockSpec(slotw.shape, lambda i: (0, 0, 0))]
        + [anywhere] * 3,
        out_specs=[anywhere] * 8,
        scratch_shapes=[
            pltpu.VMEM((2, features, hidden), jnp.bfloat16),
            pltpu.VMEM((2, features, hidden), jnp.bfloat16),
            pltpu.VMEM((2, hidden, features), jnp.bfloat16),
            xbuf,
            pltpu.VMEM((exp_dev, every, features), jnp.bfloat16),
            pbuf,
            tbuf,
            act,
            pltpu.VMEM((exp_dev, every, 1), jnp.float32),
            small,
            small,
            pltpu.SemaphoreType.DMA((3, 2)),
            pltpu.SemaphoreType.DMA((2, 2 * GROUP)),
            pltpu.SemaphoreType.DMA((2, 2 * GROUP)),
            pltpu.SemaphoreType.DMA((exp_dev,)),
            pltpu.SemaphoreType.DMA,
        ],
        compiler_params=pltpu.CompilerParams(vmem_limit_bytes=LIMIT),
        cost_estimate=pl.CostEstimate(
            flops=6 * exp_dev * every * features * hidden,
            bytes_accessed=6 * exp_dev * features * hidden + 4 * nb * tok * features,
            transcendentals=0,
        ),
        name="experts",
    )(first, *[half for block in late for half in block], rows, table, slotw, w_gate, w_up, w_down)
    return list(got)


def body(tokens, norm_gain, gate_weights, routes, moves, w_gate, w_up, w_down):
    tok_rows, features = tokens.shape
    per_token = routes.shape[1]
    exp_dev = w_gate.shape[0]
    group = lax.axis_size("row") * lax.axis_size("col")
    experts = group * exp_dev
    capacity = tok_rows * per_token * 3 // (2 * experts)
    half = tok_rows // 2
    halves = pl.pallas_call(
        head_kernel,
        out_shape=[
            jax.ShapeDtypeStruct((half, features + tok_rows), jnp.bfloat16),
            jax.ShapeDtypeStruct((half, features), jnp.bfloat16),
        ],
        name="head",
    )(tokens, norm_gain.reshape(1, features), gate_weights.T, routes.T)
    first = (lax.axis_index(("row", "col")) * exp_dev).astype(jnp.int32).reshape(1)
    ready, late = spread(
        list(halves), lambda blocks: gathered(blocks, first, capacity, exp_dev)
    )
    stacks = experts_of(ready, late, first, capacity, w_gate, w_up, w_down)
    part = features // 2
    rows = jnp.arange(tok_rows, dtype=jnp.int32)
    second = lax.axis_index("rep") == 1
    pick = (moves[0, 0][:, None] == rows[None, :]).astype(jnp.bfloat16)
    target = jnp.where(second, moves[0, 1], moves[0, 0])
    match = rows[:, None] == target[None, :]
    taken = jnp.any(match, axis=1, keepdims=True)
    match = match.astype(jnp.bfloat16)

    def served(pieces, start):
        total = added(tokens[:, start : start + part], *pieces)
        leaving = jnp.dot(pick, total, preferred_element_type=jnp.float32).astype(jnp.bfloat16)
        incoming = shifted(leaving, "rep", 1)
        placed = jnp.dot(match, incoming, preferred_element_type=jnp.float32)
        placed = jnp.where(second, placed, 0.0).astype(jnp.bfloat16)
        return jnp.where(taken, placed, total)

    left, right = [
        served(collected(*stacks[i : i + 4]), i // 4 * part) for i in range(0, 8, 4)
    ]
    return jnp.concatenate([left, right], axis=1)


def solution(mesh):
    return jax.shard_map(
        body,
        mesh=mesh,
        in_specs=(
            P(("rep", "row", "col"), None),
            P(),
            P(("rep", "row", "col"), None),
            P(("rep", "row", "col"), None),
            P(("row", "col"), None, None),
            P(("row", "col"), None, None),
            P(("row", "col"), None, None),
            P(("row", "col"), None, None),
        ),
        out_specs=P(("rep", "row", "col"), None),
        check_vma=False,
    )
```

```python
import functools

import jax
import jax.numpy as jnp
from jax import lax
from jax.experimental import pallas as pl
from jax.experimental.pallas import tpu as pltpu
from jax.sharding import PartitionSpec as P

GROUP = 8
PIECES = 4
LANE = 8
WIDE = 512
NARROW = 512
LIMIT = 60 * 1024 * 1024
LIGHT = pl.CostEstimate(flops=1, bytes_accessed=1, transcendentals=0)


def shifted(value, axis, steps):
    count = lax.axis_size(axis)
    first, last = (max(0, -steps), min(count, count - steps))
    return lax.ppermute(value, axis, [(source, source + steps) for source in range(first, last)])


def turned(value, steps):
    count = lax.axis_size("col")
    return lax.ppermute(value, "col", [(source, (source + steps) % count) for source in range(count)])


def swapped(value, bit):
    count = lax.axis_size("row")
    return lax.ppermute(value, "row", [(source, source ^ bit) for source in range(count)])


def spread(halves, gather):
    line, other, last = [halves], [], halves
    for _ in range(1, lax.axis_size("col")):
        pairs = [lax.optimization_barrier((turned(one, 1), swapped(one, 2))) for one in last]
        last = [ahead for ahead, _ in pairs]
        line.append(last)
        other.append([across for _, across in pairs])
    ready = gather(line + [[swapped(one, 1) for one in block] for block in line])
    final = [swapped(one, 2) for one in last]
    held = lax.optimization_barrier((*final, ready[2]))[: len(final)]
    far = [[swapped(one, 1) for one in block] for block in other + [list(held)]]
    return ready, other + [final] + far


def added(*parts):
    return sum(part.astype(jnp.float32) for part in parts).astype(jnp.bfloat16)


def collected(late, early):
    cols = lax.axis_size("col")
    order = list(range(cols // 2, 0, -1)) + list(range(cols // 2 + 1, cols)) + [0]
    held = {step: swapped(late[cols + step], 1) for step in order}
    sent = {step: swapped(added(late[step], held[step]), 2) for step in order}
    far = {
        step: swapped(lax.optimization_barrier((early[cols + step], held[step]))[0], 1)
        for step in order
    }
    line = [[early[step], far[step], sent[step]] for step in range(cols)]
    down, up = [], []
    for step in range(cols // 2, 0, -1):
        down = [turned(added(*(line[step] + down)), -1)]
        if step == cols // 2:
            ahead = down[0]
    for step in range(cols // 2 + 1, cols):
        value = added(*(line[step] + up))
        if not up:
            value = lax.optimization_barrier((value, ahead))[0]
        up = [turned(value, 1)]
    return line[0] + up + down


def head_kernel(tokens_ref, gain_ref, weights_ref, routes_ref, *outs):
    features, per_token = tokens_ref.shape[1], routes_ref.shape[0]
    widened = tokens_ref[...].astype(jnp.float32)
    scale = lax.rsqrt(jnp.mean(widened * widened, axis=-1, keepdims=True) + 1e-06)
    normed = (widened * scale * gain_ref[...]).astype(jnp.bfloat16)
    half = outs[0].shape[0]
    for i, out_ref in enumerate(outs):
        out_ref[:, :features] = normed[i * half : (i + 1) * half]
    weights = weights_ref[...]
    high = weights.astype(jnp.bfloat16).astype(jnp.float32)
    middle = (weights - high).astype(jnp.bfloat16).astype(jnp.float32)
    low = weights - high - middle
    gap = jnp.zeros((LANE - per_token, weights.shape[1]), jnp.float32)
    meta = [routes_ref[...].astype(jnp.float32), gap - 1.0, high, gap, middle, gap, low, gap]
    outs[0][: 4 * LANE, features:] = jnp.concatenate(meta, axis=0).astype(jnp.bfloat16)
    outs[0][4 * LANE :, features:] = jnp.zeros(
        (half - 4 * LANE, weights.shape[1]), jnp.bfloat16
    )


def gather_groups(xs, first, slots, xbuf, xsem, named_s, weight_s, pbuf, tbuf, put_weight, put_rows, begin=None):
    groups = len(xs) // (2 * GROUP)
    half = xs[0].shape[0]
    tok = 2 * half
    features = xs[1].shape[1]
    pairs = named_s.shape[0]
    exp_dev = pairs // GROUP

    def copies(g):
        for b in range(GROUP):
            for h in range(2):
                source = xs[2 * (g * GROUP + b) + h]
                target = xbuf.at[
                    g % 2, pl.ds(b * tok + h * half, half), pl.ds(0, source.shape[1])
                ]
                yield pltpu.make_async_copy(source, target, xsem.at[g % 2, 2 * b + h])

    def load(g):
        for copy in copies(g):
            copy.start()

    for g in range(min(2, groups)):
        load(g)
    if begin is not None:
        begin()
    lane = lax.broadcasted_iota(jnp.int32, (tok, tok), 1)
    sub = lax.broadcasted_iota(jnp.int32, (tok, tok), 0)
    upto = (sub <= lane).astype(jnp.bfloat16)
    pair_r = lax.broadcasted_iota(jnp.int32, (pairs, pairs), 0)
    pair_c = lax.broadcasted_iota(jnp.int32, (pairs, pairs), 1)
    before = ((pair_r // GROUP == pair_c // GROUP) & (pair_c < pair_r)).astype(jnp.bfloat16)
    slot_id = lax.broadcasted_iota(jnp.int32, (slots, tok), 0).astype(jnp.float32)
    wide_id = lax.broadcasted_iota(jnp.int32, (tok, exp_dev * slots), 1).astype(jnp.float32)
    offset = lax.broadcasted_iota(jnp.int32, (pairs, tok), 0) // GROUP * slots
    offset = offset.astype(jnp.float32)

    for g in range(groups):
        for copy in copies(g):
            copy.wait()
        for b in range(GROUP):
            meta = xbuf[g % 2, b * tok : b * tok + 4 * LANE, features:].astype(jnp.float32)
            chosen = meta[:LANE]
            given = meta[LANE : 2 * LANE] + meta[2 * LANE : 3 * LANE] + meta[3 * LANE : 4 * LANE]
            for e in range(exp_dev):
                hit = chosen == (first + e).astype(jnp.float32)
                named_s[e * GROUP + b : e * GROUP + b + 1, :] = jnp.sum(
                    hit.astype(jnp.float32), axis=0, keepdims=True
                )
                weight_s[e * GROUP + b : e * GROUP + b + 1, :] = jnp.sum(
                    jnp.where(hit, given, 0.0), axis=0, keepdims=True
                )
        named = named_s[...]
        count = jnp.dot(named.astype(jnp.bfloat16), upto, preferred_element_type=jnp.float32)
        totals = jnp.broadcast_to(count[:, tok - 1 :], (pairs, tok)).astype(jnp.bfloat16)
        base = jnp.dot(before, totals, preferred_element_type=jnp.float32)
        named_s[...] = jnp.where(named > 0.5, base + count - 1.0, -1.0)
        for e in range(exp_dev):
            total = jnp.zeros((slots, tok), jnp.float32)
            for b in range(GROUP):
                pick = slot_id == named_s[e * GROUP + b : e * GROUP + b + 1, :]
                pbuf[e * slots : (e + 1) * slots, b * tok : (b + 1) * tok] = pick.astype(
                    jnp.float32
                ).astype(jnp.bfloat16)
                total += jnp.where(pick, weight_s[e * GROUP + b : e * GROUP + b + 1, :], 0.0)
            put_weight(g, e, jnp.sum(total, axis=1, keepdims=True))
        place = named_s[...]
        place = jnp.where(place < -0.5, place, place + offset)
        place = jnp.concatenate([place, jnp.zeros((tok - pairs, tok), jnp.float32)], axis=0).T
        for b in range(GROUP):
            pick = wide_id == place[:, b : b + 1]
            for e in range(1, exp_dev):
                pick = pick | (wide_id == place[:, e * GROUP + b : e * GROUP + b + 1])
            tbuf[g, b * tok : (b + 1) * tok, :] = pick.astype(jnp.float32).astype(jnp.bfloat16)

        @pl.loop(0, features // WIDE)
        def _(n):
            cols = pl.ds(pl.multiple_of(n * WIDE, WIDE), WIDE)
            got = jnp.dot(pbuf[...], xbuf[g % 2, :, cols], preferred_element_type=jnp.float32)
            got = got.astype(jnp.bfloat16)
            for e in range(exp_dev):
                put_rows(g, e, cols, got[e * slots : (e + 1) * slots])

        if g + 2 < groups:
            load(g + 2)


def early_kernel(plan, first_ref, *refs):
    nb, slots = plan
    xs, refs = refs[: 2 * nb], refs[2 * nb :]
    rows_ref, tbuf, slotw, xbuf, pbuf, named_s, weight_s, xsem = refs

    def put_weight(g, e, value):
        slotw[e, g * slots : (g + 1) * slots, :] = value

    def put_rows(g, e, cols, value):
        rows_ref[e, g * slots : (g + 1) * slots, cols] = value

    gather_groups(
        xs, first_ref[0], slots, xbuf, xsem, named_s, weight_s, pbuf, tbuf, put_weight, put_rows
    )


def expert_kernel(plan, first_ref, *refs):
    nb, exp_dev, slots, tiles = plan
    xs, refs = refs[: 2 * nb], refs[2 * nb :]
    rows_ref, table_ref, slotw_ref, gate_ref, up_ref, down_ref = refs[:6]
    outs, refs = refs[6 : 6 + 2 * nb], refs[6 + 2 * nb :]
    gate_b, up_b, down_b, xbuf, gbuf, pbuf, tbuf, act, slotw = refs[:9]
    named_s, weight_s, wsem, xsem, osem, rsem, tsem = refs[9:]
    groups = nb // GROUP
    features = down_ref.shape[2]
    early = groups * slots

    def weight_refs(kind, e, slot):
        source = (gate_ref, up_ref, down_ref)[kind]
        target = (gate_b, up_b, down_b)[kind]
        return source.at[e], target.at[slot], wsem.at[kind, slot]

    def fetch(kind, e, slot):
        source, target, sem = weight_refs(kind, e, slot)
        size = target.shape[0] // PIECES
        for piece in range(PIECES):
            rows = pl.ds(piece * size, size)
            pltpu.make_async_copy(source.at[rows, :], target.at[rows, :], sem).start()

    def arrive(kind, e, slot):
        pltpu.make_async_copy(*weight_refs(kind, e, slot)).wait()

    def rows_copy(e):
        return pltpu.make_async_copy(rows_ref.at[e], gbuf.at[e, pl.ds(0, early), :], rsem.at[e])

    table_in = pltpu.make_async_copy(table_ref, tbuf.at[pl.ds(groups, groups)], tsem)

    def put_weight(g, e, value):
        slotw[e, early + g * slots : early + (g + 1) * slots, :] = value

    def put_rows(g, e, cols, value):
        gbuf[e, early + g * slots : early + (g + 1) * slots, cols] = value

    def begin():
        fetch(0, 0, 0)
        for e in range(exp_dev):
            rows_copy(e).start()
        fetch(1, 0, 0)
        fetch(2, 0, 0)
        table_in.start()
        if exp_dev > 1:
            for kind in range(3):
                fetch(kind, 1, 1)
        slotw[:, :early, :] = slotw_ref[...]

    gather_groups(
        xs,
        first_ref[0],
        slots,
        xbuf,
        xsem,
        named_s,
        weight_s,
        pbuf,
        tbuf,
        put_weight,
        put_rows,
        begin,
    )

    @pl.loop(0, exp_dev)
    def _(e):
        slot = lax.rem(e, gate_b.shape[0])
        rows_copy(e).wait()
        arrive(0, e, slot)
        arrive(1, e, slot)
        for start, size in tiles:
            gate = jnp.dot(
                gbuf[e], gate_b[slot, :, start : start + size], preferred_element_type=jnp.float32
            )
            upward = jnp.dot(
                gbuf[e], up_b[slot, :, start : start + size], preferred_element_type=jnp.float32
            )
            act[:, start : start + size] = (
                0.5 * gate * (1.0 + jnp.tanh(0.5 * gate)) * upward * slotw[e]
            ).astype(jnp.bfloat16)

        @pl.when(e + 2 < exp_dev)
        def _():
            fetch(0, e + 2, slot)
            fetch(1, e + 2, slot)

        arrive(2, e, slot)

        @pl.loop(0, features // WIDE)
        def _(n):
            cols = pl.ds(pl.multiple_of(n * WIDE, WIDE), WIDE)
            gbuf[e, :, cols] = jnp.dot(
                act[...], down_b[slot, :, cols], preferred_element_type=jnp.float32
            ).astype(jnp.bfloat16)

        @pl.when(e + 2 < exp_dev)
        def _():
            fetch(2, e + 2, slot)

    table_in.wait()
    scatter_groups(groups, slots, exp_dev, gbuf, tbuf, xbuf, outs, osem)


def scatter_groups(groups, slots, exp_dev, gbuf, tbuf, xbuf, outs, osem):
    tok, features = outs[0].shape

    def out_copies(g):
        for b in range(GROUP):
            yield pltpu.make_async_copy(
                xbuf.at[g % 2, pl.ds(b * tok, tok), pl.ds(0, features)],
                outs[g * GROUP + b],
                osem.at[g % 2, b],
            )

    for g in range(2 * groups):
        if g >= 2:
            for copy in out_copies(g - 2):
                copy.wait()
        here = (groups + g if g < groups else g - groups) * slots

        @pl.loop(0, features // WIDE)
        def _(n):
            cols = pl.ds(pl.multiple_of(n * WIDE, WIDE), WIDE)
            made = jnp.concatenate(
                [gbuf[e, here : here + slots, cols] for e in range(exp_dev)], axis=0
            )
            xbuf[g % 2, :, cols] = jnp.dot(
                tbuf[g], made, preferred_element_type=jnp.float32
            ).astype(jnp.bfloat16)

        for copy in out_copies(g):
            copy.start()
    for g in range(2 * groups - 2, 2 * groups):
        for copy in out_copies(g):
            copy.wait()


def sizes(blocks, capacity, exp_dev):
    slots = -(-GROUP * capacity // 16) * 16
    return len(blocks), 2 * blocks[0][0].shape[0], slots, len(blocks) // GROUP, exp_dev * GROUP


def scratch(tok, features, exp_dev, slots):
    return [
        pltpu.VMEM((2, GROUP * tok, features + tok), jnp.bfloat16),
        pltpu.VMEM((exp_dev * slots, GROUP * tok), jnp.bfloat16),
        pltpu.VMEM((exp_dev * GROUP, tok), jnp.float32),
    ]


def gathered(blocks, first, capacity, exp_dev):
    nb, tok, slots, groups, _ = sizes(blocks, capacity, exp_dev)
    features = blocks[0][1].shape[1]
    xbuf, pbuf, small = scratch(tok, features, exp_dev, slots)
    return pl.pallas_call(
        functools.partial(early_kernel, (nb, slots)),
        out_shape=[
            jax.ShapeDtypeStruct((exp_dev, groups * slots, features), jnp.bfloat16),
            jax.ShapeDtypeStruct((groups, GROUP * tok, exp_dev * slots), jnp.bfloat16),
            jax.ShapeDtypeStruct((exp_dev, groups * slots, 1), jnp.float32),
        ],
        in_specs=[pl.BlockSpec(memory_space=pltpu.SMEM)]
        + [pl.BlockSpec(memory_space=pl.ANY)] * (2 * nb),
        grid=(1,),
        out_specs=[
            pl.BlockSpec((exp_dev, groups * slots, features), lambda i: (0, 0, 0)),
            pl.BlockSpec((groups, GROUP * tok, exp_dev * slots), lambda i: (0, 0, 0)),
            pl.BlockSpec((exp_dev, groups * slots, 1), lambda i: (0, 0, 0)),
        ],
        scratch_shapes=[xbuf, pbuf, small, small, pltpu.SemaphoreType.DMA((2, 2 * GROUP))],
        compiler_params=pltpu.CompilerParams(vmem_limit_bytes=LIMIT),
        cost_estimate=LIGHT,
        name="early",
    )(first, *[half for block in blocks for half in block])


def experts_of(ready, late, first, capacity, w_gate, w_up, w_down):
    rows, table, slotw = ready
    exp_dev, features, hidden = w_gate.shape
    nb, tok, slots, groups, pairs = sizes(late, capacity, exp_dev)
    every = 2 * groups * slots
    held = min(2, exp_dev)
    tiles = [(start, min(NARROW, hidden - start)) for start in range(0, hidden, NARROW)]
    smem = pl.BlockSpec(memory_space=pltpu.SMEM)
    anywhere = pl.BlockSpec(memory_space=pl.ANY)
    xbuf, pbuf, small = scratch(tok, features, exp_dev, slots)
    tbuf = pltpu.VMEM((2 * groups,) + table.shape[1:], jnp.bfloat16)
    act = pltpu.VMEM((every, hidden), jnp.bfloat16)
    blocks = [jax.ShapeDtypeStruct((tok, features), jnp.bfloat16)] * (2 * nb)
    got = pl.pallas_call(
        functools.partial(expert_kernel, (nb, exp_dev, slots, tiles)),
        grid=(1,),
        out_shape=blocks,
        in_specs=[smem]
        + [anywhere] * (2 * nb + 2)
        + [pl.BlockSpec(slotw.shape, lambda i: (0, 0, 0))]
        + [anywhere] * 3,
        out_specs=[anywhere] * (2 * nb),
        scratch_shapes=[
            pltpu.VMEM((held, features, hidden), jnp.bfloat16),
            pltpu.VMEM((held, features, hidden), jnp.bfloat16),
            pltpu.VMEM((held, hidden, features), jnp.bfloat16),
            xbuf,
            pltpu.VMEM((exp_dev, every, features), jnp.bfloat16),
            pbuf,
            tbuf,
            act,
            pltpu.VMEM((exp_dev, every, 1), jnp.float32),
            small,
            small,
            pltpu.SemaphoreType.DMA((3, held)),
            pltpu.SemaphoreType.DMA((2, 2 * GROUP)),
            pltpu.SemaphoreType.DMA((2, 2 * GROUP)),
            pltpu.SemaphoreType.DMA((exp_dev,)),
            pltpu.SemaphoreType.DMA,
        ],
        compiler_params=pltpu.CompilerParams(vmem_limit_bytes=LIMIT),
        cost_estimate=pl.CostEstimate(
            flops=6 * exp_dev * every * features * hidden,
            bytes_accessed=6 * exp_dev * features * hidden + 4 * nb * tok * features,
            transcendentals=0,
        ),
        name="experts",
    )(first, *[half for block in late for half in block], rows, table, slotw, w_gate, w_up, w_down)
    return list(got[:nb]), list(got[nb:])


def body(tokens, norm_gain, gate_weights, routes, moves, w_gate, w_up, w_down):
    tok_rows, features = tokens.shape
    per_token = routes.shape[1]
    exp_dev = w_gate.shape[0]
    group = lax.axis_size("row") * lax.axis_size("col")
    experts = group * exp_dev
    capacity = tok_rows * per_token * 3 // (2 * experts)
    half = tok_rows // 2
    halves = pl.pallas_call(
        head_kernel,
        out_shape=[
            jax.ShapeDtypeStruct((half, features + tok_rows), jnp.bfloat16),
            jax.ShapeDtypeStruct((half, features), jnp.bfloat16),
        ],
        name="head",
    )(tokens, norm_gain.reshape(1, features), gate_weights.T, routes.T)
    first = (lax.axis_index(("row", "col")) * exp_dev).astype(jnp.int32).reshape(1)
    ready, late = spread(
        list(halves), lambda blocks: gathered(blocks, first, capacity, exp_dev)
    )
    late, early = experts_of(ready, late, first, capacity, w_gate, w_up, w_down)
    total = added(tokens, *collected(late, early))
    rows = jnp.arange(tok_rows, dtype=jnp.int32)
    pick = (moves[0, 0][:, None] == rows[None, :]).astype(jnp.bfloat16)
    leaving = jnp.dot(pick, total, preferred_element_type=jnp.float32).astype(jnp.bfloat16)
    incoming = shifted(leaving, "rep", 1)
    second = lax.axis_index("rep") == 1
    target = jnp.where(second, moves[0, 1], moves[0, 0])
    match = rows[:, None] == target[None, :]
    placed = jnp.dot(match.astype(jnp.bfloat16), incoming, preferred_element_type=jnp.float32)
    placed = jnp.where(second, placed, 0.0).astype(jnp.bfloat16)
    return jnp.where(jnp.any(match, axis=1, keepdims=True), placed, total)


def solution(mesh):
    return jax.shard_map(
        body,
        mesh=mesh,
        in_specs=(
            P(("rep", "row", "col"), None),
            P(),
            P(("rep", "row", "col"), None),
            P(("rep", "row", "col"), None),
            P(("row", "col"), None, None),
            P(("row", "col"), None, None),
            P(("row", "col"), None, None),
            P(("row", "col"), None, None),
        ),
        out_specs=P(("rep", "row", "col"), None),
        check_vma=False,
    )
```

```python
import functools

import jax
import jax.numpy as jnp
from jax import lax
from jax.experimental import pallas as pl
from jax.experimental.pallas import tpu as pltpu
from jax.sharding import PartitionSpec as P

GROUP = 8
PIECES = 4
LANE = 8
WIDE = 512
NARROW = 512
LIMIT = 60 * 1024 * 1024
LIGHT = pl.CostEstimate(flops=1, bytes_accessed=1, transcendentals=0)


def shifted(value, axis, steps):
    count = lax.axis_size(axis)
    first, last = (max(0, -steps), min(count, count - steps))
    return lax.ppermute(value, axis, [(source, source + steps) for source in range(first, last)])


def turned(value, steps):
    count = lax.axis_size("col")
    return lax.ppermute(value, "col", [(source, (source + steps) % count) for source in range(count)])


def swapped(value, bit):
    count = lax.axis_size("row")
    return lax.ppermute(value, "row", [(source, source ^ bit) for source in range(count)])


def spread(halves, gather):
    line, other, last = [halves], [], halves
    for _ in range(1, lax.axis_size("col")):
        pairs = [lax.optimization_barrier((turned(one, 1), swapped(one, 2))) for one in last]
        last = [ahead for ahead, _ in pairs]
        line.append(last)
        other.append([across for _, across in pairs])
    ready = gather(line + [[swapped(one, 1) for one in block] for block in line])
    final = [swapped(one, 2) for one in last]
    held = lax.optimization_barrier((*final, ready[2]))[: len(final)]
    far = [[swapped(one, 1) for one in block] for block in other + [list(held)]]
    return ready, other + [final] + far


def added(*parts):
    return sum(part.astype(jnp.float32) for part in parts).astype(jnp.bfloat16)


def collected(late, early):
    cols = lax.axis_size("col")
    order = list(range(cols // 2, 0, -1)) + list(range(cols // 2 + 1, cols)) + [0]
    held = {step: swapped(late[cols + step], 1) for step in order}
    sent = {step: swapped(added(late[step], held[step]), 2) for step in order}
    far = {
        step: swapped(lax.optimization_barrier((early[cols + step], held[step]))[0], 1)
        for step in order
    }
    line = [[early[step], far[step], sent[step]] for step in range(cols)]
    down, up = [], []
    for step in range(cols // 2, 0, -1):
        down = [turned(added(*(line[step] + down)), -1)]
        if step == cols // 2:
            ahead = down[0]
    for step in range(cols // 2 + 1, cols):
        value = added(*(line[step] + up))
        if not up:
            value = lax.optimization_barrier((value, ahead))[0]
        up = [turned(value, 1)]
    return line[0] + up + down


def head_kernel(tokens_ref, gain_ref, weights_ref, routes_ref, *outs):
    features, per_token = tokens_ref.shape[1], routes_ref.shape[0]
    widened = tokens_ref[...].astype(jnp.float32)
    scale = lax.rsqrt(jnp.mean(widened * widened, axis=-1, keepdims=True) + 1e-06)
    normed = (widened * scale * gain_ref[...]).astype(jnp.bfloat16)
    half = outs[0].shape[0]
    for i, out_ref in enumerate(outs):
        out_ref[:, :features] = normed[i * half : (i + 1) * half]
    weights = weights_ref[...]
    high = weights.astype(jnp.bfloat16).astype(jnp.float32)
    middle = (weights - high).astype(jnp.bfloat16).astype(jnp.float32)
    low = weights - high - middle
    gap = jnp.zeros((LANE - per_token, weights.shape[1]), jnp.float32)
    meta = [routes_ref[...].astype(jnp.float32), gap - 1.0, high, gap, middle, gap, low, gap]
    outs[0][: 4 * LANE, features:] = jnp.concatenate(meta, axis=0).astype(jnp.bfloat16)
    outs[0][4 * LANE :, features:] = jnp.zeros(
        (half - 4 * LANE, weights.shape[1]), jnp.bfloat16
    )


def gather_groups(xs, first, slots, xbuf, xsem, named_s, weight_s, pbuf, tbuf, put_weight, put_rows, begin=None):
    groups = len(xs) // (2 * GROUP)
    half = xs[0].shape[0]
    tok = 2 * half
    features = xs[1].shape[1]
    pairs = named_s.shape[0]
    exp_dev = pairs // GROUP

    def copies(g):
        for b in range(GROUP):
            for h in range(2):
                source = xs[2 * (g * GROUP + b) + h]
                target = xbuf.at[
                    g % 2, pl.ds(b * tok + h * half, half), pl.ds(0, source.shape[1])
                ]
                yield pltpu.make_async_copy(source, target, xsem.at[g % 2, 2 * b + h])

    def load(g):
        for copy in copies(g):
            copy.start()

    for g in range(min(2, groups)):
        load(g)
    if begin is not None:
        begin()
    lane = lax.broadcasted_iota(jnp.int32, (tok, tok), 1)
    sub = lax.broadcasted_iota(jnp.int32, (tok, tok), 0)
    upto = (sub <= lane).astype(jnp.bfloat16)
    pair_r = lax.broadcasted_iota(jnp.int32, (pairs, pairs), 0)
    pair_c = lax.broadcasted_iota(jnp.int32, (pairs, pairs), 1)
    before = ((pair_r // GROUP == pair_c // GROUP) & (pair_c < pair_r)).astype(jnp.bfloat16)
    slot_id = lax.broadcasted_iota(jnp.int32, (slots, tok), 0).astype(jnp.float32)
    wide_id = lax.broadcasted_iota(jnp.int32, (tok, exp_dev * slots), 1).astype(jnp.float32)
    offset = lax.broadcasted_iota(jnp.int32, (pairs, tok), 0) // GROUP * slots
    offset = offset.astype(jnp.float32)

    for g in range(groups):
        for copy in copies(g):
            copy.wait()
        for b in range(GROUP):
            meta = xbuf[g % 2, b * tok : b * tok + 4 * LANE, features:].astype(jnp.float32)
            chosen = meta[:LANE]
            given = meta[LANE : 2 * LANE] + meta[2 * LANE : 3 * LANE] + meta[3 * LANE : 4 * LANE]
            for e in range(exp_dev):
                hit = chosen == (first + e).astype(jnp.float32)
                named_s[e * GROUP + b : e * GROUP + b + 1, :] = jnp.sum(
                    hit.astype(jnp.float32), axis=0, keepdims=True
                )
                weight_s[e * GROUP + b : e * GROUP + b + 1, :] = jnp.sum(
                    jnp.where(hit, given, 0.0), axis=0, keepdims=True
                )
        named = named_s[...]
        count = jnp.dot(named.astype(jnp.bfloat16), upto, preferred_element_type=jnp.float32)
        totals = jnp.broadcast_to(count[:, tok - 1 :], (pairs, tok)).astype(jnp.bfloat16)
        base = jnp.dot(before, totals, preferred_element_type=jnp.float32)
        named_s[...] = jnp.where(named > 0.5, base + count - 1.0, -1.0)
        for e in range(exp_dev):
            total = jnp.zeros((slots, tok), jnp.float32)
            for b in range(GROUP):
                pick = slot_id == named_s[e * GROUP + b : e * GROUP + b + 1, :]
                pbuf[e * slots : (e + 1) * slots, b * tok : (b + 1) * tok] = pick.astype(
                    jnp.float32
                ).astype(jnp.bfloat16)
                total += jnp.where(pick, weight_s[e * GROUP + b : e * GROUP + b + 1, :], 0.0)
            put_weight(g, e, jnp.sum(total, axis=1, keepdims=True))
        place = named_s[...]
        place = jnp.where(place < -0.5, place, place + offset)
        place = jnp.concatenate([place, jnp.zeros((tok - pairs, tok), jnp.float32)], axis=0).T
        for b in range(GROUP):
            pick = wide_id == place[:, b : b + 1]
            for e in range(1, exp_dev):
                pick = pick | (wide_id == place[:, e * GROUP + b : e * GROUP + b + 1])
            tbuf[g, b * tok : (b + 1) * tok, :] = pick.astype(jnp.float32).astype(jnp.bfloat16)

        @pl.loop(0, features // WIDE)
        def _(n):
            cols = pl.ds(pl.multiple_of(n * WIDE, WIDE), WIDE)
            got = jnp.dot(pbuf[...], xbuf[g % 2, :, cols], preferred_element_type=jnp.float32)
            got = got.astype(jnp.bfloat16)
            for e in range(exp_dev):
                put_rows(g, e, cols, got[e * slots : (e + 1) * slots])

        if g + 2 < groups:
            load(g + 2)


def early_kernel(plan, first_ref, *refs):
    nb, slots = plan
    xs, refs = refs[: 2 * nb], refs[2 * nb :]
    rows_ref, tbuf, slotw, xbuf, pbuf, named_s, weight_s, xsem = refs

    def put_weight(g, e, value):
        slotw[e, g * slots : (g + 1) * slots, :] = value

    def put_rows(g, e, cols, value):
        rows_ref[e, g * slots : (g + 1) * slots, cols] = value

    gather_groups(
        xs, first_ref[0], slots, xbuf, xsem, named_s, weight_s, pbuf, tbuf, put_weight, put_rows
    )


def expert_kernel(plan, first_ref, *refs):
    nb, exp_dev, slots, tiles = plan
    xs, refs = refs[: 2 * nb], refs[2 * nb :]
    rows_ref, table_ref, slotw_ref, gate_ref, up_ref, down_ref = refs[:6]
    outs, refs = refs[6 : 6 + 2 * nb], refs[6 + 2 * nb :]
    gate_b, up_b, down_b, xbuf, gbuf, pbuf, tbuf, act, obuf, stage, slotw = refs[:11]
    named_s, weight_s, wsem, downsem, xsem, osem, rsem, tsem = refs[11:]
    groups = nb // GROUP
    tok, features = outs[0].shape
    early = groups * slots
    steps = features // WIDE

    def pieces_start(source, target, sem):
        size = target.shape[0] // PIECES
        for piece in range(PIECES):
            part = pl.ds(piece * size, size)
            copy = pltpu.make_async_copy(source.at[part, :], target.at[part, :], sem)
            copy.start(priority=piece % 2)

    def weight_refs(kind, e, slot):
        source, target = ((gate_ref, gate_b), (up_ref, up_b))[kind]
        return source.at[e], target.at[slot], wsem.at[kind, slot]

    def down_refs(n, e):
        source = down_ref.at[e, :, pl.ds(n * WIDE, WIDE)]
        return source, down_b.at[n % 2, e], downsem.at[n % 2, e]

    def fetch(e, slot):
        for kind in range(2):
            pieces_start(*weight_refs(kind, e, slot))

    def fetch_down(n):
        for e in range(exp_dev):
            pieces_start(*down_refs(n, e))

    def arrive(kind, e, slot):
        pltpu.make_async_copy(*weight_refs(kind, e, slot)).wait()

    def rows_copy(e):
        return pltpu.make_async_copy(rows_ref.at[e], gbuf.at[e, pl.ds(0, early), :], rsem.at[e])

    def out_copy(n, g, b):
        return pltpu.make_async_copy(
            stage.at[n % 2, g, pl.ds(b * tok, tok), :],
            outs[g * GROUP + b].at[:, pl.ds(n * WIDE, WIDE)],
            osem.at[n % 2, g, b],
        )

    table_in = pltpu.make_async_copy(table_ref, tbuf.at[pl.ds(groups, groups)], tsem)

    def put_weight(g, e, value):
        slotw[e, early + g * slots : early + (g + 1) * slots, :] = value

    def put_rows(g, e, cols, value):
        gbuf[e, early + g * slots : early + (g + 1) * slots, cols] = value

    def begin():
        pieces_start(*weight_refs(0, 0, 0))
        for e in range(exp_dev):
            rows_copy(e).start()
        pieces_start(*weight_refs(1, 0, 0))
        if exp_dev > 1:
            fetch(1, 1)
        table_in.start()
        for n in range(min(2, steps)):
            fetch_down(n)
        slotw[:, :early, :] = slotw_ref[...]

    gather_groups(
        xs,
        first_ref[0],
        slots,
        xbuf,
        xsem,
        named_s,
        weight_s,
        pbuf,
        tbuf,
        put_weight,
        put_rows,
        begin,
    )

    @pl.loop(0, exp_dev)
    def _(e):
        slot = lax.rem(e, gate_b.shape[0])
        rows_copy(e).wait()
        arrive(0, e, slot)
        arrive(1, e, slot)
        for start, size in tiles:
            gate = jnp.dot(
                gbuf[e], gate_b[slot, :, start : start + size], preferred_element_type=jnp.float32
            )
            upward = jnp.dot(
                gbuf[e], up_b[slot, :, start : start + size], preferred_element_type=jnp.float32
            )
            act[e, :, start : start + size] = (
                0.5 * gate * (1.0 + jnp.tanh(0.5 * gate)) * upward * slotw[e]
            ).astype(jnp.bfloat16)

        @pl.when(e + 2 < exp_dev)
        def _():
            fetch(e + 2, slot)

    table_in.wait()
    for n in range(steps):
        for e in range(exp_dev):
            pltpu.make_async_copy(*down_refs(n, e)).wait()
            obuf[e] = jnp.dot(
                act[e], down_b[n % 2, e], preferred_element_type=jnp.float32
            ).astype(jnp.bfloat16)
        if n + 2 < steps:
            fetch_down(n + 2)
        for g in range(2 * groups):
            if n >= 2:
                for b in range(GROUP):
                    out_copy(n - 2, g, b).wait()
            here = (groups + g if g < groups else g - groups) * slots
            made = jnp.concatenate(
                [obuf[e, here : here + slots, :] for e in range(exp_dev)], axis=0
            )
            stage[n % 2, g] = jnp.dot(
                tbuf[g], made, preferred_element_type=jnp.float32
            ).astype(jnp.bfloat16)
            for b in range(GROUP):
                out_copy(n, g, b).start()
    for n in range(max(0, steps - 2), steps):
        for g in range(2 * groups):
            for b in range(GROUP):
                out_copy(n, g, b).wait()


def sizes(blocks, capacity, exp_dev):
    slots = -(-GROUP * capacity // 16) * 16
    return len(blocks), 2 * blocks[0][0].shape[0], slots, len(blocks) // GROUP, exp_dev * GROUP


def scratch(tok, features, exp_dev, slots, groups):
    return [
        pltpu.VMEM((min(2, groups), GROUP * tok, features + tok), jnp.bfloat16),
        pltpu.VMEM((exp_dev * slots, GROUP * tok), jnp.bfloat16),
        pltpu.VMEM((exp_dev * GROUP, tok), jnp.float32),
    ]


def gathered(blocks, first, capacity, exp_dev):
    nb, tok, slots, groups, _ = sizes(blocks, capacity, exp_dev)
    features = blocks[0][1].shape[1]
    xbuf, pbuf, small = scratch(tok, features, exp_dev, slots, groups)
    return pl.pallas_call(
        functools.partial(early_kernel, (nb, slots)),
        out_shape=[
            jax.ShapeDtypeStruct((exp_dev, groups * slots, features), jnp.bfloat16),
            jax.ShapeDtypeStruct((groups, GROUP * tok, exp_dev * slots), jnp.bfloat16),
            jax.ShapeDtypeStruct((exp_dev, groups * slots, 1), jnp.float32),
        ],
        in_specs=[pl.BlockSpec(memory_space=pltpu.SMEM)]
        + [pl.BlockSpec(memory_space=pl.ANY)] * (2 * nb),
        grid=(1,),
        out_specs=[
            pl.BlockSpec((exp_dev, groups * slots, features), lambda i: (0, 0, 0)),
            pl.BlockSpec((groups, GROUP * tok, exp_dev * slots), lambda i: (0, 0, 0)),
            pl.BlockSpec((exp_dev, groups * slots, 1), lambda i: (0, 0, 0)),
        ],
        scratch_shapes=[xbuf, pbuf, small, small, pltpu.SemaphoreType.DMA((2, 2 * GROUP))],
        compiler_params=pltpu.CompilerParams(vmem_limit_bytes=LIMIT),
        cost_estimate=LIGHT,
        name="early",
    )(first, *[half for block in blocks for half in block])


def experts_of(ready, late, first, capacity, w_gate, w_up, w_down):
    rows, table, slotw = ready
    exp_dev, features, hidden = w_gate.shape
    nb, tok, slots, groups, pairs = sizes(late, capacity, exp_dev)
    every = 2 * groups * slots
    held = min(2, exp_dev)
    tiles = [(start, min(NARROW, hidden - start)) for start in range(0, hidden, NARROW)]
    smem = pl.BlockSpec(memory_space=pltpu.SMEM)
    anywhere = pl.BlockSpec(memory_space=pl.ANY)
    xbuf, pbuf, small = scratch(tok, features, exp_dev, slots, groups)
    tbuf = pltpu.VMEM((2 * groups,) + table.shape[1:], jnp.bfloat16)
    act = pltpu.VMEM((exp_dev, every, hidden), jnp.bfloat16)
    blocks = [jax.ShapeDtypeStruct((tok, features), jnp.bfloat16)] * (2 * nb)
    got = pl.pallas_call(
        functools.partial(expert_kernel, (nb, exp_dev, slots, tiles)),
        grid=(1,),
        out_shape=blocks,
        in_specs=[smem]
        + [anywhere] * (2 * nb + 2)
        + [pl.BlockSpec(slotw.shape, lambda i: (0, 0, 0))]
        + [anywhere] * 3,
        out_specs=[anywhere] * (2 * nb),
        scratch_shapes=[
            pltpu.VMEM((held, features, hidden), jnp.bfloat16),
            pltpu.VMEM((held, features, hidden), jnp.bfloat16),
            pltpu.VMEM((2, exp_dev, hidden, WIDE), jnp.bfloat16),
            xbuf,
            pltpu.VMEM((exp_dev, every, features), jnp.bfloat16),
            pbuf,
            tbuf,
            act,
            pltpu.VMEM((exp_dev, every, WIDE), jnp.bfloat16),
            pltpu.VMEM((2, 2 * groups, GROUP * tok, WIDE), jnp.bfloat16),
            pltpu.VMEM((exp_dev, every, 1), jnp.float32),
            small,
            small,
            pltpu.SemaphoreType.DMA((2, held)),
            pltpu.SemaphoreType.DMA((2, exp_dev)),
            pltpu.SemaphoreType.DMA((2, 2 * GROUP)),
            pltpu.SemaphoreType.DMA((2, 2 * groups, GROUP)),
            pltpu.SemaphoreType.DMA((exp_dev,)),
            pltpu.SemaphoreType.DMA,
        ],
        compiler_params=pltpu.CompilerParams(vmem_limit_bytes=LIMIT),
        cost_estimate=pl.CostEstimate(
            flops=6 * exp_dev * every * features * hidden,
            bytes_accessed=6 * exp_dev * features * hidden + 4 * nb * tok * features,
            transcendentals=0,
        ),
        name="experts",
    )(first, *[half for block in late for half in block], rows, table, slotw, w_gate, w_up, w_down)
    return list(got[:nb]), list(got[nb:])


def body(tokens, norm_gain, gate_weights, routes, moves, w_gate, w_up, w_down):
    tok_rows, features = tokens.shape
    per_token = routes.shape[1]
    exp_dev = w_gate.shape[0]
    group = lax.axis_size("row") * lax.axis_size("col")
    experts = group * exp_dev
    capacity = tok_rows * per_token * 3 // (2 * experts)
    half = tok_rows // 2
    halves = pl.pallas_call(
        head_kernel,
        out_shape=[
            jax.ShapeDtypeStruct((half, features + tok_rows), jnp.bfloat16),
            jax.ShapeDtypeStruct((half, features), jnp.bfloat16),
        ],
        name="head",
    )(tokens, norm_gain.reshape(1, features), gate_weights.T, routes.T)
    first = (lax.axis_index(("row", "col")) * exp_dev).astype(jnp.int32).reshape(1)
    ready, late = spread(
        list(halves), lambda blocks: gathered(blocks, first, capacity, exp_dev)
    )
    late, early = experts_of(ready, late, first, capacity, w_gate, w_up, w_down)
    total = added(tokens, *collected(late, early))
    rows = jnp.arange(tok_rows, dtype=jnp.int32)
    pick = (moves[0, 0][:, None] == rows[None, :]).astype(jnp.bfloat16)
    leaving = jnp.dot(pick, total, preferred_element_type=jnp.float32).astype(jnp.bfloat16)
    incoming = shifted(leaving, "rep", 1)
    second = lax.axis_index("rep") == 1
    target = jnp.where(second, moves[0, 1], moves[0, 0])
    match = rows[:, None] == target[None, :]
    placed = jnp.dot(match.astype(jnp.bfloat16), incoming, preferred_element_type=jnp.float32)
    placed = jnp.where(second, placed, 0.0).astype(jnp.bfloat16)
    return jnp.where(jnp.any(match, axis=1, keepdims=True), placed, total)


def solution(mesh):
    return jax.shard_map(
        body,
        mesh=mesh,
        in_specs=(
            P(("rep", "row", "col"), None),
            P(),
            P(("rep", "row", "col"), None),
            P(("rep", "row", "col"), None),
            P(("row", "col"), None, None),
            P(("row", "col"), None, None),
            P(("row", "col"), None, None),
            P(("row", "col"), None, None),
        ),
        out_specs=P(("rep", "row", "col"), None),
        check_vma=False,
    )
```

```python
import functools

import jax
import jax.numpy as jnp
from jax import lax
from jax.experimental import pallas as pl
from jax.experimental.pallas import tpu as pltpu
from jax.sharding import PartitionSpec as P

GROUP = 8
PIECES = 4
LANE = 8
WIDE = 512
NARROW = 512
LIMIT = 60 * 1024 * 1024
LIGHT = pl.CostEstimate(flops=1, bytes_accessed=1, transcendentals=0)


def shifted(value, axis, steps):
    count = lax.axis_size(axis)
    first, last = (max(0, -steps), min(count, count - steps))
    return lax.ppermute(value, axis, [(source, source + steps) for source in range(first, last)])


def turned(value, steps):
    count = lax.axis_size("col")
    return lax.ppermute(value, "col", [(source, (source + steps) % count) for source in range(count)])


def swapped(value, bit):
    count = lax.axis_size("row")
    return lax.ppermute(value, "row", [(source, source ^ bit) for source in range(count)])


def spread(halves, gather):
    line, other, last = [halves], [], halves
    for _ in range(1, lax.axis_size("col")):
        pairs = [lax.optimization_barrier((turned(one, 1), swapped(one, 2))) for one in last]
        last = [ahead for ahead, _ in pairs]
        line.append(last)
        other.append([across for _, across in pairs])
    ready = gather(line + [[swapped(one, 1) for one in block] for block in line])
    final = [swapped(one, 2) for one in last]
    held = lax.optimization_barrier((*final, ready[2]))[: len(final)]
    far = [[swapped(one, 1) for one in block] for block in other + [list(held)]]
    return ready, other + [final] + far


def added(*parts):
    return sum(part.astype(jnp.float32) for part in parts).astype(jnp.bfloat16)


def collected(late, early):
    cols = lax.axis_size("col")
    order = list(range(cols // 2, 0, -1)) + list(range(cols // 2 + 1, cols)) + [0]
    held = {step: swapped(late[cols + step], 1) for step in order}
    sent = {step: swapped(added(late[step], held[step]), 2) for step in order}
    far = {
        step: swapped(lax.optimization_barrier((early[cols + step], held[step]))[0], 1)
        for step in order
    }
    line = [[early[step], far[step], sent[step]] for step in range(cols)]
    down, up = [], []
    for step in range(cols // 2, 0, -1):
        down = [turned(added(*(line[step] + down)), -1)]
        if step == cols // 2:
            ahead = down[0]
    for step in range(cols // 2 + 1, cols):
        value = added(*(line[step] + up))
        if not up:
            value = lax.optimization_barrier((value, ahead))[0]
        up = [turned(value, 1)]
    return line[0] + up, down[0]


def head_kernel(tokens_ref, gain_ref, weights_ref, routes_ref, *outs):
    features, per_token = tokens_ref.shape[1], routes_ref.shape[0]
    widened = tokens_ref[...].astype(jnp.float32)
    scale = lax.rsqrt(jnp.mean(widened * widened, axis=-1, keepdims=True) + 1e-06)
    normed = (widened * scale * gain_ref[...]).astype(jnp.bfloat16)
    half = outs[0].shape[0]
    for i, out_ref in enumerate(outs):
        out_ref[:, :features] = normed[i * half : (i + 1) * half]
    weights = weights_ref[...]
    high = weights.astype(jnp.bfloat16).astype(jnp.float32)
    middle = (weights - high).astype(jnp.bfloat16).astype(jnp.float32)
    low = weights - high - middle
    gap = jnp.zeros((LANE - per_token, weights.shape[1]), jnp.float32)
    meta = [routes_ref[...].astype(jnp.float32), gap - 1.0, high, gap, middle, gap, low, gap]
    outs[0][: 4 * LANE, features:] = jnp.concatenate(meta, axis=0).astype(jnp.bfloat16)
    outs[0][4 * LANE :, features:] = jnp.zeros(
        (half - 4 * LANE, weights.shape[1]), jnp.bfloat16
    )


def gather_groups(xs, first, slots, xbuf, xsem, named_s, weight_s, pbuf, tbuf, put_weight, put_rows, begin=None):
    groups = len(xs) // (2 * GROUP)
    half = xs[0].shape[0]
    tok = 2 * half
    features = xs[1].shape[1]
    pairs = named_s.shape[0]
    exp_dev = pairs // GROUP

    def copies(g):
        for b in range(GROUP):
            for h in range(2):
                source = xs[2 * (g * GROUP + b) + h]
                target = xbuf.at[
                    g % 2, pl.ds(b * tok + h * half, half), pl.ds(0, source.shape[1])
                ]
                yield pltpu.make_async_copy(source, target, xsem.at[g % 2, 2 * b + h])

    def load(g):
        for copy in copies(g):
            copy.start()

    for g in range(min(2, groups)):
        load(g)
    if begin is not None:
        begin()
    lane = lax.broadcasted_iota(jnp.int32, (tok, tok), 1)
    sub = lax.broadcasted_iota(jnp.int32, (tok, tok), 0)
    upto = (sub <= lane).astype(jnp.bfloat16)
    pair_r = lax.broadcasted_iota(jnp.int32, (pairs, pairs), 0)
    pair_c = lax.broadcasted_iota(jnp.int32, (pairs, pairs), 1)
    before = ((pair_r // GROUP == pair_c // GROUP) & (pair_c < pair_r)).astype(jnp.bfloat16)
    slot_id = lax.broadcasted_iota(jnp.int32, (slots, tok), 0).astype(jnp.float32)
    wide_id = lax.broadcasted_iota(jnp.int32, (tok, exp_dev * slots), 1).astype(jnp.float32)
    offset = lax.broadcasted_iota(jnp.int32, (pairs, tok), 0) // GROUP * slots
    offset = offset.astype(jnp.float32)

    for g in range(groups):
        for copy in copies(g):
            copy.wait()
        for b in range(GROUP):
            meta = xbuf[g % 2, b * tok : b * tok + 4 * LANE, features:].astype(jnp.float32)
            chosen = meta[:LANE]
            given = meta[LANE : 2 * LANE] + meta[2 * LANE : 3 * LANE] + meta[3 * LANE : 4 * LANE]
            for e in range(exp_dev):
                hit = chosen == (first + e).astype(jnp.float32)
                named_s[e * GROUP + b : e * GROUP + b + 1, :] = jnp.sum(
                    hit.astype(jnp.float32), axis=0, keepdims=True
                )
                weight_s[e * GROUP + b : e * GROUP + b + 1, :] = jnp.sum(
                    jnp.where(hit, given, 0.0), axis=0, keepdims=True
                )
        named = named_s[...]
        count = jnp.dot(named.astype(jnp.bfloat16), upto, preferred_element_type=jnp.float32)
        totals = jnp.broadcast_to(count[:, tok - 1 :], (pairs, tok)).astype(jnp.bfloat16)
        base = jnp.dot(before, totals, preferred_element_type=jnp.float32)
        named_s[...] = jnp.where(named > 0.5, base + count - 1.0, -1.0)
        for e in range(exp_dev):
            total = jnp.zeros((slots, tok), jnp.float32)
            for b in range(GROUP):
                pick = slot_id == named_s[e * GROUP + b : e * GROUP + b + 1, :]
                pbuf[e * slots : (e + 1) * slots, b * tok : (b + 1) * tok] = pick.astype(
                    jnp.float32
                ).astype(jnp.bfloat16)
                total += jnp.where(pick, weight_s[e * GROUP + b : e * GROUP + b + 1, :], 0.0)
            put_weight(g, e, jnp.sum(total, axis=1, keepdims=True))
        place = named_s[...]
        place = jnp.where(place < -0.5, place, place + offset)
        place = jnp.concatenate([place, jnp.zeros((tok - pairs, tok), jnp.float32)], axis=0).T
        for b in range(GROUP):
            pick = wide_id == place[:, b : b + 1]
            for e in range(1, exp_dev):
                pick = pick | (wide_id == place[:, e * GROUP + b : e * GROUP + b + 1])
            tbuf[g, b * tok : (b + 1) * tok, :] = pick.astype(jnp.float32).astype(jnp.bfloat16)

        @pl.loop(0, features // WIDE)
        def _(n):
            cols = pl.ds(pl.multiple_of(n * WIDE, WIDE), WIDE)
            got = jnp.dot(pbuf[...], xbuf[g % 2, :, cols], preferred_element_type=jnp.float32)
            got = got.astype(jnp.bfloat16)
            for e in range(exp_dev):
                put_rows(g, e, cols, got[e * slots : (e + 1) * slots])

        if g + 2 < groups:
            load(g + 2)


def early_kernel(plan, first_ref, *refs):
    nb, slots = plan
    xs, refs = refs[: 2 * nb], refs[2 * nb :]
    rows_ref, tbuf, slotw, xbuf, pbuf, named_s, weight_s, xsem = refs

    def put_weight(g, e, value):
        slotw[e, g * slots : (g + 1) * slots, :] = value

    def put_rows(g, e, cols, value):
        rows_ref[e, g * slots : (g + 1) * slots, cols] = value

    gather_groups(
        xs, first_ref[0], slots, xbuf, xsem, named_s, weight_s, pbuf, tbuf, put_weight, put_rows
    )


def expert_kernel(plan, first_ref, *refs):
    nb, exp_dev, slots, tiles = plan
    xs, refs = refs[: 2 * nb], refs[2 * nb :]
    rows_ref, table_ref, slotw_ref, gate_ref, up_ref, down_ref = refs[:6]
    outs, refs = refs[6 : 6 + 2 * nb], refs[6 + 2 * nb :]
    gate_b, up_b, down_b, xbuf, gbuf, pbuf, tbuf, act, obuf, stage, slotw = refs[:11]
    named_s, weight_s, wsem, downsem, xsem, osem, rsem, tsem = refs[11:]
    groups = nb // GROUP
    tok, features = outs[0].shape
    early = groups * slots
    steps = features // WIDE

    def pieces_start(source, target, sem):
        size = target.shape[0] // PIECES
        for piece in range(PIECES):
            part = pl.ds(piece * size, size)
            copy = pltpu.make_async_copy(source.at[part, :], target.at[part, :], sem)
            copy.start(priority=piece % 2)

    def weight_refs(kind, e, slot):
        source, target = ((gate_ref, gate_b), (up_ref, up_b))[kind]
        return source.at[e], target.at[slot], wsem.at[kind, slot]

    def down_refs(n, e):
        source = down_ref.at[e, :, pl.ds(n * WIDE, WIDE)]
        return source, down_b.at[n % 2, e], downsem.at[n % 2, e]

    def fetch(e, slot):
        for kind in range(2):
            pieces_start(*weight_refs(kind, e, slot))

    def fetch_down(n):
        for e in range(exp_dev):
            pieces_start(*down_refs(n, e))

    def arrive(kind, e, slot):
        pltpu.make_async_copy(*weight_refs(kind, e, slot)).wait()

    def rows_copy(e):
        return pltpu.make_async_copy(rows_ref.at[e], gbuf.at[e, pl.ds(0, early), :], rsem.at[e])

    def out_copy(n, g, b):
        return pltpu.make_async_copy(
            stage.at[n % 2, g, pl.ds(b * tok, tok), :],
            outs[g * GROUP + b].at[:, pl.ds(n * WIDE, WIDE)],
            osem.at[n % 2, g, b],
        )

    table_in = pltpu.make_async_copy(table_ref, tbuf.at[pl.ds(groups, groups)], tsem)

    def put_weight(g, e, value):
        slotw[e, early + g * slots : early + (g + 1) * slots, :] = value

    def put_rows(g, e, cols, value):
        gbuf[e, early + g * slots : early + (g + 1) * slots, cols] = value

    def begin():
        pieces_start(*weight_refs(0, 0, 0))
        for e in range(exp_dev):
            rows_copy(e).start()
        pieces_start(*weight_refs(1, 0, 0))
        if exp_dev > 1:
            fetch(1, 1)
        table_in.start()
        for n in range(min(2, steps)):
            fetch_down(n)
        slotw[:, :early, :] = slotw_ref[...]

    gather_groups(
        xs,
        first_ref[0],
        slots,
        xbuf,
        xsem,
        named_s,
        weight_s,
        pbuf,
        tbuf,
        put_weight,
        put_rows,
        begin,
    )

    @pl.loop(0, exp_dev)
    def _(e):
        slot = lax.rem(e, gate_b.shape[0])
        rows_copy(e).wait()
        arrive(0, e, slot)
        arrive(1, e, slot)
        for start, size in tiles:
            gate = jnp.dot(
                gbuf[e], gate_b[slot, :, start : start + size], preferred_element_type=jnp.float32
            )
            upward = jnp.dot(
                gbuf[e], up_b[slot, :, start : start + size], preferred_element_type=jnp.float32
            )
            act[e, :, start : start + size] = (
                0.5 * gate * (1.0 + jnp.tanh(0.5 * gate)) * upward * slotw[e]
            ).astype(jnp.bfloat16)

        @pl.when(e + 2 < exp_dev)
        def _():
            fetch(e + 2, slot)

    table_in.wait()
    for n in range(steps):
        for e in range(exp_dev):
            pltpu.make_async_copy(*down_refs(n, e)).wait()
            obuf[e] = jnp.dot(
                act[e], down_b[n % 2, e], preferred_element_type=jnp.float32
            ).astype(jnp.bfloat16)
        if n + 2 < steps:
            fetch_down(n + 2)
        for g in range(2 * groups):
            if n >= 2:
                for b in range(GROUP):
                    out_copy(n - 2, g, b).wait()
            here = (groups + g if g < groups else g - groups) * slots
            made = jnp.concatenate(
                [obuf[e, here : here + slots, :] for e in range(exp_dev)], axis=0
            )
            stage[n % 2, g] = jnp.dot(
                tbuf[g], made, preferred_element_type=jnp.float32
            ).astype(jnp.bfloat16)
            for b in range(GROUP):
                out_copy(n, g, b).start()
    for n in range(max(0, steps - 2), steps):
        for g in range(2 * groups):
            for b in range(GROUP):
                out_copy(n, g, b).wait()


def sizes(blocks, capacity, exp_dev):
    slots = -(-GROUP * capacity // 16) * 16
    return len(blocks), 2 * blocks[0][0].shape[0], slots, len(blocks) // GROUP, exp_dev * GROUP


def scratch(tok, features, exp_dev, slots, groups):
    return [
        pltpu.VMEM((min(2, groups), GROUP * tok, features + tok), jnp.bfloat16),
        pltpu.VMEM((exp_dev * slots, GROUP * tok), jnp.bfloat16),
        pltpu.VMEM((exp_dev * GROUP, tok), jnp.float32),
    ]


def gathered(blocks, first, capacity, exp_dev):
    nb, tok, slots, groups, _ = sizes(blocks, capacity, exp_dev)
    features = blocks[0][1].shape[1]
    xbuf, pbuf, small = scratch(tok, features, exp_dev, slots, groups)
    return pl.pallas_call(
        functools.partial(early_kernel, (nb, slots)),
        out_shape=[
            jax.ShapeDtypeStruct((exp_dev, groups * slots, features), jnp.bfloat16),
            jax.ShapeDtypeStruct((groups, GROUP * tok, exp_dev * slots), jnp.bfloat16),
            jax.ShapeDtypeStruct((exp_dev, groups * slots, 1), jnp.float32),
        ],
        in_specs=[pl.BlockSpec(memory_space=pltpu.SMEM)]
        + [pl.BlockSpec(memory_space=pl.ANY)] * (2 * nb),
        grid=(1,),
        out_specs=[
            pl.BlockSpec((exp_dev, groups * slots, features), lambda i: (0, 0, 0)),
            pl.BlockSpec((groups, GROUP * tok, exp_dev * slots), lambda i: (0, 0, 0)),
            pl.BlockSpec((exp_dev, groups * slots, 1), lambda i: (0, 0, 0)),
        ],
        scratch_shapes=[xbuf, pbuf, small, small, pltpu.SemaphoreType.DMA((2, 2 * GROUP))],
        compiler_params=pltpu.CompilerParams(vmem_limit_bytes=LIMIT),
        cost_estimate=LIGHT,
        name="early",
    )(first, *[half for block in blocks for half in block])


def experts_of(ready, late, first, capacity, w_gate, w_up, w_down):
    rows, table, slotw = ready
    exp_dev, features, hidden = w_gate.shape
    nb, tok, slots, groups, pairs = sizes(late, capacity, exp_dev)
    every = 2 * groups * slots
    held = min(2, exp_dev)
    tiles = [(start, min(NARROW, hidden - start)) for start in range(0, hidden, NARROW)]
    smem = pl.BlockSpec(memory_space=pltpu.SMEM)
    anywhere = pl.BlockSpec(memory_space=pl.ANY)
    xbuf, pbuf, small = scratch(tok, features, exp_dev, slots, groups)
    tbuf = pltpu.VMEM((2 * groups,) + table.shape[1:], jnp.bfloat16)
    act = pltpu.VMEM((exp_dev, every, hidden), jnp.bfloat16)
    blocks = [jax.ShapeDtypeStruct((tok, features), jnp.bfloat16)] * (2 * nb)
    got = pl.pallas_call(
        functools.partial(expert_kernel, (nb, exp_dev, slots, tiles)),
        grid=(1,),
        out_shape=blocks,
        in_specs=[smem]
        + [anywhere] * (2 * nb + 2)
        + [pl.BlockSpec(slotw.shape, lambda i: (0, 0, 0))]
        + [anywhere] * 3,
        out_specs=[anywhere] * (2 * nb),
        scratch_shapes=[
            pltpu.VMEM((held, features, hidden), jnp.bfloat16),
            pltpu.VMEM((held, features, hidden), jnp.bfloat16),
            pltpu.VMEM((2, exp_dev, hidden, WIDE), jnp.bfloat16),
            xbuf,
            pltpu.VMEM((exp_dev, every, features), jnp.bfloat16),
            pbuf,
            tbuf,
            act,
            pltpu.VMEM((exp_dev, every, WIDE), jnp.bfloat16),
            pltpu.VMEM((2, 2 * groups, GROUP * tok, WIDE), jnp.bfloat16),
            pltpu.VMEM((exp_dev, every, 1), jnp.float32),
            small,
            small,
            pltpu.SemaphoreType.DMA((2, held)),
            pltpu.SemaphoreType.DMA((2, exp_dev)),
            pltpu.SemaphoreType.DMA((2, 2 * GROUP)),
            pltpu.SemaphoreType.DMA((2, 2 * groups, GROUP)),
            pltpu.SemaphoreType.DMA((exp_dev,)),
            pltpu.SemaphoreType.DMA,
        ],
        compiler_params=pltpu.CompilerParams(vmem_limit_bytes=LIMIT),
        cost_estimate=pl.CostEstimate(
            flops=6 * exp_dev * every * features * hidden,
            bytes_accessed=6 * exp_dev * features * hidden + 4 * nb * tok * features,
            transcendentals=0,
        ),
        name="experts",
    )(first, *[half for block in late for half in block], rows, table, slotw, w_gate, w_up, w_down)
    return list(got[:nb]), list(got[nb:])


def body(tokens, norm_gain, gate_weights, routes, moves, w_gate, w_up, w_down):
    tok_rows, features = tokens.shape
    per_token = routes.shape[1]
    exp_dev = w_gate.shape[0]
    group = lax.axis_size("row") * lax.axis_size("col")
    experts = group * exp_dev
    capacity = tok_rows * per_token * 3 // (2 * experts)
    half = tok_rows // 2
    halves = pl.pallas_call(
        head_kernel,
        out_shape=[
            jax.ShapeDtypeStruct((half, features + tok_rows), jnp.bfloat16),
            jax.ShapeDtypeStruct((half, features), jnp.bfloat16),
        ],
        name="head",
    )(tokens, norm_gain.reshape(1, features), gate_weights.T, routes.T)
    first = (lax.axis_index(("row", "col")) * exp_dev).astype(jnp.int32).reshape(1)
    ready, late = spread(
        list(halves), lambda blocks: gathered(blocks, first, capacity, exp_dev)
    )
    late, early = experts_of(ready, late, first, capacity, w_gate, w_up, w_down)
    pieces, last = collected(late, early)
    rows = jnp.arange(tok_rows, dtype=jnp.int32)
    pick = (moves[0, 0][:, None] == rows[None, :]).astype(jnp.bfloat16)
    known = sum(piece.astype(jnp.float32) for piece in [tokens] + pieces)
    picked = jnp.dot(
        pick.astype(jnp.float32),
        known,
        precision=lax.Precision.HIGHEST,
        preferred_element_type=jnp.float32,
    )
    leaving = jnp.dot(pick, last, preferred_element_type=jnp.float32)
    leaving = (picked + leaving).astype(jnp.bfloat16)
    total = (known + last.astype(jnp.float32)).astype(jnp.bfloat16)
    incoming = shifted(leaving, "rep", 1)
    second = lax.axis_index("rep") == 1
    target = jnp.where(second, moves[0, 1], moves[0, 0])
    match = rows[:, None] == target[None, :]
    placed = jnp.dot(match.astype(jnp.bfloat16), incoming, preferred_element_type=jnp.float32)
    placed = jnp.where(second, placed, 0.0).astype(jnp.bfloat16)
    return jnp.where(jnp.any(match, axis=1, keepdims=True), placed, total)


def solution(mesh):
    return jax.shard_map(
        body,
        mesh=mesh,
        in_specs=(
            P(("rep", "row", "col"), None),
            P(),
            P(("rep", "row", "col"), None),
            P(("rep", "row", "col"), None),
            P(("row", "col"), None, None),
            P(("row", "col"), None, None),
            P(("row", "col"), None, None),
            P(("row", "col"), None, None),
        ),
        out_specs=P(("rep", "row", "col"), None),
        check_vma=False,
    )
```

```python
import functools

import jax
import jax.numpy as jnp
from jax import lax
from jax.experimental import pallas as pl
from jax.experimental.pallas import tpu as pltpu
from jax.sharding import PartitionSpec as P

GROUP = 8
PIECES = 4
LANE = 8
WIDE = 512
NARROW = 512
LIMIT = 60 * 1024 * 1024
LIGHT = pl.CostEstimate(flops=1, bytes_accessed=1, transcendentals=0)


def shifted(value, axis, steps):
    count = lax.axis_size(axis)
    first, last = (max(0, -steps), min(count, count - steps))
    return lax.ppermute(value, axis, [(source, source + steps) for source in range(first, last)])


def turned(value, steps):
    count = lax.axis_size("col")
    return lax.ppermute(value, "col", [(source, (source + steps) % count) for source in range(count)])


def swapped(value, bit):
    count = lax.axis_size("row")
    return lax.ppermute(value, "row", [(source, source ^ bit) for source in range(count)])


def spread(halves, gather):
    line, other, last = [halves], [], halves
    for _ in range(1, lax.axis_size("col")):
        pairs = [lax.optimization_barrier((turned(one, 1), swapped(one, 2))) for one in last]
        last = [ahead for ahead, _ in pairs]
        line.append(last)
        other.append([across for _, across in pairs])
    ready = gather(line + [[swapped(one, 1) for one in block] for block in line])
    final = [swapped(one, 2) for one in last]
    held = lax.optimization_barrier((*final, ready[2]))[: len(final)]
    far = [[swapped(one, 1) for one in block] for block in other + [list(held)]]
    return ready, other + [final] + far


def added(*parts):
    return sum(part.astype(jnp.float32) for part in parts).astype(jnp.bfloat16)


def collected(late, early):
    cols = lax.axis_size("col")
    order = list(range(cols // 2, 0, -1)) + list(range(cols // 2 + 1, cols)) + [0]
    held = {step: swapped(late[cols + step], 1) for step in order}
    sent = {step: swapped(added(late[step], held[step]), 2) for step in order}
    far = {
        step: swapped(lax.optimization_barrier((early[cols + step], held[step]))[0], 1)
        for step in order
    }
    line = [[early[step], far[step], sent[step]] for step in range(cols)]
    down, up = [], []
    for step in range(cols // 2, 0, -1):
        down = [turned(added(*(line[step] + down)), -1)]
        if step == cols // 2:
            ahead = down[0]
    for step in range(cols // 2 + 1, cols):
        value = added(lax.optimization_barrier(added(*line[step][:2], *up)), line[step][2])
        if not up:
            value = lax.optimization_barrier((value, ahead))[0]
        up = [turned(value, 1)]
    return line[0] + down, up[0]


def head_kernel(tokens_ref, gain_ref, weights_ref, routes_ref, *outs):
    features, per_token = tokens_ref.shape[1], routes_ref.shape[0]
    widened = tokens_ref[...].astype(jnp.float32)
    scale = lax.rsqrt(jnp.mean(widened * widened, axis=-1, keepdims=True) + 1e-06)
    normed = (widened * scale * gain_ref[...]).astype(jnp.bfloat16)
    half = outs[0].shape[0]
    for i, out_ref in enumerate(outs):
        out_ref[:, :features] = normed[i * half : (i + 1) * half]
    weights = weights_ref[...]
    high = weights.astype(jnp.bfloat16).astype(jnp.float32)
    middle = (weights - high).astype(jnp.bfloat16).astype(jnp.float32)
    low = weights - high - middle
    gap = jnp.zeros((LANE - per_token, weights.shape[1]), jnp.float32)
    meta = [routes_ref[...].astype(jnp.float32), gap - 1.0, high, gap, middle, gap, low, gap]
    outs[0][: 4 * LANE, features:] = jnp.concatenate(meta, axis=0).astype(jnp.bfloat16)
    outs[0][4 * LANE :, features:] = jnp.zeros(
        (half - 4 * LANE, weights.shape[1]), jnp.bfloat16
    )


def gather_groups(xs, first, slots, xbuf, xsem, named_s, weight_s, pbuf, tbuf, put_weight, put_rows, begin=None):
    groups = len(xs) // (2 * GROUP)
    half = xs[0].shape[0]
    tok = 2 * half
    features = xs[1].shape[1]
    pairs = named_s.shape[0]
    exp_dev = pairs // GROUP

    def copies(g):
        for b in range(GROUP):
            for h in range(2):
                source = xs[2 * (g * GROUP + b) + h]
                target = xbuf.at[
                    g % 2, pl.ds(b * tok + h * half, half), pl.ds(0, source.shape[1])
                ]
                yield pltpu.make_async_copy(source, target, xsem.at[g % 2, 2 * b + h])

    def load(g):
        for copy in copies(g):
            copy.start()

    for g in range(min(2, groups)):
        load(g)
    if begin is not None:
        begin()
    lane = lax.broadcasted_iota(jnp.int32, (tok, tok), 1)
    sub = lax.broadcasted_iota(jnp.int32, (tok, tok), 0)
    upto = (sub <= lane).astype(jnp.bfloat16)
    pair_r = lax.broadcasted_iota(jnp.int32, (pairs, pairs), 0)
    pair_c = lax.broadcasted_iota(jnp.int32, (pairs, pairs), 1)
    before = ((pair_r // GROUP == pair_c // GROUP) & (pair_c < pair_r)).astype(jnp.bfloat16)
    slot_id = lax.broadcasted_iota(jnp.int32, (slots, tok), 0).astype(jnp.float32)
    wide_id = lax.broadcasted_iota(jnp.int32, (tok, exp_dev * slots), 1).astype(jnp.float32)
    offset = lax.broadcasted_iota(jnp.int32, (pairs, tok), 0) // GROUP * slots
    offset = offset.astype(jnp.float32)

    for g in range(groups):
        for copy in copies(g):
            copy.wait()
        for b in range(GROUP):
            meta = xbuf[g % 2, b * tok : b * tok + 4 * LANE, features:].astype(jnp.float32)
            chosen = meta[:LANE]
            given = meta[LANE : 2 * LANE] + meta[2 * LANE : 3 * LANE] + meta[3 * LANE : 4 * LANE]
            for e in range(exp_dev):
                hit = chosen == (first + e).astype(jnp.float32)
                named_s[e * GROUP + b : e * GROUP + b + 1, :] = jnp.sum(
                    hit.astype(jnp.float32), axis=0, keepdims=True
                )
                weight_s[e * GROUP + b : e * GROUP + b + 1, :] = jnp.sum(
                    jnp.where(hit, given, 0.0), axis=0, keepdims=True
                )
        named = named_s[...]
        count = jnp.dot(named.astype(jnp.bfloat16), upto, preferred_element_type=jnp.float32)
        totals = jnp.broadcast_to(count[:, tok - 1 :], (pairs, tok)).astype(jnp.bfloat16)
        base = jnp.dot(before, totals, preferred_element_type=jnp.float32)
        named_s[...] = jnp.where(named > 0.5, base + count - 1.0, -1.0)
        for e in range(exp_dev):
            total = jnp.zeros((slots, tok), jnp.float32)
            for b in range(GROUP):
                pick = slot_id == named_s[e * GROUP + b : e * GROUP + b + 1, :]
                pbuf[e * slots : (e + 1) * slots, b * tok : (b + 1) * tok] = pick.astype(
                    jnp.float32
                ).astype(jnp.bfloat16)
                total += jnp.where(pick, weight_s[e * GROUP + b : e * GROUP + b + 1, :], 0.0)
            put_weight(g, e, jnp.sum(total, axis=1, keepdims=True))
        place = named_s[...]
        place = jnp.where(place < -0.5, place, place + offset)
        place = jnp.concatenate([place, jnp.zeros((tok - pairs, tok), jnp.float32)], axis=0).T
        for b in range(GROUP):
            pick = wide_id == place[:, b : b + 1]
            for e in range(1, exp_dev):
                pick = pick | (wide_id == place[:, e * GROUP + b : e * GROUP + b + 1])
            tbuf[g, b * tok : (b + 1) * tok, :] = pick.astype(jnp.float32).astype(jnp.bfloat16)

        @pl.loop(0, features // WIDE)
        def _(n):
            cols = pl.ds(pl.multiple_of(n * WIDE, WIDE), WIDE)
            got = jnp.dot(pbuf[...], xbuf[g % 2, :, cols], preferred_element_type=jnp.float32)
            got = got.astype(jnp.bfloat16)
            for e in range(exp_dev):
                put_rows(g, e, cols, got[e * slots : (e + 1) * slots])

        if g + 2 < groups:
            load(g + 2)


def early_kernel(plan, first_ref, *refs):
    nb, slots = plan
    xs, refs = refs[: 2 * nb], refs[2 * nb :]
    rows_ref, tbuf, slotw, xbuf, pbuf, named_s, weight_s, xsem = refs

    def put_weight(g, e, value):
        slotw[e, g * slots : (g + 1) * slots, :] = value

    def put_rows(g, e, cols, value):
        rows_ref[e, g * slots : (g + 1) * slots, cols] = value

    gather_groups(
        xs, first_ref[0], slots, xbuf, xsem, named_s, weight_s, pbuf, tbuf, put_weight, put_rows
    )


def expert_kernel(plan, first_ref, *refs):
    nb, exp_dev, slots, tiles = plan
    xs, refs = refs[: 2 * nb], refs[2 * nb :]
    rows_ref, table_ref, slotw_ref, gate_ref, up_ref, down_ref = refs[:6]
    outs, refs = refs[6 : 6 + 2 * nb], refs[6 + 2 * nb :]
    gate_b, up_b, down_b, xbuf, gbuf, pbuf, tbuf, act, obuf, stage, slotw = refs[:11]
    named_s, weight_s, wsem, downsem, xsem, osem, rsem, tsem = refs[11:]
    groups = nb // GROUP
    tok, features = outs[0].shape
    early = groups * slots
    steps = features // WIDE

    def pieces_start(source, target, sem):
        size = target.shape[0] // PIECES
        for piece in range(PIECES):
            part = pl.ds(piece * size, size)
            copy = pltpu.make_async_copy(source.at[part, :], target.at[part, :], sem)
            copy.start(priority=piece % 2)

    def weight_refs(kind, e, slot):
        source, target = ((gate_ref, gate_b), (up_ref, up_b))[kind]
        return source.at[e], target.at[slot], wsem.at[kind, slot]

    def down_refs(n, e):
        source = down_ref.at[e, :, pl.ds(n * WIDE, WIDE)]
        return source, down_b.at[n % 2, e], downsem.at[n % 2, e]

    def fetch(e, slot):
        for kind in range(2):
            pieces_start(*weight_refs(kind, e, slot))

    def fetch_down(n):
        for e in range(exp_dev):
            pieces_start(*down_refs(n, e))

    def arrive(kind, e, slot):
        pltpu.make_async_copy(*weight_refs(kind, e, slot)).wait()

    def rows_copy(e):
        return pltpu.make_async_copy(rows_ref.at[e], gbuf.at[e, pl.ds(0, early), :], rsem.at[e])

    def out_copy(n, g, b):
        return pltpu.make_async_copy(
            stage.at[n % 2, g, pl.ds(b * tok, tok), :],
            outs[g * GROUP + b].at[:, pl.ds(n * WIDE, WIDE)],
            osem.at[n % 2, g, b],
        )

    table_in = pltpu.make_async_copy(table_ref, tbuf.at[pl.ds(groups, groups)], tsem)

    def put_weight(g, e, value):
        slotw[e, early + g * slots : early + (g + 1) * slots, :] = value

    def put_rows(g, e, cols, value):
        gbuf[e, early + g * slots : early + (g + 1) * slots, cols] = value

    def begin():
        pieces_start(*weight_refs(0, 0, 0))
        for e in range(exp_dev):
            rows_copy(e).start()
        pieces_start(*weight_refs(1, 0, 0))
        if exp_dev > 1:
            fetch(1, 1)
        table_in.start()
        for n in range(min(2, steps)):
            fetch_down(n)
        slotw[:, :early, :] = slotw_ref[...]

    gather_groups(
        xs,
        first_ref[0],
        slots,
        xbuf,
        xsem,
        named_s,
        weight_s,
        pbuf,
        tbuf,
        put_weight,
        put_rows,
        begin,
    )

    @pl.loop(0, exp_dev)
    def _(e):
        slot = lax.rem(e, gate_b.shape[0])
        rows_copy(e).wait()
        arrive(0, e, slot)
        arrive(1, e, slot)
        for start, size in tiles:
            gate = jnp.dot(
                gbuf[e], gate_b[slot, :, start : start + size], preferred_element_type=jnp.float32
            )
            upward = jnp.dot(
                gbuf[e], up_b[slot, :, start : start + size], preferred_element_type=jnp.float32
            )
            act[e, :, start : start + size] = (
                0.5 * gate * (1.0 + jnp.tanh(0.5 * gate)) * upward * slotw[e]
            ).astype(jnp.bfloat16)

        @pl.when(e + 2 < exp_dev)
        def _():
            fetch(e + 2, slot)

    table_in.wait()
    for n in range(steps):
        for e in range(exp_dev):
            pltpu.make_async_copy(*down_refs(n, e)).wait()
            obuf[e] = jnp.dot(
                act[e], down_b[n % 2, e], preferred_element_type=jnp.float32
            ).astype(jnp.bfloat16)
        if n + 2 < steps:
            fetch_down(n + 2)
        for g in range(2 * groups):
            if n >= 2:
                for b in range(GROUP):
                    out_copy(n - 2, g, b).wait()
            here = (groups + g if g < groups else g - groups) * slots
            made = jnp.concatenate(
                [obuf[e, here : here + slots, :] for e in range(exp_dev)], axis=0
            )
            stage[n % 2, g] = jnp.dot(
                tbuf[g], made, preferred_element_type=jnp.float32
            ).astype(jnp.bfloat16)
            for b in range(GROUP):
                out_copy(n, g, b).start()
    for n in range(max(0, steps - 2), steps):
        for g in range(2 * groups):
            for b in range(GROUP):
                out_copy(n, g, b).wait()


def sizes(blocks, capacity, exp_dev):
    slots = -(-GROUP * capacity // 16) * 16
    return len(blocks), 2 * blocks[0][0].shape[0], slots, len(blocks) // GROUP, exp_dev * GROUP


def scratch(tok, features, exp_dev, slots, groups):
    return [
        pltpu.VMEM((min(2, groups), GROUP * tok, features + tok), jnp.bfloat16),
        pltpu.VMEM((exp_dev * slots, GROUP * tok), jnp.bfloat16),
        pltpu.VMEM((exp_dev * GROUP, tok), jnp.float32),
    ]


def gathered(blocks, first, capacity, exp_dev):
    nb, tok, slots, groups, _ = sizes(blocks, capacity, exp_dev)
    features = blocks[0][1].shape[1]
    xbuf, pbuf, small = scratch(tok, features, exp_dev, slots, groups)
    return pl.pallas_call(
        functools.partial(early_kernel, (nb, slots)),
        out_shape=[
            jax.ShapeDtypeStruct((exp_dev, groups * slots, features), jnp.bfloat16),
            jax.ShapeDtypeStruct((groups, GROUP * tok, exp_dev * slots), jnp.bfloat16),
            jax.ShapeDtypeStruct((exp_dev, groups * slots, 1), jnp.float32),
        ],
        in_specs=[pl.BlockSpec(memory_space=pltpu.SMEM)]
        + [pl.BlockSpec(memory_space=pl.ANY)] * (2 * nb),
        grid=(1,),
        out_specs=[
            pl.BlockSpec((exp_dev, groups * slots, features), lambda i: (0, 0, 0)),
            pl.BlockSpec((groups, GROUP * tok, exp_dev * slots), lambda i: (0, 0, 0)),
            pl.BlockSpec((exp_dev, groups * slots, 1), lambda i: (0, 0, 0)),
        ],
        scratch_shapes=[xbuf, pbuf, small, small, pltpu.SemaphoreType.DMA((2, 2 * GROUP))],
        compiler_params=pltpu.CompilerParams(vmem_limit_bytes=LIMIT),
        cost_estimate=LIGHT,
        name="early",
    )(first, *[half for block in blocks for half in block])


def experts_of(ready, late, first, capacity, w_gate, w_up, w_down):
    rows, table, slotw = ready
    exp_dev, features, hidden = w_gate.shape
    nb, tok, slots, groups, pairs = sizes(late, capacity, exp_dev)
    every = 2 * groups * slots
    held = min(2, exp_dev)
    tiles = [(start, min(NARROW, hidden - start)) for start in range(0, hidden, NARROW)]
    smem = pl.BlockSpec(memory_space=pltpu.SMEM)
    anywhere = pl.BlockSpec(memory_space=pl.ANY)
    xbuf, pbuf, small = scratch(tok, features, exp_dev, slots, groups)
    tbuf = pltpu.VMEM((2 * groups,) + table.shape[1:], jnp.bfloat16)
    act = pltpu.VMEM((exp_dev, every, hidden), jnp.bfloat16)
    blocks = [jax.ShapeDtypeStruct((tok, features), jnp.bfloat16)] * (2 * nb)
    got = pl.pallas_call(
        functools.partial(expert_kernel, (nb, exp_dev, slots, tiles)),
        grid=(1,),
        out_shape=blocks,
        in_specs=[smem]
        + [anywhere] * (2 * nb + 2)
        + [pl.BlockSpec(slotw.shape, lambda i: (0, 0, 0))]
        + [anywhere] * 3,
        out_specs=[anywhere] * (2 * nb),
        scratch_shapes=[
            pltpu.VMEM((held, features, hidden), jnp.bfloat16),
            pltpu.VMEM((held, features, hidden), jnp.bfloat16),
            pltpu.VMEM((2, exp_dev, hidden, WIDE), jnp.bfloat16),
            xbuf,
            pltpu.VMEM((exp_dev, every, features), jnp.bfloat16),
            pbuf,
            tbuf,
            act,
            pltpu.VMEM((exp_dev, every, WIDE), jnp.bfloat16),
            pltpu.VMEM((2, 2 * groups, GROUP * tok, WIDE), jnp.bfloat16),
            pltpu.VMEM((exp_dev, every, 1), jnp.float32),
            small,
            small,
            pltpu.SemaphoreType.DMA((2, held)),
            pltpu.SemaphoreType.DMA((2, exp_dev)),
            pltpu.SemaphoreType.DMA((2, 2 * GROUP)),
            pltpu.SemaphoreType.DMA((2, 2 * groups, GROUP)),
            pltpu.SemaphoreType.DMA((exp_dev,)),
            pltpu.SemaphoreType.DMA,
        ],
        compiler_params=pltpu.CompilerParams(vmem_limit_bytes=LIMIT),
        cost_estimate=pl.CostEstimate(
            flops=6 * exp_dev * every * features * hidden,
            bytes_accessed=6 * exp_dev * features * hidden + 4 * nb * tok * features,
            transcendentals=0,
        ),
        name="experts",
    )(first, *[half for block in late for half in block], rows, table, slotw, w_gate, w_up, w_down)
    return list(got[:nb]), list(got[nb:])


def body(tokens, norm_gain, gate_weights, routes, moves, w_gate, w_up, w_down):
    tok_rows, features = tokens.shape
    per_token = routes.shape[1]
    exp_dev = w_gate.shape[0]
    group = lax.axis_size("row") * lax.axis_size("col")
    experts = group * exp_dev
    capacity = tok_rows * per_token * 3 // (2 * experts)
    half = tok_rows // 2
    halves = pl.pallas_call(
        head_kernel,
        out_shape=[
            jax.ShapeDtypeStruct((half, features + tok_rows), jnp.bfloat16),
            jax.ShapeDtypeStruct((half, features), jnp.bfloat16),
        ],
        name="head",
    )(tokens, norm_gain.reshape(1, features), gate_weights.T, routes.T)
    first = (lax.axis_index(("row", "col")) * exp_dev).astype(jnp.int32).reshape(1)
    ready, late = spread(
        list(halves), lambda blocks: gathered(blocks, first, capacity, exp_dev)
    )
    late, early = experts_of(ready, late, first, capacity, w_gate, w_up, w_down)
    pieces, last = collected(late, early)
    rows = jnp.arange(tok_rows, dtype=jnp.int32)
    pick = (moves[0, 0][:, None] == rows[None, :]).astype(jnp.bfloat16)
    known = sum(piece.astype(jnp.float32) for piece in [tokens] + pieces)
    known = lax.optimization_barrier(known)
    picked = jnp.dot(
        pick.astype(jnp.float32),
        known,
        precision=lax.Precision.HIGHEST,
        preferred_element_type=jnp.float32,
    )
    picked = lax.optimization_barrier(picked)
    leaving = jnp.dot(pick, last, preferred_element_type=jnp.float32)
    leaving = (picked + leaving).astype(jnp.bfloat16)
    total = (known + last.astype(jnp.float32)).astype(jnp.bfloat16)
    incoming = shifted(leaving, "rep", 1)
    second = lax.axis_index("rep") == 1
    target = jnp.where(second, moves[0, 1], moves[0, 0])
    match = rows[:, None] == target[None, :]
    placed = jnp.dot(match.astype(jnp.bfloat16), incoming, preferred_element_type=jnp.float32)
    placed = jnp.where(second, placed, 0.0).astype(jnp.bfloat16)
    return jnp.where(jnp.any(match, axis=1, keepdims=True), placed, total)


def solution(mesh):
    return jax.shard_map(
        body,
        mesh=mesh,
        in_specs=(
            P(("rep", "row", "col"), None),
            P(),
            P(("rep", "row", "col"), None),
            P(("rep", "row", "col"), None),
            P(("row", "col"), None, None),
            P(("row", "col"), None, None),
            P(("row", "col"), None, None),
            P(("row", "col"), None, None),
        ),
        out_specs=P(("rep", "row", "col"), None),
        check_vma=False,
    )
```

```python
import functools

import jax
import jax.numpy as jnp
from jax import lax
from jax.experimental import pallas as pl
from jax.experimental.pallas import tpu as pltpu
from jax.sharding import PartitionSpec as P

GROUP = 8
PIECES = 4
LANE = 8
WIDE = 512
NARROW = 512
LIMIT = 60 * 1024 * 1024
LIGHT = pl.CostEstimate(flops=1, bytes_accessed=1, transcendentals=0)


def shifted(value, axis, steps):
    count = lax.axis_size(axis)
    first, last = (max(0, -steps), min(count, count - steps))
    return lax.ppermute(value, axis, [(source, source + steps) for source in range(first, last)])


def turned(value, steps):
    count = lax.axis_size("col")
    return lax.ppermute(value, "col", [(source, (source + steps) % count) for source in range(count)])


def swapped(value, bit):
    count = lax.axis_size("row")
    return lax.ppermute(value, "row", [(source, source ^ bit) for source in range(count)])


def spread(halves, gather):
    line, other, last = [halves], [], halves
    for _ in range(1, lax.axis_size("col")):
        pairs = [lax.optimization_barrier((turned(one, 1), swapped(one, 2))) for one in last]
        last = [ahead for ahead, _ in pairs]
        line.append(last)
        other.append([across for _, across in pairs])
    ready = gather(line + [[swapped(one, 1) for one in block] for block in line])
    final = [swapped(one, 2) for one in last]
    held = lax.optimization_barrier((*final, ready[2]))[: len(final)]
    far = [[swapped(one, 1) for one in block] for block in other + [list(held)]]
    return ready, other + [final] + far


def added(*parts):
    return sum(part.astype(jnp.float32) for part in parts).astype(jnp.bfloat16)


def collected(late, early):
    cols = lax.axis_size("col")
    direct = list(range(cols // 2, 0, -1))
    around = list(range(cols // 2 + 1, cols))
    order = direct + around + [0]
    held = {step: swapped(late[cols + step], 1) for step in order}
    far = {
        step: swapped(lax.optimization_barrier((early[cols + step], held[step]))[0], 1)
        for step in order
    }
    across, up = [], []
    for step in around:
        across = [turned(added(late[step], held[step], *across), 1)]
    for step in around:
        up = [turned(added(early[step], far[step], *up), 1)]
    sent = {step: swapped(added(late[step], held[step]), 2) for step in direct}
    sent[0] = swapped(added(late[0], held[0], *across), 2)
    down = []
    for step in direct:
        ready = lax.optimization_barrier(added(early[step], far[step], *down))
        down = [turned(added(ready, sent[step]), -1)]
    return [early[0], far[0], sent[0]] + up, down[0]


def head_kernel(tokens_ref, gain_ref, weights_ref, routes_ref, *outs):
    features, per_token = tokens_ref.shape[1], routes_ref.shape[0]
    widened = tokens_ref[...].astype(jnp.float32)
    scale = lax.rsqrt(jnp.mean(widened * widened, axis=-1, keepdims=True) + 1e-06)
    normed = (widened * scale * gain_ref[...]).astype(jnp.bfloat16)
    half = outs[0].shape[0]
    for i, out_ref in enumerate(outs):
        out_ref[:, :features] = normed[i * half : (i + 1) * half]
    weights = weights_ref[...]
    high = weights.astype(jnp.bfloat16).astype(jnp.float32)
    middle = (weights - high).astype(jnp.bfloat16).astype(jnp.float32)
    low = weights - high - middle
    gap = jnp.zeros((LANE - per_token, weights.shape[1]), jnp.float32)
    meta = [routes_ref[...].astype(jnp.float32), gap - 1.0, high, gap, middle, gap, low, gap]
    outs[0][: 4 * LANE, features:] = jnp.concatenate(meta, axis=0).astype(jnp.bfloat16)
    outs[0][4 * LANE :, features:] = jnp.zeros(
        (half - 4 * LANE, weights.shape[1]), jnp.bfloat16
    )


def gather_groups(xs, first, slots, xbuf, xsem, named_s, weight_s, pbuf, tbuf, put_weight, put_rows, begin=None):
    groups = len(xs) // (2 * GROUP)
    half = xs[0].shape[0]
    tok = 2 * half
    features = xs[1].shape[1]
    pairs = named_s.shape[0]
    exp_dev = pairs // GROUP

    def copies(g):
        for b in range(GROUP):
            for h in range(2):
                source = xs[2 * (g * GROUP + b) + h]
                target = xbuf.at[
                    g % 2, pl.ds(b * tok + h * half, half), pl.ds(0, source.shape[1])
                ]
                yield pltpu.make_async_copy(source, target, xsem.at[g % 2, 2 * b + h])

    def load(g):
        for copy in copies(g):
            copy.start()

    for g in range(min(2, groups)):
        load(g)
    if begin is not None:
        begin()
    lane = lax.broadcasted_iota(jnp.int32, (tok, tok), 1)
    sub = lax.broadcasted_iota(jnp.int32, (tok, tok), 0)
    upto = (sub <= lane).astype(jnp.bfloat16)
    pair_r = lax.broadcasted_iota(jnp.int32, (pairs, pairs), 0)
    pair_c = lax.broadcasted_iota(jnp.int32, (pairs, pairs), 1)
    before = ((pair_r // GROUP == pair_c // GROUP) & (pair_c < pair_r)).astype(jnp.bfloat16)
    slot_id = lax.broadcasted_iota(jnp.int32, (slots, tok), 0).astype(jnp.float32)
    wide_id = lax.broadcasted_iota(jnp.int32, (tok, exp_dev * slots), 1).astype(jnp.float32)
    offset = lax.broadcasted_iota(jnp.int32, (pairs, tok), 0) // GROUP * slots
    offset = offset.astype(jnp.float32)

    for g in range(groups):
        for copy in copies(g):
            copy.wait()
        for b in range(GROUP):
            meta = xbuf[g % 2, b * tok : b * tok + 4 * LANE, features:].astype(jnp.float32)
            chosen = meta[:LANE]
            given = meta[LANE : 2 * LANE] + meta[2 * LANE : 3 * LANE] + meta[3 * LANE : 4 * LANE]
            for e in range(exp_dev):
                hit = chosen == (first + e).astype(jnp.float32)
                named_s[e * GROUP + b : e * GROUP + b + 1, :] = jnp.sum(
                    hit.astype(jnp.float32), axis=0, keepdims=True
                )
                weight_s[e * GROUP + b : e * GROUP + b + 1, :] = jnp.sum(
                    jnp.where(hit, given, 0.0), axis=0, keepdims=True
                )
        named = named_s[...]
        count = jnp.dot(named.astype(jnp.bfloat16), upto, preferred_element_type=jnp.float32)
        totals = jnp.broadcast_to(count[:, tok - 1 :], (pairs, tok)).astype(jnp.bfloat16)
        base = jnp.dot(before, totals, preferred_element_type=jnp.float32)
        named_s[...] = jnp.where(named > 0.5, base + count - 1.0, -1.0)
        for e in range(exp_dev):
            total = jnp.zeros((slots, tok), jnp.float32)
            for b in range(GROUP):
                pick = slot_id == named_s[e * GROUP + b : e * GROUP + b + 1, :]
                pbuf[e * slots : (e + 1) * slots, b * tok : (b + 1) * tok] = pick.astype(
                    jnp.float32
                ).astype(jnp.bfloat16)
                total += jnp.where(pick, weight_s[e * GROUP + b : e * GROUP + b + 1, :], 0.0)
            put_weight(g, e, jnp.sum(total, axis=1, keepdims=True))
        place = named_s[...]
        place = jnp.where(place < -0.5, place, place + offset)
        place = jnp.concatenate([place, jnp.zeros((tok - pairs, tok), jnp.float32)], axis=0).T
        for b in range(GROUP):
            pick = wide_id == place[:, b : b + 1]
            for e in range(1, exp_dev):
                pick = pick | (wide_id == place[:, e * GROUP + b : e * GROUP + b + 1])
            tbuf[g, b * tok : (b + 1) * tok, :] = pick.astype(jnp.float32).astype(jnp.bfloat16)

        @pl.loop(0, features // WIDE)
        def _(n):
            cols = pl.ds(pl.multiple_of(n * WIDE, WIDE), WIDE)
            got = jnp.dot(pbuf[...], xbuf[g % 2, :, cols], preferred_element_type=jnp.float32)
            got = got.astype(jnp.bfloat16)
            for e in range(exp_dev):
                put_rows(g, e, cols, got[e * slots : (e + 1) * slots])

        if g + 2 < groups:
            load(g + 2)


def early_kernel(plan, first_ref, *refs):
    nb, slots = plan
    xs, refs = refs[: 2 * nb], refs[2 * nb :]
    rows_ref, tbuf, slotw, xbuf, pbuf, named_s, weight_s, xsem = refs

    def put_weight(g, e, value):
        slotw[e, g * slots : (g + 1) * slots, :] = value

    def put_rows(g, e, cols, value):
        rows_ref[e, g * slots : (g + 1) * slots, cols] = value

    gather_groups(
        xs, first_ref[0], slots, xbuf, xsem, named_s, weight_s, pbuf, tbuf, put_weight, put_rows
    )


def expert_kernel(plan, first_ref, *refs):
    nb, exp_dev, slots, tiles = plan
    xs, refs = refs[: 2 * nb], refs[2 * nb :]
    rows_ref, table_ref, slotw_ref, gate_ref, up_ref, down_ref = refs[:6]
    outs, refs = refs[6 : 6 + 2 * nb], refs[6 + 2 * nb :]
    gate_b, up_b, down_b, xbuf, gbuf, pbuf, tbuf, act, obuf, stage, slotw = refs[:11]
    named_s, weight_s, wsem, downsem, xsem, osem, rsem, tsem = refs[11:]
    groups = nb // GROUP
    tok, features = outs[0].shape
    early = groups * slots
    steps = features // WIDE

    def pieces_start(source, target, sem):
        size = target.shape[0] // PIECES
        for piece in range(PIECES):
            part = pl.ds(piece * size, size)
            copy = pltpu.make_async_copy(source.at[part, :], target.at[part, :], sem)
            copy.start(priority=piece % 2)

    def weight_refs(kind, e, slot):
        source, target = ((gate_ref, gate_b), (up_ref, up_b))[kind]
        return source.at[e], target.at[slot], wsem.at[kind, slot]

    def down_refs(n, e):
        source = down_ref.at[e, :, pl.ds(n * WIDE, WIDE)]
        return source, down_b.at[n % 2, e], downsem.at[n % 2, e]

    def fetch(e, slot):
        for kind in range(2):
            pieces_start(*weight_refs(kind, e, slot))

    def fetch_down(n):
        for e in range(exp_dev):
            pieces_start(*down_refs(n, e))

    def arrive(kind, e, slot):
        pltpu.make_async_copy(*weight_refs(kind, e, slot)).wait()

    def rows_copy(e):
        return pltpu.make_async_copy(rows_ref.at[e], gbuf.at[e, pl.ds(0, early), :], rsem.at[e])

    def out_copy(n, g, b):
        return pltpu.make_async_copy(
            stage.at[n % 2, g, pl.ds(b * tok, tok), :],
            outs[g * GROUP + b].at[:, pl.ds(n * WIDE, WIDE)],
            osem.at[n % 2, g, b],
        )

    table_in = pltpu.make_async_copy(table_ref, tbuf.at[pl.ds(groups, groups)], tsem)

    def put_weight(g, e, value):
        slotw[e, early + g * slots : early + (g + 1) * slots, :] = value

    def put_rows(g, e, cols, value):
        gbuf[e, early + g * slots : early + (g + 1) * slots, cols] = value

    def begin():
        pieces_start(*weight_refs(0, 0, 0))
        for e in range(exp_dev):
            rows_copy(e).start()
        pieces_start(*weight_refs(1, 0, 0))
        if exp_dev > 1:
            fetch(1, 1)
        table_in.start()
        for n in range(min(2, steps)):
            fetch_down(n)
        slotw[:, :early, :] = slotw_ref[...]

    gather_groups(
        xs,
        first_ref[0],
        slots,
        xbuf,
        xsem,
        named_s,
        weight_s,
        pbuf,
        tbuf,
        put_weight,
        put_rows,
        begin,
    )

    @pl.loop(0, exp_dev)
    def _(e):
        slot = lax.rem(e, gate_b.shape[0])
        rows_copy(e).wait()
        arrive(0, e, slot)
        arrive(1, e, slot)
        for start, size in tiles:
            gate = jnp.dot(
                gbuf[e], gate_b[slot, :, start : start + size], preferred_element_type=jnp.float32
            )
            upward = jnp.dot(
                gbuf[e], up_b[slot, :, start : start + size], preferred_element_type=jnp.float32
            )
            act[e, :, start : start + size] = (
                0.5 * gate * (1.0 + jnp.tanh(0.5 * gate)) * upward * slotw[e]
            ).astype(jnp.bfloat16)

        @pl.when(e + 2 < exp_dev)
        def _():
            fetch(e + 2, slot)

    table_in.wait()
    for n in range(steps):
        for e in range(exp_dev):
            pltpu.make_async_copy(*down_refs(n, e)).wait()
            obuf[e] = jnp.dot(
                act[e], down_b[n % 2, e], preferred_element_type=jnp.float32
            ).astype(jnp.bfloat16)
        if n + 2 < steps:
            fetch_down(n + 2)
        for g in range(2 * groups):
            if n >= 2:
                for b in range(GROUP):
                    out_copy(n - 2, g, b).wait()
            here = (groups + g if g < groups else g - groups) * slots
            made = jnp.concatenate(
                [obuf[e, here : here + slots, :] for e in range(exp_dev)], axis=0
            )
            stage[n % 2, g] = jnp.dot(
                tbuf[g], made, preferred_element_type=jnp.float32
            ).astype(jnp.bfloat16)
            for b in range(GROUP):
                out_copy(n, g, b).start()
    for n in range(max(0, steps - 2), steps):
        for g in range(2 * groups):
            for b in range(GROUP):
                out_copy(n, g, b).wait()


def sizes(blocks, capacity, exp_dev):
    slots = -(-GROUP * capacity // 16) * 16
    return len(blocks), 2 * blocks[0][0].shape[0], slots, len(blocks) // GROUP, exp_dev * GROUP


def scratch(tok, features, exp_dev, slots, groups):
    return [
        pltpu.VMEM((min(2, groups), GROUP * tok, features + tok), jnp.bfloat16),
        pltpu.VMEM((exp_dev * slots, GROUP * tok), jnp.bfloat16),
        pltpu.VMEM((exp_dev * GROUP, tok), jnp.float32),
    ]


def gathered(blocks, first, capacity, exp_dev):
    nb, tok, slots, groups, _ = sizes(blocks, capacity, exp_dev)
    features = blocks[0][1].shape[1]
    xbuf, pbuf, small = scratch(tok, features, exp_dev, slots, groups)
    return pl.pallas_call(
        functools.partial(early_kernel, (nb, slots)),
        out_shape=[
            jax.ShapeDtypeStruct((exp_dev, groups * slots, features), jnp.bfloat16),
            jax.ShapeDtypeStruct((groups, GROUP * tok, exp_dev * slots), jnp.bfloat16),
            jax.ShapeDtypeStruct((exp_dev, groups * slots, 1), jnp.float32),
        ],
        in_specs=[pl.BlockSpec(memory_space=pltpu.SMEM)]
        + [pl.BlockSpec(memory_space=pl.ANY)] * (2 * nb),
        grid=(1,),
        out_specs=[
            pl.BlockSpec((exp_dev, groups * slots, features), lambda i: (0, 0, 0)),
            pl.BlockSpec((groups, GROUP * tok, exp_dev * slots), lambda i: (0, 0, 0)),
            pl.BlockSpec((exp_dev, groups * slots, 1), lambda i: (0, 0, 0)),
        ],
        scratch_shapes=[xbuf, pbuf, small, small, pltpu.SemaphoreType.DMA((2, 2 * GROUP))],
        compiler_params=pltpu.CompilerParams(vmem_limit_bytes=LIMIT),
        cost_estimate=LIGHT,
        name="early",
    )(first, *[half for block in blocks for half in block])


def experts_of(ready, late, first, capacity, w_gate, w_up, w_down):
    rows, table, slotw = ready
    exp_dev, features, hidden = w_gate.shape
    nb, tok, slots, groups, pairs = sizes(late, capacity, exp_dev)
    every = 2 * groups * slots
    held = min(2, exp_dev)
    tiles = [(start, min(NARROW, hidden - start)) for start in range(0, hidden, NARROW)]
    smem = pl.BlockSpec(memory_space=pltpu.SMEM)
    anywhere = pl.BlockSpec(memory_space=pl.ANY)
    xbuf, pbuf, small = scratch(tok, features, exp_dev, slots, groups)
    tbuf = pltpu.VMEM((2 * groups,) + table.shape[1:], jnp.bfloat16)
    act = pltpu.VMEM((exp_dev, every, hidden), jnp.bfloat16)
    blocks = [jax.ShapeDtypeStruct((tok, features), jnp.bfloat16)] * (2 * nb)
    got = pl.pallas_call(
        functools.partial(expert_kernel, (nb, exp_dev, slots, tiles)),
        grid=(1,),
        out_shape=blocks,
        in_specs=[smem]
        + [anywhere] * (2 * nb + 2)
        + [pl.BlockSpec(slotw.shape, lambda i: (0, 0, 0))]
        + [anywhere] * 3,
        out_specs=[anywhere] * (2 * nb),
        scratch_shapes=[
            pltpu.VMEM((held, features, hidden), jnp.bfloat16),
            pltpu.VMEM((held, features, hidden), jnp.bfloat16),
            pltpu.VMEM((2, exp_dev, hidden, WIDE), jnp.bfloat16),
            xbuf,
            pltpu.VMEM((exp_dev, every, features), jnp.bfloat16),
            pbuf,
            tbuf,
            act,
            pltpu.VMEM((exp_dev, every, WIDE), jnp.bfloat16),
            pltpu.VMEM((2, 2 * groups, GROUP * tok, WIDE), jnp.bfloat16),
            pltpu.VMEM((exp_dev, every, 1), jnp.float32),
            small,
            small,
            pltpu.SemaphoreType.DMA((2, held)),
            pltpu.SemaphoreType.DMA((2, exp_dev)),
            pltpu.SemaphoreType.DMA((2, 2 * GROUP)),
            pltpu.SemaphoreType.DMA((2, 2 * groups, GROUP)),
            pltpu.SemaphoreType.DMA((exp_dev,)),
            pltpu.SemaphoreType.DMA,
        ],
        compiler_params=pltpu.CompilerParams(vmem_limit_bytes=LIMIT),
        cost_estimate=pl.CostEstimate(
            flops=6 * exp_dev * every * features * hidden,
            bytes_accessed=6 * exp_dev * features * hidden + 4 * nb * tok * features,
            transcendentals=0,
        ),
        name="experts",
    )(first, *[half for block in late for half in block], rows, table, slotw, w_gate, w_up, w_down)
    return list(got[:nb]), list(got[nb:])


def body(tokens, norm_gain, gate_weights, routes, moves, w_gate, w_up, w_down):
    tok_rows, features = tokens.shape
    per_token = routes.shape[1]
    exp_dev = w_gate.shape[0]
    group = lax.axis_size("row") * lax.axis_size("col")
    experts = group * exp_dev
    capacity = tok_rows * per_token * 3 // (2 * experts)
    half = tok_rows // 2
    halves = pl.pallas_call(
        head_kernel,
        out_shape=[
            jax.ShapeDtypeStruct((half, features + tok_rows), jnp.bfloat16),
            jax.ShapeDtypeStruct((half, features), jnp.bfloat16),
        ],
        name="head",
    )(tokens, norm_gain.reshape(1, features), gate_weights.T, routes.T)
    first = (lax.axis_index(("row", "col")) * exp_dev).astype(jnp.int32).reshape(1)
    ready, late = spread(
        list(halves), lambda blocks: gathered(blocks, first, capacity, exp_dev)
    )
    late, early = experts_of(ready, late, first, capacity, w_gate, w_up, w_down)
    pieces, last = collected(late, early)
    rows = jnp.arange(tok_rows, dtype=jnp.int32)
    pick = (moves[0, 0][:, None] == rows[None, :]).astype(jnp.bfloat16)
    known = sum(piece.astype(jnp.float32) for piece in [tokens] + pieces)
    known = lax.optimization_barrier(known)
    picked = jnp.dot(
        pick.astype(jnp.float32),
        known,
        precision=lax.Precision.HIGHEST,
        preferred_element_type=jnp.float32,
    )
    picked = lax.optimization_barrier(picked)
    leaving = jnp.dot(pick, last, preferred_element_type=jnp.float32)
    leaving = (picked + leaving).astype(jnp.bfloat16)
    total = (known + last.astype(jnp.float32)).astype(jnp.bfloat16)
    incoming = shifted(leaving, "rep", 1)
    second = lax.axis_index("rep") == 1
    target = jnp.where(second, moves[0, 1], moves[0, 0])
    match = rows[:, None] == target[None, :]
    placed = jnp.dot(match.astype(jnp.bfloat16), incoming, preferred_element_type=jnp.float32)
    placed = jnp.where(second, placed, 0.0).astype(jnp.bfloat16)
    return jnp.where(jnp.any(match, axis=1, keepdims=True), placed, total)


def solution(mesh):
    return jax.shard_map(
        body,
        mesh=mesh,
        in_specs=(
            P(("rep", "row", "col"), None),
            P(),
            P(("rep", "row", "col"), None),
            P(("rep", "row", "col"), None),
            P(("row", "col"), None, None),
            P(("row", "col"), None, None),
            P(("row", "col"), None, None),
            P(("row", "col"), None, None),
        ),
        out_specs=P(("rep", "row", "col"), None),
        check_vma=False,
    )
```
